512 devices in a mesh: dp: 16 (over x, y_lo), seq: 32 (over y_hi, z, core).
Axes of the slice: x: 4, y: 8 (y_hi: 2, y_lo: 4; y = y_hi * 4 + y_lo), z: 8, core: 2. Of those that a mesh axis runs over, the one named last changes fastest.
Arguments:
- hidden_in: bfloat16 [16, 4096, 4096], P('dp', 'seq'), may hold values from -6 to 6
- queries: bfloat16 [16, 4096, 1024], P('dp', 'seq'), may hold values from -6 to 6
- out_grad: bfloat16 [16, 4096, 1024], P('dp', 'seq'), may hold values from -16 to 16
- kv_weight: bfloat16 [4096, 256], P('dp'), may hold values from -0.09375 to 0.09375
- block_pos: int32 [16, 32], P('dp'), may hold values from 0 to 31, each once within a row
- precision: int32 [16, 32, 2], P('dp', 'seq'), may hold values from 2 to 8, as said below
Outputs:
- query_grad: bfloat16 [16, 4096, 1024], P('dp', 'seq')
- kv_grad: bfloat16 [16, 4096, 256], P('dp', 'seq')
- input_grad: bfloat16 [16, 4096, 4096], P('dp', 'seq')
- weight_grad: float32 [4096, 256], P('dp')
The draws below stay inside these ranges and needn't reach their ends.
Inputs may be any that keep to these rules, and one draw needn't show every extreme that they name: `block_pos`: each sequence's row names every block position 0 to 31 once. `precision`: every entry is 2, 4 or 8.
All inputs are finite; a program needn't handle non-finite values.
Results may differ from the reference program's by a relative error of at most 0.017.
Values may be sent and summed in bfloat16 or wider, within the bound.
No kernel may reach another device: no remote copies, remote signals or barrier semaphores. Data moves between devices by JAX's collectives and lax.ppermute only.
A program may use at most 64 MiB of HBM per device.

```python
import math
import jax
import jax.numpy as jnp
from jax import lax

D = 4096
QH = 8
HD = 128
BLOCK = 128
SEQ = 4096
GROUPS = 16
NBLK = 32


def draw_precision(key, part):
    key = jax.random.fold_in(key, 7)
    picked = jax.random.randint(key, (GROUPS, NBLK, 2), 0, 3)
    return lax.shift_left(jnp.full((GROUPS, NBLK, 2), 2, jnp.int32), picked.astype(jnp.int32))


def raised(values, stream_key, source, target, blocks, factor):
    def block_of(axis_at):
        return (jnp.arange(values.shape[axis_at]) // (values.shape[axis_at] // blocks)).reshape((-1,) + (1,) * (values.ndim - 1 - axis_at))

    first = jax.random.permutation(stream_key, blocks)[block_of(target)]
    other_side = (block_of(target) + blocks // 2) % blocks
    return jnp.where((block_of(source) == first) | (block_of(source) == other_side), factor * values, values)


def shard_levels(own_key, extent, split, smallest, top_value):
    def one(dim, blocks):
        heights = jax.random.uniform(jax.random.fold_in(jax.random.fold_in(own_key, 6), dim), (blocks,), jnp.float32, smallest / len(split), top_value / len(split))
        return jnp.repeat(jnp.exp(heights), extent[dim] // blocks).reshape((-1,) + (1,) * (len(extent) - dim - 1))

    level = one(*split[0])
    for cut in split[1:]:
        level = level * one(*cut)
    return level


def normal_values(stream_key, shape, spread, bound, cuts=(), kind=jnp.bfloat16):
    factor_of = shard_levels(stream_key, shape, cuts, -0.22, 0.18) if cuts else 1.0
    drawn = jax.random.normal(stream_key, shape, jnp.float32) * spread * factor_of
    return jnp.minimum(jnp.maximum(drawn, -bound), bound).astype(kind)


def bell_draw_with(stream_key, extent, deviation, most, pieces, heavy, kind=jnp.bfloat16):
    array = deviation * jax.random.normal(stream_key, extent, jnp.float32)
    if pieces:
        array = array * shard_levels(stream_key, extent, pieces, -0.22, 0.18)
    return jnp.clip(raised(array, jax.random.fold_in(stream_key, 3), *heavy), -most, most).astype(kind)


def setup_inputs(seed: int = 0) -> dict:
    keys = jax.random.split(jax.random.key(seed), 7)
    return {
        "hidden_in": bell_draw_with(keys[0], (GROUPS, SEQ, D), 1.0, 6.0, ((0, 16), (1, 32)), (0, 2, 16, 2.0)),
        "queries": normal_values(keys[1], (GROUPS, SEQ, QH * HD), 1.0, 6.0, ((0, 16), (1, 32))),
        "out_grad": normal_values(keys[2], (GROUPS, SEQ, QH * HD), 4.0, 16.0, ((0, 16), (1, 32))),
        "kv_weight": normal_values(keys[3], (D, 2 * HD), D ** -0.5, 0.09375, ((0, 16),)),
        "block_pos": jax.vmap(lambda own: jax.random.permutation(own, NBLK))(jax.random.split(keys[4], GROUPS)).reshape((GROUPS, NBLK)).astype(jnp.int32),
        "precision": draw_precision(jax.random.fold_in(keys[6], 71), 0),
    }


EPSILON = 1e-06

def frequencies(size):
    expo = jnp.arange(0, size, 2).astype(jnp.float32) / size
    base = 1.0 / jnp.power(jnp.float32(500000.0), expo)
    wavelen = 2.0 * math.pi / base
    mixing = (8192.0 / wavelen - 1.0) / 3.0
    blended = (1.0 - mixing) * base / 8.0 + mixing * base
    return jnp.where(wavelen < 2048.0, base, jnp.where(wavelen > 8192.0, base / 8.0, blended))

def rotate(values, cosine, sine_part):
    half = values.shape[1] // 2
    first, second = (values[:, :half], values[:, half:])
    return jnp.concatenate([first * cosine - second * sine_part, second * cosine + first * sine_part], axis=1)

def rotate_back(grads, cosine, sine_part):
    half = grads.shape[1] // 2
    first, second = (grads[:, :half], grads[:, half:])
    return jnp.concatenate([first * cosine + second * sine_part, second * cosine - first * sine_part], axis=1)

def softstep(scaled):
    return scaled - jnp.sin(2.0 * math.pi * scaled) / (2.0 * math.pi)

def quantize(values, bits_here):
    nblocks = bits_here.shape[0]
    grouped = values.reshape(nblocks, values.shape[0] // nblocks, values.shape[1])
    largest = lax.optimization_barrier(jnp.max(jnp.abs(grouped), axis=1, keepdims=True))
    levels = (lax.shift_left(jnp.ones_like(bits_here), bits_here - 1) - 1).astype(jnp.float32)
    level_step = (largest + EPSILON) / levels[:, None, None]
    return (level_step * softstep(grouped / level_step)).reshape(values.shape)

def matmul(left, right):
    return jnp.dot(left.astype(jnp.float32), right.astype(jnp.float32), preferred_element_type=jnp.float32)

def reference(hidden_in, queries, out_grad, kv_weight, block_pos, precision):
    score_scale = 1.0 / math.sqrt(HD)
    inv_freq = frequencies(HD)

    def one_group(w_sum, group_items):
        x_rows, query_rows, dout_all, layout, bits_here = group_items
        projected = matmul(x_rows, kv_weight)
        positions = (layout[:, None] * BLOCK + jnp.arange(BLOCK, dtype=jnp.int32)[None, :]).reshape(-1)
        angles = positions.astype(jnp.float32)[:, None] * inv_freq[None, :]
        cosine = jnp.cos(angles)
        sine_part = jnp.sin(angles)
        key_quant = quantize(rotate(projected[:, :HD], cosine, sine_part), bits_here[:, 0]).astype(jnp.bfloat16)
        value_quant = quantize(projected[:, HD:], bits_here[:, 1]).astype(jnp.bfloat16)
        query_blocks = query_rows.reshape(NBLK, BLOCK * QH, HD)
        dout_blocks = dout_all.reshape(NBLK, BLOCK * QH, HD)
        pos_blocks = positions.reshape(NBLK, BLOCK)

        def query_block(running, block_items):
            q_rows, d_rows, qpos = block_items
            row_pos = jnp.repeat(qpos, QH)
            visible = positions[None, :] <= row_pos[:, None]
            scores = matmul(q_rows, key_quant.T) * score_scale
            exponent = jnp.where(visible, jnp.exp(scores), 0.0)
            row_total = lax.optimization_barrier(jnp.sum(exponent, axis=1))
            numerator = matmul(exponent.astype(jnp.bfloat16), value_quant)
            attended = numerator / row_total[:, None]
            row_delta = lax.optimization_barrier(jnp.sum(d_rows.astype(jnp.float32) * attended, axis=1))
            log_total = jnp.log(row_total)
            probs = jnp.where(visible, jnp.exp(scores - log_total[:, None]), 0.0)
            probs_low = probs.astype(jnp.bfloat16)
            value_grad = matmul(probs_low.T, d_rows)
            prob_grad = matmul(d_rows, value_quant.T)
            score_grad = (probs * (prob_grad - row_delta[:, None])).astype(jnp.bfloat16)
            dq_block = matmul(score_grad, key_quant) * score_scale
            key_grad = matmul(score_grad.T, q_rows)
            return (running + jnp.concatenate([key_grad, value_grad], axis=1), dq_block.astype(jnp.bfloat16))
        running, dq_all = lax.scan(query_block, jnp.zeros((SEQ, 2 * HD), jnp.float32), (query_blocks, dout_blocks, pos_blocks))
        key_part = rotate_back(running[:, :HD] * score_scale, cosine, sine_part)
        proj_grad = jnp.concatenate([key_part, running[:, HD:]], axis=1).astype(jnp.bfloat16)
        x_grad = matmul(proj_grad, kv_weight.T).astype(jnp.bfloat16)
        w_sum = w_sum + matmul(x_rows.T, proj_grad)
        return (w_sum, (dq_all.reshape(SEQ, QH * HD), proj_grad, x_grad))
    w_sum, (query_grad, kv_grad, input_grad) = lax.scan(one_group, jnp.zeros((D, 2 * HD), jnp.float32), (hidden_in, queries, out_grad, block_pos, precision))
    weight_grad = w_sum * (1.0 / math.sqrt(GROUPS * SEQ))
    return (query_grad, kv_grad, input_grad, weight_grad)
```

```python
import functools
import math

import jax
import jax.numpy as jnp
from jax import lax
from jax.experimental import pallas as pl
from jax.experimental.pallas import tpu as pltpu
from jax.sharding import PartitionSpec as P

QH = 8
HD = 128
BLOCK = 128
TILE_BLOCKS = 4

EPSILON = 1e-06
LOG2E = math.log2(math.e)


def frequencies(size):
    expo = jnp.arange(0, size, 2).astype(jnp.float32) / size
    base = 1.0 / jnp.power(jnp.float32(500000.0), expo)
    wavelen = 2.0 * math.pi / base
    mixing = (8192.0 / wavelen - 1.0) / 3.0
    blended = (1.0 - mixing) * base / 8.0 + mixing * base
    return jnp.where(wavelen < 2048.0, base, jnp.where(wavelen > 8192.0, base / 8.0, blended))


def rotate(values, cosine, sine_part):
    half = values.shape[1] // 2
    first, second = (values[:, :half], values[:, half:])
    return jnp.concatenate(
        [first * cosine - second * sine_part, second * cosine + first * sine_part], axis=1
    )


def rotate_back(grads, cosine, sine_part):
    half = grads.shape[1] // 2
    first, second = (grads[:, :half], grads[:, half:])
    return jnp.concatenate(
        [first * cosine + second * sine_part, second * cosine - first * sine_part], axis=1
    )


def softstep(scaled):
    return scaled - jnp.sin(2.0 * math.pi * scaled) / (2.0 * math.pi)


def quantize(values, bits_here):
    nblocks = bits_here.shape[0]
    grouped = values.reshape(nblocks, values.shape[0] // nblocks, values.shape[1])
    largest = jnp.max(jnp.abs(grouped), axis=1, keepdims=True)
    levels = (lax.shift_left(jnp.ones_like(bits_here), bits_here - 1) - 1).astype(jnp.float32)
    level_step = (largest + EPSILON) / levels[:, None, None]
    return (level_step * softstep(grouped / level_step)).reshape(values.shape)


def dot_rows(left, right):
    return lax.dot_general(
        left, right, (((0,), (0,)), ((), ())), preferred_element_type=jnp.float32
    )


def dot_cols(left, right):
    return lax.dot_general(
        left, right, (((1,), (1,)), ((), ())), preferred_element_type=jnp.float32
    )


def dot(left, right):
    return jnp.dot(left, right, preferred_element_type=jnp.float32)


def attention_kernel(
    order_ref, place_ref, near_ref, far_ref, q_ref, g_ref,
    dq_ref, near_grad_ref, far_grad_ref,
    exp_store, prob_store, top_store, q_cols, g_cols, q_rows, g_rows, dq_cols,
):
    side = near_ref.shape[0]
    blocks = 2 * side
    rows = QH * BLOCK
    span = TILE_BLOCKS * BLOCK
    score_scale = LOG2E / math.sqrt(HD)
    place = place_ref[0]
    tiles = lax.div(place + TILE_BLOCKS, TILE_BLOCKS)

    for head in range(QH):
        part = pl.ds(head * HD, HD)
        q_cols[:, part] = q_ref[:, part].T
        g_cols[:, part] = g_ref[:, part].T
        q_rows[part, :] = q_ref[:, part]
        g_rows[part, :] = g_ref[:, part]
    dq_cols[...] = jnp.zeros_like(dq_cols)

    def gathered(tile):
        found = []
        for step in range(TILE_BLOCKS):
            slot = order_ref[tile * TILE_BLOCKS + step]
            near = near_ref[jnp.minimum(slot, side - 1)]
            far = far_ref[jnp.maximum(slot - side, 0)]
            found.append(jnp.where(slot < side, near, far))
        return jnp.concatenate(found, axis=0)

    def folded(values):
        return jnp.sum(values.reshape(span // 8, 8, rows), axis=0)

    def forward(tile, sums, masked):
        total, weighted, top = sums
        keys = gathered(tile)
        scores = dot(keys[:, :HD], q_cols[...]) * score_scale
        if masked:
            key_at = tile * span + lax.broadcasted_iota(jnp.int32, (span, rows), 0)
            row_at = place * BLOCK + lax.rem(
                lax.broadcasted_iota(jnp.int32, (span, rows), 1), BLOCK
            )
            visible = key_at <= row_at
            scores = jnp.where(visible, scores, -jnp.inf)
        highest = jnp.maximum(top, jnp.max(scores, axis=0, keepdims=True))
        shrink = jnp.exp2(top - highest)
        exponent = jnp.exp2(scores - highest)
        prob_grad = dot(keys[:, HD:], g_cols[...])
        exp_store[tile] = exponent
        prob_store[tile] = prob_grad
        top_store[tile] = highest
        total = total * shrink + folded(exponent)
        weighted = weighted * shrink + folded(exponent * prob_grad)
        return (total, weighted, highest)

    empty = jnp.zeros((8, rows), jnp.float32)
    start = forward(tiles - 1, (empty, empty, jnp.full((1, rows), -1e30, jnp.float32)), True)
    total, weighted, top = lax.fori_loop(
        0, tiles - 1, lambda tile, sums: forward(tile, sums, False), start
    )
    inverse = 1.0 / jnp.sum(total, axis=0, keepdims=True)
    row_delta = jnp.sum(weighted, axis=0, keepdims=True) * inverse

    def store(slot, value):
        @pl.when(slot < side)
        def _():
            near_grad_ref[slot] = value

        @pl.when(slot >= side)
        def _():
            far_grad_ref[slot - side] = value

    @pl.loop(0, tiles)
    def _(tile):
        keys = gathered(tile)[:, :HD]
        factor = jnp.exp2(top_store[tile] - top) * inverse
        probs = exp_store[tile] * factor
        score_grad = (probs * (prob_store[tile] - row_delta)).astype(jnp.bfloat16)
        value_grad = dot(probs.astype(jnp.bfloat16), g_rows[...])
        key_grad = dot(score_grad, q_rows[...])
        dq_cols[...] += dot(keys.T, score_grad)
        grads = jnp.concatenate([key_grad, value_grad], axis=1).astype(jnp.bfloat16)
        for step in range(TILE_BLOCKS):
            store(
                order_ref[tile * TILE_BLOCKS + step], grads[step * BLOCK : (step + 1) * BLOCK]
            )

    @pl.loop(tiles * TILE_BLOCKS, blocks)
    def _(place_at):
        store(order_ref[place_at], jnp.zeros((BLOCK, 2 * HD), jnp.bfloat16))

    for head in range(QH):
        part = pl.ds(head * HD, HD)
        dq_ref[:, part] = (dq_cols[:, part].T * (1.0 / math.sqrt(HD))).astype(jnp.bfloat16)


def attention_backward(order, place, near, far, queries, out_grad):
    tokens = queries.shape[0]
    rows = QH * tokens
    blocks = 2 * near.shape[0]
    tiles = blocks // TILE_BLOCKS
    span = TILE_BLOCKS * BLOCK
    smem = pl.BlockSpec(memory_space=pltpu.SMEM)
    vmem = pl.BlockSpec(memory_space=pltpu.VMEM)
    return pl.pallas_call(
        attention_kernel,
        out_shape=(
            jax.ShapeDtypeStruct(queries.shape, jnp.bfloat16),
            jax.ShapeDtypeStruct(near.shape, jnp.bfloat16),
            jax.ShapeDtypeStruct(far.shape, jnp.bfloat16),
        ),
        in_specs=[smem, smem, vmem, vmem, vmem, vmem],
        out_specs=(vmem, vmem, vmem),
        scratch_shapes=[
            pltpu.VMEM((tiles, span, rows), jnp.float32),
            pltpu.VMEM((tiles, span, rows), jnp.float32),
            pltpu.VMEM((tiles, 1, rows), jnp.float32),
            pltpu.VMEM((HD, rows), jnp.bfloat16),
            pltpu.VMEM((HD, rows), jnp.bfloat16),
            pltpu.VMEM((rows, HD), jnp.bfloat16),
            pltpu.VMEM((rows, HD), jnp.bfloat16),
            pltpu.VMEM((HD, rows), jnp.float32),
        ],
        compiler_params=pltpu.CompilerParams(vmem_limit_bytes=56 * 1024 * 1024),
        name="attention_backward",
    )(order, place, near, far, queries, out_grad)


def spread(value, axis, groups=None):
    count = lax.axis_size(axis) if groups is None else len(groups[0])
    copies = lax.optimization_barrier(jnp.broadcast_to(value[None], (count, *value.shape)))
    return lax.all_to_all(copies, axis, 0, 0, axis_index_groups=groups)


def added(value, axis, groups=None):
    arrived = lax.all_to_all(value, axis, 0, 0, axis_index_groups=groups)
    return jnp.sum(arrived.astype(jnp.float32), axis=0)


def body(hidden_in, queries, out_grad, kv_weight, block_pos, precision):
    score_scale = 1.0 / math.sqrt(HD)
    tokens = hidden_in.shape[1]
    width = hidden_in.shape[2]
    seq_count = lax.axis_size("seq")
    dp_count = lax.axis_size("dp")
    chips = seq_count // 2
    grad_scale = 1.0 / math.sqrt(dp_count * seq_count * tokens)
    self_index = lax.axis_index("seq")
    core = lax.rem(self_index, 2)
    is_first = core == 0
    same_core = [[2 * chip + side for chip in range(chips)] for side in range(2)]
    swap = [(source, source ^ 1) for source in range(seq_count)]

    def swapped(value):
        return lax.ppermute(value, "seq", swap)

    x_rows = hidden_in[0]
    places = block_pos[0]
    place = lax.dynamic_slice_in_dim(places, self_index, 1)
    by_core = places.reshape(chips, 2)
    slot_places = jnp.where(
        is_first,
        jnp.concatenate([by_core[:, 0], by_core[:, 1]]),
        jnp.concatenate([by_core[:, 1], by_core[:, 0]]),
    )
    slots = jnp.arange(seq_count, dtype=jnp.int32)
    order = jnp.sum(
        jnp.where(slot_places[None, :] == slots[:, None], slots[None, :], 0), axis=1
    ).astype(jnp.int32)
    my_pos = place * BLOCK + jnp.arange(tokens, dtype=jnp.int32)
    angles = my_pos.astype(jnp.float32)[:, None] * frequencies(HD)[None, :]
    cosine = jnp.cos(angles)
    sine_part = jnp.sin(angles)

    with jax.named_scope("weight_gather"):
        half = jnp.where(is_first, kv_weight[:, :HD], kv_weight[:, HD:])
        near_weight = spread(half, "dp").reshape(width, HD)
        far_weight = swapped(near_weight)
    with jax.named_scope("projection"):
        near_raw = dot(x_rows, near_weight)
        far_raw = dot(x_rows, far_weight)
        raw_keys = jnp.where(is_first, near_raw, far_raw)
        raw_values = jnp.where(is_first, far_raw, near_raw)
        key_quant = quantize(rotate(raw_keys, cosine, sine_part), precision[0, :, 0])
        value_quant = quantize(raw_values, precision[0, :, 1])
        stacked = jnp.concatenate([key_quant, value_quant], axis=1).astype(jnp.bfloat16)
    with jax.named_scope("kv_gather"):
        near = spread(stacked, "seq", same_core)
        far = swapped(near)
    with jax.named_scope("attention"):
        query_grad, near_grad, far_grad = attention_backward(
            order, place, near, far, queries[0], out_grad[0]
        )
    with jax.named_scope("kv_reduce"):
        pair = near_grad.astype(jnp.float32) + swapped(far_grad).astype(jnp.float32)
        carried = added(pair.astype(jnp.bfloat16), "seq", same_core)
    with jax.named_scope("projection_grad"):
        key_part = rotate_back(carried[:, :HD] * score_scale, cosine, sine_part)
        proj_grad = jnp.concatenate([key_part, carried[:, HD:]], axis=1).astype(jnp.bfloat16)
    with jax.named_scope("weight_grad"):
        share = dot_rows(x_rows, proj_grad).reshape(dp_count, 2, width // dp_count // 2, 2 * HD)
        kept = jnp.where(is_first, share[:, 0], share[:, 1])
        given = jnp.where(is_first, share[:, 1], share[:, 0]).astype(jnp.bfloat16)
        pair_share = kept + swapped(given).astype(jnp.float32)
        group_sum = added(pair_share.astype(jnp.bfloat16), "dp")
        piece = group_sum.shape[0] // chips
        chip_sum = added(
            group_sum.astype(jnp.bfloat16).reshape(chips, piece, 2 * HD), "seq", same_core
        )
        gathered = spread(chip_sum * grad_scale, "seq")
        weight_grad = (
            gathered.reshape(chips, 2, piece, 2 * HD)
            .transpose(1, 0, 2, 3)
            .reshape(width // dp_count, 2 * HD)
        )
    with jax.named_scope("input_grad"):
        key_weight = jnp.where(is_first, near_weight, far_weight)
        value_weight = jnp.where(is_first, far_weight, near_weight)
        weight = jnp.concatenate([key_weight, value_weight], axis=1)
        input_grad = dot_cols(proj_grad, weight).astype(jnp.bfloat16)
    return (query_grad[None], proj_grad[None], input_grad[None], weight_grad)


def solution(mesh):
    in_specs = (
        P("dp", "seq", None),
        P("dp", "seq", None),
        P("dp", "seq", None),
        P("dp", None),
        P("dp", None),
        P("dp", "seq", None),
    )
    out_specs = (P("dp", "seq", None), P("dp", "seq", None), P("dp", "seq", None), P("dp", None))
    return jax.shard_map(body, mesh=mesh, in_specs=in_specs, out_specs=out_specs, check_vma=False)
```

```python
import functools
import math

import jax
import jax.numpy as jnp
from jax import lax
from jax.experimental import pallas as pl
from jax.experimental.pallas import tpu as pltpu
from jax.sharding import PartitionSpec as P

QH = 8
HD = 128
BLOCK = 128
TILE_BLOCKS = 4

EPSILON = 1e-06
LOG2E = math.log2(math.e)


def frequencies(size):
    expo = jnp.arange(0, size, 2).astype(jnp.float32) / size
    base = 1.0 / jnp.power(jnp.float32(500000.0), expo)
    wavelen = 2.0 * math.pi / base
    mixing = (8192.0 / wavelen - 1.0) / 3.0
    blended = (1.0 - mixing) * base / 8.0 + mixing * base
    return jnp.where(wavelen < 2048.0, base, jnp.where(wavelen > 8192.0, base / 8.0, blended))


def rotate(values, cosine, sine_part):
    half = values.shape[1] // 2
    first, second = (values[:, :half], values[:, half:])
    return jnp.concatenate(
        [first * cosine - second * sine_part, second * cosine + first * sine_part], axis=1
    )


def rotate_back(grads, cosine, sine_part):
    half = grads.shape[1] // 2
    first, second = (grads[:, :half], grads[:, half:])
    return jnp.concatenate(
        [first * cosine + second * sine_part, second * cosine - first * sine_part], axis=1
    )


def softstep(scaled):
    return scaled - jnp.sin(2.0 * math.pi * scaled) / (2.0 * math.pi)


def quantize(values, bits_here):
    nblocks = bits_here.shape[0]
    grouped = values.reshape(nblocks, values.shape[0] // nblocks, values.shape[1])
    largest = jnp.max(jnp.abs(grouped), axis=1, keepdims=True)
    levels = (lax.shift_left(jnp.ones_like(bits_here), bits_here - 1) - 1).astype(jnp.float32)
    level_step = (largest + EPSILON) / levels[:, None, None]
    return (level_step * softstep(grouped / level_step)).reshape(values.shape)


def dot_rows(left, right):
    return lax.dot_general(
        left, right, (((0,), (0,)), ((), ())), preferred_element_type=jnp.float32
    )


def dot_cols(left, right):
    return lax.dot_general(
        left, right, (((1,), (1,)), ((), ())), preferred_element_type=jnp.float32
    )


def dot(left, right):
    return jnp.dot(left, right, preferred_element_type=jnp.float32)


def attention_kernel(
    order_ref, place_ref, near_ref, far_ref, q_ref, g_ref,
    dq_ref, near_grad_ref, far_grad_ref,
    exp_store, prob_store, top_store, q_cols, g_cols, q_rows, g_rows, dq_cols,
):
    side = near_ref.shape[0]
    blocks = 2 * side
    rows = QH * BLOCK
    span = TILE_BLOCKS * BLOCK
    score_scale = LOG2E / math.sqrt(HD)
    place = place_ref[0]
    tiles = lax.div(place + TILE_BLOCKS, TILE_BLOCKS)

    for head in range(QH):
        part = pl.ds(head * HD, HD)
        q_cols[:, part] = q_ref[:, part].T
        g_cols[:, part] = g_ref[:, part].T
        q_rows[part, :] = q_ref[:, part]
        g_rows[part, :] = g_ref[:, part]
    dq_cols[...] = jnp.zeros_like(dq_cols)

    def gathered(tile):
        found = []
        for step in range(TILE_BLOCKS):
            slot = order_ref[tile * TILE_BLOCKS + step]
            near = near_ref[jnp.minimum(slot, side - 1)]
            far = far_ref[jnp.maximum(slot - side, 0)]
            found.append(jnp.where(slot < side, near, far))
        return jnp.concatenate(found, axis=0)

    def folded(values):
        return jnp.sum(values.reshape(span // 8, 8, rows), axis=0)

    def forward(tile, sums, masked):
        total, weighted, top = sums
        keys = gathered(tile)
        scores = dot(keys[:, :HD], q_cols[...]) * score_scale
        if masked:
            key_at = tile * span + lax.broadcasted_iota(jnp.int32, (span, rows), 0)
            row_at = place * BLOCK + lax.rem(
                lax.broadcasted_iota(jnp.int32, (span, rows), 1), BLOCK
            )
            visible = key_at <= row_at
            scores = jnp.where(visible, scores, -jnp.inf)
        highest = jnp.maximum(top, jnp.max(scores, axis=0, keepdims=True))
        shrink = jnp.exp2(top - highest)
        exponent = jnp.exp2(scores - highest)
        prob_grad = dot(keys[:, HD:], g_cols[...])
        exp_store[tile] = exponent
        prob_store[tile] = prob_grad
        top_store[tile] = highest
        total = total * shrink + folded(exponent)
        weighted = weighted * shrink + folded(exponent * prob_grad)
        return (total, weighted, highest)

    empty = jnp.zeros((8, rows), jnp.float32)
    start = forward(tiles - 1, (empty, empty, jnp.full((1, rows), -1e30, jnp.float32)), True)
    total, weighted, top = lax.fori_loop(
        0, tiles - 1, lambda tile, sums: forward(tile, sums, False), start
    )
    inverse = 1.0 / jnp.sum(total, axis=0, keepdims=True)
    row_delta = jnp.sum(weighted, axis=0, keepdims=True) * inverse

    def store(slot, value):
        @pl.when(slot < side)
        def _():
            near_grad_ref[slot] = value

        @pl.when(slot >= side)
        def _():
            far_grad_ref[slot - side] = value

    @pl.loop(0, tiles)
    def _(tile):
        keys = gathered(tile)[:, :HD]
        factor = jnp.exp2(top_store[tile] - top) * inverse
        probs = exp_store[tile] * factor
        score_grad = (probs * (prob_store[tile] - row_delta)).astype(jnp.bfloat16)
        value_grad = dot(probs.astype(jnp.bfloat16), g_rows[...])
        key_grad = dot(score_grad, q_rows[...])
        dq_cols[...] += dot(keys.T, score_grad)
        grads = jnp.concatenate([key_grad, value_grad], axis=1).astype(jnp.bfloat16)
        for step in range(TILE_BLOCKS):
            store(
                order_ref[tile * TILE_BLOCKS + step], grads[step * BLOCK : (step + 1) * BLOCK]
            )

    @pl.loop(tiles * TILE_BLOCKS, blocks)
    def _(place_at):
        store(order_ref[place_at], jnp.zeros((BLOCK, 2 * HD), jnp.bfloat16))

    for head in range(QH):
        part = pl.ds(head * HD, HD)
        dq_ref[:, part] = (dq_cols[:, part].T * (1.0 / math.sqrt(HD))).astype(jnp.bfloat16)


def attention_backward(order, place, near, far, queries, out_grad):
    tokens = queries.shape[0]
    rows = QH * tokens
    blocks = 2 * near.shape[0]
    tiles = blocks // TILE_BLOCKS
    span = TILE_BLOCKS * BLOCK
    smem = pl.BlockSpec(memory_space=pltpu.SMEM)
    vmem = pl.BlockSpec(memory_space=pltpu.VMEM)
    return pl.pallas_call(
        attention_kernel,
        out_shape=(
            jax.ShapeDtypeStruct(queries.shape, jnp.bfloat16),
            jax.ShapeDtypeStruct(near.shape, jnp.bfloat16),
            jax.ShapeDtypeStruct(far.shape, jnp.bfloat16),
        ),
        in_specs=[smem, smem, vmem, vmem, vmem, vmem],
        out_specs=(vmem, vmem, vmem),
        scratch_shapes=[
            pltpu.VMEM((tiles, span, rows), jnp.float32),
            pltpu.VMEM((tiles, span, rows), jnp.float32),
            pltpu.VMEM((tiles, 1, rows), jnp.float32),
            pltpu.VMEM((HD, rows), jnp.bfloat16),
            pltpu.VMEM((HD, rows), jnp.bfloat16),
            pltpu.VMEM((rows, HD), jnp.bfloat16),
            pltpu.VMEM((rows, HD), jnp.bfloat16),
            pltpu.VMEM((HD, rows), jnp.float32),
        ],
        compiler_params=pltpu.CompilerParams(vmem_limit_bytes=56 * 1024 * 1024),
        name="attention_backward",
    )(order, place, near, far, queries, out_grad)


def share_kernel(side_ref, x_ref, grad_ref, out_ref):
    columns, groups, piece, _ = out_ref.shape
    part = columns * piece
    grads = grad_ref[...]
    for group in range(groups):
        start = pl.multiple_of((2 * group + side_ref[0]) * part, part)
        chosen = x_ref[:, pl.ds(start, part)].T
        share = dot(chosen, grads).astype(out_ref.dtype)
        for column in range(columns):
            out_ref[column, group] = share[column * piece : (column + 1) * piece]


def weight_share(side, x_rows, proj_grad, columns, groups, kind):
    piece = x_rows.shape[1] // groups // columns // 2
    vmem = pl.BlockSpec(memory_space=pltpu.VMEM)
    return pl.pallas_call(
        share_kernel,
        out_shape=jax.ShapeDtypeStruct((columns, groups, piece, proj_grad.shape[1]), kind),
        in_specs=[pl.BlockSpec(memory_space=pltpu.SMEM), vmem, vmem],
        out_specs=vmem,
        compiler_params=pltpu.CompilerParams(vmem_limit_bytes=32 * 1024 * 1024),
        name="weight_share",
    )(side, x_rows, proj_grad)


def spread(value, axis, groups=None):
    count = lax.axis_size(axis) if groups is None else len(groups[0])
    copies = lax.optimization_barrier(jnp.broadcast_to(value[None], (count, *value.shape)))
    return lax.all_to_all(copies, axis, 0, 0, axis_index_groups=groups)


def added(value, axis, groups=None):
    arrived = lax.all_to_all(value, axis, 0, 0, axis_index_groups=groups)
    return jnp.sum(arrived.astype(jnp.float32), axis=0)


def body(hidden_in, queries, out_grad, kv_weight, block_pos, precision):
    score_scale = 1.0 / math.sqrt(HD)
    tokens = hidden_in.shape[1]
    width = hidden_in.shape[2]
    seq_count = lax.axis_size("seq")
    dp_count = lax.axis_size("dp")
    half_count = seq_count // 2
    columns = half_count // 2
    grad_scale = 1.0 / math.sqrt(dp_count * seq_count * tokens)
    self_index = lax.axis_index("seq")
    core = lax.rem(self_index, 2)
    is_first = core == 0
    in_low = self_index < half_count
    column_groups = [
        [start * half_count + 2 * column + side for column in range(columns)]
        for start in range(2)
        for side in range(2)
    ]
    row_count = math.gcd(dp_count, 4)
    runs = [
        [start + step for step in range(row_count)] for start in range(0, dp_count, row_count)
    ]
    strides = [
        [start + step for step in range(0, dp_count, row_count)] for start in range(row_count)
    ]
    swap = [(source, source ^ 1) for source in range(seq_count)]
    cross = [(source, (source + half_count) % seq_count) for source in range(seq_count)]

    def swapped(value):
        return lax.ppermute(value, "seq", swap)

    def crossed(value):
        return lax.ppermute(value, "seq", cross)

    x_rows = hidden_in[0]
    places = block_pos[0]
    place = lax.dynamic_slice_in_dim(places, self_index, 1)
    cube = places.reshape(2, columns, 2)
    cube = jnp.where(in_low, cube, cube[::-1])
    cube = jnp.where(is_first, cube, cube[:, :, ::-1])
    slot_places = cube.transpose(2, 1, 0).reshape(-1)
    slots = jnp.arange(seq_count, dtype=jnp.int32)
    order = jnp.sum(
        jnp.where(slot_places[None, :] == slots[:, None], slots[None, :], 0), axis=1
    ).astype(jnp.int32)
    my_pos = place * BLOCK + jnp.arange(tokens, dtype=jnp.int32)
    angles = my_pos.astype(jnp.float32)[:, None] * frequencies(HD)[None, :]
    cosine = jnp.cos(angles)
    sine_part = jnp.sin(angles)

    with jax.named_scope("weight_gather"):
        half = jnp.where(is_first, kv_weight[:, :HD], kv_weight[:, HD:])
        run_weight = spread(half, "dp", runs)
        near_weight = spread(run_weight, "dp", strides).reshape(width, HD)
        far_weight = swapped(near_weight)
    with jax.named_scope("projection"):
        near_raw = dot(x_rows, near_weight)
        far_raw = dot(x_rows, far_weight)
        raw_keys = jnp.where(is_first, near_raw, far_raw)
        raw_values = jnp.where(is_first, far_raw, near_raw)
        key_quant = quantize(rotate(raw_keys, cosine, sine_part), precision[0, :, 0])
        value_quant = quantize(raw_values, precision[0, :, 1])
        stacked = jnp.concatenate([key_quant, value_quant], axis=1).astype(jnp.bfloat16)
    with jax.named_scope("kv_gather"):
        both = jnp.stack([stacked, crossed(stacked)])
        near = spread(both, "seq", column_groups).reshape(half_count, tokens, 2 * HD)
        far = swapped(near)
    with jax.named_scope("attention"):
        query_grad, near_grad, far_grad = attention_backward(
            order, place, near, far, queries[0], out_grad[0]
        )
    with jax.named_scope("kv_reduce"):
        pair = near_grad.astype(jnp.float32) + swapped(far_grad).astype(jnp.float32)
        column_sum = added(
            pair.astype(jnp.bfloat16).reshape(columns, 2, tokens, 2 * HD), "seq", column_groups
        )
        carried = column_sum[0] + crossed(column_sum[1].astype(jnp.bfloat16)).astype(jnp.float32)
    with jax.named_scope("projection_grad"):
        key_part = rotate_back(carried[:, :HD] * score_scale, cosine, sine_part)
        proj_grad = jnp.concatenate([key_part, carried[:, HD:]], axis=1).astype(jnp.bfloat16)
    with jax.named_scope("weight_grad"):
        side = core.reshape(1).astype(jnp.int32)
        given = weight_share(1 - side, x_rows, proj_grad, columns, dp_count, jnp.bfloat16)
        kept = weight_share(side, x_rows, proj_grad, columns, dp_count, jnp.float32)
        pair_share = kept + swapped(given).astype(jnp.float32)
        column_share = added(pair_share.astype(jnp.bfloat16), "seq", column_groups)
        group_share = added(column_share.astype(jnp.bfloat16), "dp")
        gathered = spread(group_share.astype(jnp.bfloat16), "seq")
        piece = group_share.shape[0]
        weight_grad = (
            jnp.sum(
                gathered.reshape(2, columns, 2, piece, 2 * HD).astype(jnp.float32), axis=0
            )
            .transpose(1, 0, 2, 3)
            .reshape(width // dp_count, 2 * HD)
        ) * grad_scale
    with jax.named_scope("input_grad"):
        key_weight = jnp.where(is_first, near_weight, far_weight)
        value_weight = jnp.where(is_first, far_weight, near_weight)
        weight = jnp.concatenate([key_weight, value_weight], axis=1)
        input_grad = dot_cols(proj_grad, weight).astype(jnp.bfloat16)
    return (query_grad[None], proj_grad[None], input_grad[None], weight_grad)


def solution(mesh):
    in_specs = (
        P("dp", "seq", None),
        P("dp", "seq", None),
        P("dp", "seq", None),
        P("dp", None),
        P("dp", None),
        P("dp", "seq", None),
    )
    out_specs = (P("dp", "seq", None), P("dp", "seq", None), P("dp", "seq", None), P("dp", None))
    return jax.shard_map(body, mesh=mesh, in_specs=in_specs, out_specs=out_specs, check_vma=False)
```

```python
import functools
import math

import jax
import jax.numpy as jnp
from jax import lax
from jax.experimental import pallas as pl
from jax.experimental.pallas import tpu as pltpu
from jax.sharding import PartitionSpec as P

QH = 8
HD = 128
BLOCK = 128
TILE_BLOCKS = 4

EPSILON = 1e-06
LOG2E = math.log2(math.e)


def frequencies(size):
    expo = jnp.arange(0, size, 2).astype(jnp.float32) / size
    base = 1.0 / jnp.power(jnp.float32(500000.0), expo)
    wavelen = 2.0 * math.pi / base
    mixing = (8192.0 / wavelen - 1.0) / 3.0
    blended = (1.0 - mixing) * base / 8.0 + mixing * base
    return jnp.where(wavelen < 2048.0, base, jnp.where(wavelen > 8192.0, base / 8.0, blended))


def rotate(values, cosine, sine_part):
    half = values.shape[1] // 2
    first, second = (values[:, :half], values[:, half:])
    return jnp.concatenate(
        [first * cosine - second * sine_part, second * cosine + first * sine_part], axis=1
    )


def rotate_back(grads, cosine, sine_part):
    half = grads.shape[1] // 2
    first, second = (grads[:, :half], grads[:, half:])
    return jnp.concatenate(
        [first * cosine + second * sine_part, second * cosine - first * sine_part], axis=1
    )


def softstep(scaled):
    return scaled - jnp.sin(2.0 * math.pi * scaled) / (2.0 * math.pi)


def quantize(values, bits_here):
    nblocks = bits_here.shape[0]
    grouped = values.reshape(nblocks, values.shape[0] // nblocks, values.shape[1])
    largest = jnp.max(jnp.abs(grouped), axis=1, keepdims=True)
    levels = (lax.shift_left(jnp.ones_like(bits_here), bits_here - 1) - 1).astype(jnp.float32)
    level_step = (largest + EPSILON) / levels[:, None, None]
    return (level_step * softstep(grouped / level_step)).reshape(values.shape)


def dot_rows(left, right):
    return lax.dot_general(
        left, right, (((0,), (0,)), ((), ())), preferred_element_type=jnp.float32
    )


def dot_cols(left, right):
    return lax.dot_general(
        left, right, (((1,), (1,)), ((), ())), preferred_element_type=jnp.float32
    )


def dot(left, right):
    return jnp.dot(left, right, preferred_element_type=jnp.float32)


def attention_kernel(
    order_ref, place_ref, near_ref, far_ref, q_ref, g_ref,
    dq_ref, near_grad_ref, far_grad_ref,
    exp_store, prob_store, top_store, q_cols, g_cols, q_rows, g_rows, dq_cols,
):
    side = near_ref.shape[0]
    blocks = 2 * side
    rows = QH * BLOCK
    span = TILE_BLOCKS * BLOCK
    score_scale = LOG2E / math.sqrt(HD)
    place = place_ref[0]
    tiles = lax.div(place + TILE_BLOCKS, TILE_BLOCKS)

    for head in range(QH):
        part = pl.ds(head * HD, HD)
        q_cols[:, part] = q_ref[:, part].T
        g_cols[:, part] = g_ref[:, part].T
        q_rows[part, :] = q_ref[:, part]
        g_rows[part, :] = g_ref[:, part]
    dq_cols[...] = jnp.zeros_like(dq_cols)

    def gathered(tile):
        found = []
        for step in range(TILE_BLOCKS):
            slot = order_ref[tile * TILE_BLOCKS + step]
            near = near_ref[jnp.minimum(slot, side - 1)]
            far = far_ref[jnp.maximum(slot - side, 0)]
            found.append(jnp.where(slot < side, near, far))
        return jnp.concatenate(found, axis=0)

    def folded(values):
        return jnp.sum(values.reshape(span // 8, 8, rows), axis=0)

    def forward(tile, sums, masked):
        total, weighted, top = sums
        keys = gathered(tile)
        scores = dot(keys[:, :HD], q_cols[...]) * score_scale
        if masked:
            key_at = tile * span + lax.broadcasted_iota(jnp.int32, (span, rows), 0)
            row_at = place * BLOCK + lax.rem(
                lax.broadcasted_iota(jnp.int32, (span, rows), 1), BLOCK
            )
            visible = key_at <= row_at
            scores = jnp.where(visible, scores, -jnp.inf)
        highest = jnp.maximum(top, jnp.max(scores, axis=0, keepdims=True))
        shrink = jnp.exp2(top - highest)
        exponent = jnp.exp2(scores - highest)
        prob_grad = dot(keys[:, HD:], g_cols[...])
        exp_store[tile] = exponent
        prob_store[tile] = prob_grad
        top_store[tile] = highest
        total = total * shrink + folded(exponent)
        weighted = weighted * shrink + folded(exponent * prob_grad)
        return (total, weighted, highest)

    empty = jnp.zeros((8, rows), jnp.float32)
    start = forward(tiles - 1, (empty, empty, jnp.full((1, rows), -1e30, jnp.float32)), True)
    total, weighted, top = lax.fori_loop(
        0, tiles - 1, lambda tile, sums: forward(tile, sums, False), start
    )
    inverse = 1.0 / jnp.sum(total, axis=0, keepdims=True)
    row_delta = jnp.sum(weighted, axis=0, keepdims=True) * inverse

    def store(slot, value):
        @pl.when(slot < side)
        def _():
            near_grad_ref[slot] = value

        @pl.when(slot >= side)
        def _():
            far_grad_ref[slot - side] = value

    @pl.loop(0, tiles)
    def _(tile):
        keys = gathered(tile)[:, :HD]
        factor = jnp.exp2(top_store[tile] - top) * inverse
        probs = exp_store[tile] * factor
        score_grad = (probs * (prob_store[tile] - row_delta)).astype(jnp.bfloat16)
        value_grad = dot(probs.astype(jnp.bfloat16), g_rows[...])
        key_grad = dot(score_grad, q_rows[...])
        dq_cols[...] += dot(keys.T, score_grad)
        grads = jnp.concatenate([key_grad, value_grad], axis=1).astype(jnp.bfloat16)
        for step in range(TILE_BLOCKS):
            store(
                order_ref[tile * TILE_BLOCKS + step], grads[step * BLOCK : (step + 1) * BLOCK]
            )

    @pl.loop(tiles * TILE_BLOCKS, blocks)
    def _(place_at):
        store(order_ref[place_at], jnp.zeros((BLOCK, 2 * HD), jnp.bfloat16))

    for head in range(QH):
        part = pl.ds(head * HD, HD)
        dq_ref[:, part] = (dq_cols[:, part].T * (1.0 / math.sqrt(HD))).astype(jnp.bfloat16)


def attention_backward(order, place, near, far, queries, out_grad):
    tokens = queries.shape[0]
    rows = QH * tokens
    blocks = 2 * near.shape[0]
    tiles = blocks // TILE_BLOCKS
    span = TILE_BLOCKS * BLOCK
    smem = pl.BlockSpec(memory_space=pltpu.SMEM)
    vmem = pl.BlockSpec(memory_space=pltpu.VMEM)
    return pl.pallas_call(
        attention_kernel,
        out_shape=(
            jax.ShapeDtypeStruct(queries.shape, jnp.bfloat16),
            jax.ShapeDtypeStruct(near.shape, jnp.bfloat16),
            jax.ShapeDtypeStruct(far.shape, jnp.bfloat16),
        ),
        in_specs=[smem, smem, vmem, vmem, vmem, vmem],
        out_specs=(vmem, vmem, vmem),
        scratch_shapes=[
            pltpu.VMEM((tiles, span, rows), jnp.float32),
            pltpu.VMEM((tiles, span, rows), jnp.float32),
            pltpu.VMEM((tiles, 1, rows), jnp.float32),
            pltpu.VMEM((HD, rows), jnp.bfloat16),
            pltpu.VMEM((HD, rows), jnp.bfloat16),
            pltpu.VMEM((rows, HD), jnp.bfloat16),
            pltpu.VMEM((rows, HD), jnp.bfloat16),
            pltpu.VMEM((HD, rows), jnp.float32),
        ],
        compiler_params=pltpu.CompilerParams(vmem_limit_bytes=56 * 1024 * 1024),
        name="attention_backward",
    )(order, place, near, far, queries, out_grad)


def turn_kernel(column_ref, x_ref, *rest):
    outs, flipped = rest[:-1], rest[-1]
    columns = len(outs)
    width = x_ref.shape[1]
    piece = BLOCK // columns
    for block in range(width // BLOCK):
        part = pl.ds(block * BLOCK, BLOCK)
        flipped[part, :] = x_ref[:, part].T
    for turn, out_ref in enumerate(outs):
        column = lax.rem(column_ref[0] + turn, columns)
        for block in range(width // BLOCK):
            start = pl.multiple_of(block * BLOCK + column * piece, piece)
            out_ref[block * piece : (block + 1) * piece, :] = flipped[pl.ds(start, piece), :]


def column_pieces(column, x_rows, columns):
    tokens, width = x_rows.shape
    vmem = pl.BlockSpec(memory_space=pltpu.VMEM)
    shape = jax.ShapeDtypeStruct((width // columns, tokens), x_rows.dtype)
    return pl.pallas_call(
        turn_kernel,
        out_shape=(shape,) * columns,
        in_specs=[pl.BlockSpec(memory_space=pltpu.SMEM), vmem],
        out_specs=(vmem,) * columns,
        scratch_shapes=[pltpu.VMEM((width, tokens), x_rows.dtype)],
        compiler_params=pltpu.CompilerParams(vmem_limit_bytes=32 * 1024 * 1024),
        name="column_pieces",
    )(column, x_rows)


def share_kernel(column_ref, side_ref, grads_ref, *rest):
    pieces, (kept_ref, given_ref) = rest[:-2], rest[-2:]
    columns = len(pieces)
    groups, piece, _ = kept_ref.shape
    share = jnp.zeros((pieces[0].shape[0], grads_ref.shape[2]), jnp.float32)
    for turn, piece_ref in enumerate(pieces):
        column = lax.rem(column_ref[0] + columns - turn, columns)
        share += dot(piece_ref[...], grads_ref[column])
    parts = share.reshape(groups, 2, piece, share.shape[1])
    first = side_ref[0] == 0
    kept_ref[...] = jnp.where(first, parts[:, 0], parts[:, 1])
    given_ref[...] = jnp.where(first, parts[:, 1], parts[:, 0]).astype(jnp.bfloat16)


def weight_share(column, side, grads, pieces, groups):
    columns = len(pieces)
    piece = pieces[0].shape[0] // groups // 2
    smem = pl.BlockSpec(memory_space=pltpu.SMEM)
    vmem = pl.BlockSpec(memory_space=pltpu.VMEM)
    shape = (groups, piece, grads.shape[2])
    return pl.pallas_call(
        share_kernel,
        out_shape=(
            jax.ShapeDtypeStruct(shape, jnp.float32),
            jax.ShapeDtypeStruct(shape, jnp.bfloat16),
        ),
        in_specs=[smem, smem] + [vmem] * (columns + 1),
        out_specs=(vmem, vmem),
        compiler_params=pltpu.CompilerParams(vmem_limit_bytes=32 * 1024 * 1024),
        name="weight_share",
    )(column, side, grads, *pieces)


def spread(value, axis, groups=None):
    count = lax.axis_size(axis) if groups is None else len(groups[0])
    copies = lax.optimization_barrier(jnp.broadcast_to(value[None], (count, *value.shape)))
    return lax.all_to_all(copies, axis, 0, 0, axis_index_groups=groups)


def added(value, axis, groups=None):
    arrived = lax.all_to_all(value, axis, 0, 0, axis_index_groups=groups)
    return jnp.sum(arrived.astype(jnp.float32), axis=0)


def body(hidden_in, queries, out_grad, kv_weight, block_pos, precision):
    score_scale = 1.0 / math.sqrt(HD)
    tokens = hidden_in.shape[1]
    width = hidden_in.shape[2]
    seq_count = lax.axis_size("seq")
    dp_count = lax.axis_size("dp")
    half_count = seq_count // 2
    columns = half_count // 2
    grad_scale = 1.0 / math.sqrt(dp_count * seq_count * tokens)
    self_index = lax.axis_index("seq")
    core = lax.rem(self_index, 2)
    is_first = core == 0
    column_groups = [
        [start * half_count + 2 * column + side for column in range(columns)]
        for start in range(2)
        for side in range(2)
    ]
    plane_groups = [
        [
            group * seq_count + start * half_count + place_in
            for group in range(dp_count)
            for start in range(2)
        ]
        for place_in in range(half_count)
    ]
    half_groups = [
        [start * half_count + place_in for place_in in range(half_count)] for start in range(2)
    ]
    turns = [
        [
            (
                source,
                source // half_count * half_count
                + (source % half_count + 2 * turn) % half_count,
            )
            for source in range(seq_count)
        ]
        for turn in range(columns)
    ]
    same_core = [[2 * chip + side for chip in range(half_count)] for side in range(2)]
    swap = [(source, source ^ 1) for source in range(seq_count)]

    def swapped(value):
        return lax.ppermute(value, "seq", swap)

    x_rows = hidden_in[0]
    places = block_pos[0]
    place = lax.dynamic_slice_in_dim(places, self_index, 1)
    by_core = places.reshape(half_count, 2)
    slot_places = jnp.where(
        is_first,
        jnp.concatenate([by_core[:, 0], by_core[:, 1]]),
        jnp.concatenate([by_core[:, 1], by_core[:, 0]]),
    )
    slots = jnp.arange(seq_count, dtype=jnp.int32)
    order = jnp.sum(
        jnp.where(slot_places[None, :] == slots[:, None], slots[None, :], 0), axis=1
    ).astype(jnp.int32)
    my_pos = place * BLOCK + jnp.arange(tokens, dtype=jnp.int32)
    angles = my_pos.astype(jnp.float32)[:, None] * frequencies(HD)[None, :]
    cosine = jnp.cos(angles)
    sine_part = jnp.sin(angles)

    with jax.named_scope("column_pieces"):
        column = lax.rem(lax.div(self_index, 2), columns).reshape(1).astype(jnp.int32)
        pieces = [
            piece if turn == 0 else lax.ppermute(piece, "seq", turns[turn])
            for turn, piece in enumerate(column_pieces(column, x_rows, columns))
        ]
    with jax.named_scope("weight_gather"):
        half = jnp.where(is_first, kv_weight[:, :HD], kv_weight[:, HD:])
        near_weight = spread(half, "dp").reshape(width, HD)
        near_weight, order, cosine, sine_part, *pieces = lax.optimization_barrier(
            (near_weight, order, cosine, sine_part, *pieces)
        )
        far_weight = swapped(near_weight)
    with jax.named_scope("projection"):
        near_raw = dot(x_rows, near_weight)
        far_raw = dot(x_rows, far_weight)
        raw_keys = jnp.where(is_first, near_raw, far_raw)
        raw_values = jnp.where(is_first, far_raw, near_raw)
        key_quant = quantize(rotate(raw_keys, cosine, sine_part), precision[0, :, 0])
        value_quant = quantize(raw_values, precision[0, :, 1])
        stacked = jnp.concatenate([key_quant, value_quant], axis=1).astype(jnp.bfloat16)
    with jax.named_scope("kv_gather"):
        near = spread(stacked, "seq", same_core)
        far = swapped(near)
    with jax.named_scope("attention"):
        query_grad, near_grad, far_grad = attention_backward(
            order, place, near, far, queries[0], out_grad[0]
        )
    with jax.named_scope("kv_reduce"):
        pair = near_grad.astype(jnp.float32) + swapped(far_grad).astype(jnp.float32)
        carried = added(pair.astype(jnp.bfloat16), "seq", same_core)
    with jax.named_scope("projection_grad"):
        key_part = rotate_back(carried[:, :HD] * score_scale, cosine, sine_part)
        proj_grad = jnp.concatenate([key_part, carried[:, HD:]], axis=1).astype(jnp.bfloat16)
    with jax.named_scope("weight_grad"):
        side = core.reshape(1).astype(jnp.int32)
        column_grads = spread(proj_grad, "seq", column_groups)
        kept, given = weight_share(column, side, column_grads, pieces, dp_count)
        pair_share = kept + swapped(given).astype(jnp.float32)
        copies = jnp.broadcast_to(
            pair_share.astype(jnp.bfloat16)[:, None], (dp_count, 2, *pair_share.shape[1:])
        )
        whole_share = added(
            copies.reshape(2 * dp_count, *pair_share.shape[1:]), ("dp", "seq"), plane_groups
        )
        gathered = spread(whole_share * grad_scale, "seq", half_groups)
        piece = whole_share.shape[0]
        weight_grad = (
            gathered.reshape(columns, 2, piece, 2 * HD)
            .transpose(1, 0, 2, 3)
            .reshape(width // dp_count, 2 * HD)
        )
    with jax.named_scope("input_grad"):
        key_weight = jnp.where(is_first, near_weight, far_weight)
        value_weight = jnp.where(is_first, far_weight, near_weight)
        weight = jnp.concatenate([key_weight, value_weight], axis=1)
        input_grad = dot_cols(proj_grad, weight).astype(jnp.bfloat16)
    return (query_grad[None], proj_grad[None], input_grad[None], weight_grad)


def solution(mesh):
    in_specs = (
        P("dp", "seq", None),
        P("dp", "seq", None),
        P("dp", "seq", None),
        P("dp", None),
        P("dp", None),
        P("dp", "seq", None),
    )
    out_specs = (P("dp", "seq", None), P("dp", "seq", None), P("dp", "seq", None), P("dp", None))
    return jax.shard_map(body, mesh=mesh, in_specs=in_specs, out_specs=out_specs, check_vma=False)
```

```python
import functools
import math

import jax
import jax.numpy as jnp
from jax import lax
from jax.experimental import pallas as pl
from jax.experimental.pallas import tpu as pltpu
from jax.sharding import PartitionSpec as P

QH = 8
HD = 128
BLOCK = 128
TILE_BLOCKS = 4

EPSILON = 1e-06
LOG2E = math.log2(math.e)


def frequencies(size):
    expo = jnp.arange(0, size, 2).astype(jnp.float32) / size
    base = 1.0 / jnp.power(jnp.float32(500000.0), expo)
    wavelen = 2.0 * math.pi / base
    mixing = (8192.0 / wavelen - 1.0) / 3.0
    blended = (1.0 - mixing) * base / 8.0 + mixing * base
    return jnp.where(wavelen < 2048.0, base, jnp.where(wavelen > 8192.0, base / 8.0, blended))


def softstep(scaled):
    return scaled - jnp.sin(2.0 * math.pi * (scaled - jnp.round(scaled))) / (2.0 * math.pi)


def dot_cols(left, right):
    return lax.dot_general(
        left, right, (((1,), (1,)), ((), ())), preferred_element_type=jnp.float32
    )


def dot(left, right):
    return jnp.dot(left, right, preferred_element_type=jnp.float32)


def attention_kernel(
    order_ref, place_ref, core_ref, near_ref, far_ref, q_ref, g_ref,
    dq_ref, near_grad_ref, far_grad_ref,
    exp_store, prob_store, top_store, q_cols, g_cols, q_rows, g_rows, dq_cols,
):
    blocks = near_ref.shape[0]
    rows = QH * BLOCK
    span = TILE_BLOCKS * BLOCK
    score_scale = LOG2E / math.sqrt(HD)
    place = place_ref[0]
    is_first = core_ref[0] == 0
    tiles = lax.div(place + TILE_BLOCKS, TILE_BLOCKS)

    for head in range(QH):
        part = pl.ds(head * HD, HD)
        q_cols[:, part] = q_ref[:, part].T
        g_cols[:, part] = g_ref[:, part].T
        q_rows[part, :] = q_ref[:, part]
        g_rows[part, :] = g_ref[:, part]
    dq_cols[...] = jnp.zeros_like(dq_cols)

    def gathered(tile):
        slots = [order_ref[tile * TILE_BLOCKS + step] for step in range(TILE_BLOCKS)]
        near = jnp.concatenate([near_ref[slot] for slot in slots], axis=0)
        far = jnp.concatenate([far_ref[slot] for slot in slots], axis=0)
        return jnp.where(is_first, near, far), jnp.where(is_first, far, near)

    def folded(values):
        return jnp.sum(values.reshape(span // 8, 8, rows), axis=0)

    def forward(tile, sums, masked):
        total, weighted, top = sums
        keys, values = gathered(tile)
        scores = dot(keys, q_cols[...]) * score_scale
        if masked:
            key_at = tile * span + lax.broadcasted_iota(jnp.int32, (span, rows), 0)
            row_at = place * BLOCK + lax.rem(
                lax.broadcasted_iota(jnp.int32, (span, rows), 1), BLOCK
            )
            visible = key_at <= row_at
            scores = jnp.where(visible, scores, -jnp.inf)
        highest = jnp.maximum(top, jnp.max(scores, axis=0, keepdims=True))
        shrink = jnp.exp2(top - highest)
        exponent = jnp.exp2(scores - highest)
        prob_grad = dot(values, g_cols[...])
        exp_store[tile] = exponent
        prob_store[tile] = prob_grad
        top_store[tile] = highest
        total = total * shrink + folded(exponent)
        weighted = weighted * shrink + folded(exponent * prob_grad)
        return (total, weighted, highest)

    empty = jnp.zeros((8, rows), jnp.float32)
    start = forward(tiles - 1, (empty, empty, jnp.full((1, rows), -1e30, jnp.float32)), True)
    total, weighted, top = lax.fori_loop(
        0, tiles - 1, lambda tile, sums: forward(tile, sums, False), start
    )
    inverse = 1.0 / jnp.sum(total, axis=0, keepdims=True)
    row_delta = jnp.sum(weighted, axis=0, keepdims=True) * inverse

    @pl.loop(0, tiles)
    def _(tile):
        keys, _ = gathered(tile)
        factor = jnp.exp2(top_store[tile] - top) * inverse
        probs = exp_store[tile] * factor
        score_grad = (probs * (prob_store[tile] - row_delta)).astype(jnp.bfloat16)
        value_grad = dot(probs.astype(jnp.bfloat16), g_rows[...]).astype(jnp.bfloat16)
        key_grad = dot(score_grad, q_rows[...]).astype(jnp.bfloat16)
        dq_cols[...] += dot(keys.T, score_grad)
        near_grad = jnp.where(is_first, key_grad, value_grad)
        far_grad = jnp.where(is_first, value_grad, key_grad)
        for step in range(TILE_BLOCKS):
            slot = order_ref[tile * TILE_BLOCKS + step]
            near_grad_ref[slot] = near_grad[step * BLOCK : (step + 1) * BLOCK]
            far_grad_ref[slot] = far_grad[step * BLOCK : (step + 1) * BLOCK]

    @pl.loop(tiles * TILE_BLOCKS, blocks)
    def _(place_at):
        slot = order_ref[place_at]
        near_grad_ref[slot] = jnp.zeros((BLOCK, HD), jnp.bfloat16)
        far_grad_ref[slot] = jnp.zeros((BLOCK, HD), jnp.bfloat16)

    for head in range(QH):
        part = pl.ds(head * HD, HD)
        dq_ref[:, part] = (dq_cols[:, part].T * (1.0 / math.sqrt(HD))).astype(jnp.bfloat16)


def attention_backward(order, place, core, near, far, queries, out_grad):
    tokens = queries.shape[0]
    rows = QH * tokens
    tiles = near.shape[0] // TILE_BLOCKS
    span = TILE_BLOCKS * BLOCK
    smem = pl.BlockSpec(memory_space=pltpu.SMEM)
    vmem = pl.BlockSpec(memory_space=pltpu.VMEM)
    return pl.pallas_call(
        attention_kernel,
        out_shape=(
            jax.ShapeDtypeStruct(queries.shape, jnp.bfloat16),
            jax.ShapeDtypeStruct(near.shape, jnp.bfloat16),
            jax.ShapeDtypeStruct(far.shape, jnp.bfloat16),
        ),
        in_specs=[smem, smem, smem, vmem, vmem, vmem, vmem],
        out_specs=(vmem, vmem, vmem),
        scratch_shapes=[
            pltpu.VMEM((tiles, span, rows), jnp.float32),
            pltpu.VMEM((tiles, span, rows), jnp.float32),
            pltpu.VMEM((tiles, 1, rows), jnp.float32),
            pltpu.VMEM((HD, rows), jnp.bfloat16),
            pltpu.VMEM((HD, rows), jnp.bfloat16),
            pltpu.VMEM((rows, HD), jnp.bfloat16),
            pltpu.VMEM((rows, HD), jnp.bfloat16),
            pltpu.VMEM((HD, rows), jnp.float32),
        ],
        compiler_params=pltpu.CompilerParams(vmem_limit_bytes=56 * 1024 * 1024),
        name="attention_backward",
    )(order, place, core, near, far, queries, out_grad)


def local_call(kernel, shapes, scalars, arrays, name, scratch=()):
    smem = pl.BlockSpec(memory_space=pltpu.SMEM)
    vmem = pl.BlockSpec(memory_space=pltpu.VMEM)
    return pl.pallas_call(
        kernel,
        out_shape=shapes,
        in_specs=[smem] * len(scalars) + [vmem] * len(arrays),
        out_specs=jax.tree.map(lambda _: vmem, shapes),
        scratch_shapes=scratch,
        compiler_params=pltpu.CompilerParams(vmem_limit_bytes=32 * 1024 * 1024),
        name=name,
    )(*scalars, *arrays)


def project_kernel(core_ref, levels_ref, own_ref, far_ref, weight_ref, cos_ref, sin_ref, out_ref):
    core = core_ref[0]
    weight = weight_ref[...]
    for distance, x_ref in enumerate((own_ref, far_ref)):
        at = core if distance == 0 else 1 - core
        raw = dot(x_ref[...], weight)
        turned = raw * cos_ref[at] + pltpu.roll(raw, HD // 2, 1) * sin_ref[at]
        largest = jnp.max(jnp.abs(turned), axis=0, keepdims=True)
        level_step = (largest + EPSILON) / levels_ref[distance]
        quantized = (level_step * softstep(turned / level_step)).astype(jnp.bfloat16)
        for copy in range(out_ref.shape[0]):
            out_ref[copy, at] = quantized


def settle_kernel(arrived_ref, cos_ref, sin_ref, out_ref):
    for at in range(2):
        grads = arrived_ref[0, at].astype(jnp.float32)
        for source in range(1, arrived_ref.shape[0]):
            grads += arrived_ref[source, at].astype(jnp.float32)
        turned = grads * cos_ref[at] - pltpu.roll(grads, HD // 2, 1) * sin_ref[at]
        turned = turned.astype(jnp.bfloat16)
        for copy in range(out_ref.shape[0]):
            out_ref[copy, at] = turned


def turn_kernel(x_ref, out_ref, flipped):
    columns, extent, _ = out_ref.shape
    piece = BLOCK // columns
    for block in range(extent // piece):
        part = pl.ds(block * BLOCK, BLOCK)
        flipped[...] = x_ref[:, part].T
        for column in range(columns):
            out_ref[column, block * piece : (block + 1) * piece, :] = flipped[
                column * piece : (column + 1) * piece, :
            ]


def share_kernel(core_ref, near_ref, far_ref, grads_ref, out_ref):
    core = core_ref[0]
    share = jnp.zeros(near_ref.shape[1:], jnp.float32)
    for column in range(near_ref.shape[0]):
        share += dot(near_ref[column], grads_ref[column, core])
        share += dot(far_ref[column], grads_ref[column, 1 - core])
    out_ref[...] = share.astype(out_ref.dtype).reshape(out_ref.shape)


def total_kernel(parts_ref, out_ref):
    total = parts_ref[0].astype(jnp.float32)
    for source in range(1, parts_ref.shape[0]):
        total += parts_ref[source].astype(jnp.float32)
    total = total.astype(out_ref.dtype)
    for copy in range(out_ref.shape[0]):
        out_ref[copy] = total


def assemble_kernel(grad_scale, parts_ref, out_ref):
    columns = parts_ref.shape[1]
    piece = parts_ref.shape[3] // 2
    for column in range(columns):
        for core in range(2):
            low = parts_ref[0, column, core].astype(jnp.float32)
            high = parts_ref[1, column, core].astype(jnp.float32)
            total = (low + high) * grad_scale
            for half in range(2):
                row = half * columns * piece + column * piece
                out_ref[row : row + piece, core * HD : (core + 1) * HD] = total[
                    half * piece : (half + 1) * piece
                ]


def body(hidden_in, queries, out_grad, kv_weight, block_pos, precision):
    score_scale = 1.0 / math.sqrt(HD)
    tokens = hidden_in.shape[1]
    width = hidden_in.shape[2]
    seq_count = lax.axis_size("seq")
    dp_count = lax.axis_size("dp")
    half_count = seq_count // 2
    columns = half_count // 2
    grad_scale = 1.0 / math.sqrt(dp_count * seq_count * tokens)
    self_index = lax.axis_index("seq")
    core_index = lax.rem(self_index, 2)
    core = core_index.reshape(1).astype(jnp.int32)
    is_first = core_index == 0
    column_groups = [
        [start * half_count + 2 * column + side for column in range(columns)]
        for start in range(2)
        for side in range(2)
    ]
    same_core = [[2 * chip + side for chip in range(half_count)] for side in range(2)]
    swap = [(source, source ^ 1) for source in range(seq_count)]

    def swapped(value):
        return lax.ppermute(value, "seq", swap)

    def exchanged(value, axis, groups=None):
        return lax.all_to_all(value, axis, 0, 0, axis_index_groups=groups)

    x_rows = hidden_in[0]
    places = block_pos[0]
    place = lax.dynamic_slice_in_dim(places, self_index, 1)
    slots = jnp.arange(seq_count, dtype=jnp.int32)
    order = jnp.sum(
        jnp.where(places[None, :] == slots[:, None], slots[None, :], 0), axis=1
    ).astype(jnp.int32)

    with jax.named_scope("rotation"):
        pair_places = lax.dynamic_slice_in_dim(places, self_index - core_index, 2)
        pair_pos = pair_places[:, None] * BLOCK + jnp.arange(tokens, dtype=jnp.int32)[None, :]
        freq = frequencies(HD)
        angles = pair_pos.astype(jnp.float32)[:, :, None] * jnp.concatenate([freq, freq])
        lane = jnp.arange(HD, dtype=jnp.int32)
        cosine = jnp.where(is_first, jnp.cos(angles), 1.0)
        sine_part = jnp.where(
            is_first, jnp.sin(angles) * jnp.where(lane < HD // 2, -1.0, 1.0), 0.0
        )
        back_scale = jnp.where(is_first, score_scale, 1.0)
        back_cosine = cosine * back_scale
        back_sine = sine_part * back_scale
        pair_bits = jnp.concatenate([precision[0], swapped(precision[0])])
        bits_here = jnp.where(is_first, pair_bits[:, 0], pair_bits[:, 1])
        levels = (lax.shift_left(jnp.ones_like(bits_here), bits_here - 1) - 1).astype(jnp.float32)
        x_far = swapped(x_rows)
        x_columns = local_call(
            turn_kernel,
            jax.ShapeDtypeStruct((columns, width // columns, tokens), x_rows.dtype),
            (),
            (x_rows,),
            "x_columns",
            (pltpu.VMEM((BLOCK, tokens), x_rows.dtype),),
        )
    with jax.named_scope("weight_gather"):
        half = jnp.where(is_first, kv_weight[:, :HD], kv_weight[:, HD:])
        copies = jnp.broadcast_to(half[None], (dp_count, *half.shape))
        near_weight = exchanged(lax.optimization_barrier(copies), "dp").reshape(width, HD)
        (
            near_weight, order, cosine, sine_part, back_cosine, back_sine, levels, x_far, x_columns
        ) = lax.optimization_barrier(
            (
                near_weight, order, cosine, sine_part, back_cosine, back_sine, levels, x_far,
                x_columns,
            )
        )
    with jax.named_scope("projection"):
        stacked = local_call(
            project_kernel,
            jax.ShapeDtypeStruct((half_count, 2, tokens, HD), jnp.bfloat16),
            (core, levels),
            (x_rows, x_far, near_weight, cosine, sine_part),
            "projection",
        )
    with jax.named_scope("kv_gather"):
        near = exchanged(stacked, "seq", same_core).reshape(seq_count, tokens, HD)
        near, x_columns = lax.optimization_barrier((near, x_columns))
        near_columns = exchanged(x_columns, "seq", column_groups)
        far = swapped(near)
    with jax.named_scope("attention"):
        query_grad, near_grad, far_grad = attention_backward(
            order, place, core, near, far, queries[0], out_grad[0]
        )
    with jax.named_scope("kv_reduce"):
        pair = near_grad.astype(jnp.float32) + swapped(far_grad).astype(jnp.float32)
        pair = pair.astype(jnp.bfloat16).reshape(half_count, 2, tokens, HD)
        pair, near_columns, near_weight = lax.optimization_barrier(
            (pair, near_columns, near_weight)
        )
        arrived = exchanged(pair, "seq", same_core)
        far_columns = swapped(near_columns)
        far_weight = swapped(near_weight)
    with jax.named_scope("projection_grad"):
        settled = local_call(
            settle_kernel,
            jax.ShapeDtypeStruct((columns, 2, tokens, HD), jnp.bfloat16),
            (),
            (arrived, back_cosine, back_sine),
            "projection_grad",
        )
    with jax.named_scope("weight_grad"):
        column_grads = exchanged(settled, "seq", column_groups)
        share = local_call(
            share_kernel,
            jax.ShapeDtypeStruct((dp_count, width // columns // dp_count, HD), jnp.bfloat16),
            (core,),
            (near_columns, far_columns, column_grads),
            "weight_share",
        )
        share_parts = exchanged(share, "dp")
        group_share = local_call(
            total_kernel,
            jax.ShapeDtypeStruct((seq_count, *share.shape[1:]), jnp.bfloat16),
            (),
            (share_parts,),
            "group_share",
        )
        gathered = exchanged(group_share, "seq")
        weight_grad = local_call(
            functools.partial(assemble_kernel, grad_scale),
            jax.ShapeDtypeStruct((width // dp_count, 2 * HD), jnp.float32),
            (),
            (gathered.reshape(2, columns, 2, *share.shape[1:]),),
            "weight_grad",
        )
    with jax.named_scope("input_grad"):
        both = settled[0]
        own = jnp.where(is_first, both[0], both[1])
        other = swapped(jnp.where(is_first, both[1], both[0]))
        proj_grad = jnp.concatenate(
            [jnp.where(is_first, own, other), jnp.where(is_first, other, own)], axis=1
        )
        input_grad = (dot_cols(own, near_weight) + dot_cols(other, far_weight)).astype(
            jnp.bfloat16
        )
    return (query_grad[None], proj_grad[None], input_grad[None], weight_grad)


def solution(mesh):
    in_specs = (
        P("dp", "seq", None),
        P("dp", "seq", None),
        P("dp", "seq", None),
        P("dp", None),
        P("dp", None),
        P("dp", "seq", None),
    )
    out_specs = (P("dp", "seq", None), P("dp", "seq", None), P("dp", "seq", None), P("dp", None))
    return jax.shard_map(body, mesh=mesh, in_specs=in_specs, out_specs=out_specs, check_vma=False)
```

```python
import functools
import math

import jax
import jax.numpy as jnp
from jax import lax
from jax.experimental import pallas as pl
from jax.experimental.pallas import tpu as pltpu
from jax.sharding import PartitionSpec as P

QH = 8
HD = 128
BLOCK = 128
TILE_BLOCKS = 4

EPSILON = 1e-06
LOG2E = math.log2(math.e)


def frequencies(size):
    expo = jnp.arange(0, size, 2).astype(jnp.float32) / size
    base = 1.0 / jnp.power(jnp.float32(500000.0), expo)
    wavelen = 2.0 * math.pi / base
    mixing = (8192.0 / wavelen - 1.0) / 3.0
    blended = (1.0 - mixing) * base / 8.0 + mixing * base
    return jnp.where(wavelen < 2048.0, base, jnp.where(wavelen > 8192.0, base / 8.0, blended))


def softstep(scaled):
    return scaled - jnp.sin(2.0 * math.pi * (scaled - jnp.round(scaled))) / (2.0 * math.pi)


def dot_cols(left, right):
    return lax.dot_general(
        left, right, (((1,), (1,)), ((), ())), preferred_element_type=jnp.float32
    )


def dot(left, right):
    return jnp.dot(left, right, preferred_element_type=jnp.float32)


def attention_kernel(
    order_ref, place_ref, core_ref, near_ref, far_ref, q_cols, g_cols, q_rows, g_rows,
    dq_ref, near_grad_ref, far_grad_ref,
    exp_store, prob_store, top_store, dq_cols,
):
    blocks = near_ref.shape[0]
    rows = QH * BLOCK
    span = TILE_BLOCKS * BLOCK
    score_scale = LOG2E / math.sqrt(HD)
    place = place_ref[0]
    is_first = core_ref[0] == 0
    tiles = lax.div(place + TILE_BLOCKS, TILE_BLOCKS)

    dq_cols[...] = jnp.zeros_like(dq_cols)

    def gathered(tile):
        slots = [order_ref[tile * TILE_BLOCKS + step] for step in range(TILE_BLOCKS)]
        near = jnp.concatenate([near_ref[slot] for slot in slots], axis=0)
        far = jnp.concatenate([far_ref[slot] for slot in slots], axis=0)
        return jnp.where(is_first, near, far), jnp.where(is_first, far, near)

    def folded(values):
        return jnp.sum(values.reshape(span // 8, 8, rows), axis=0)

    def forward(tile, sums, masked):
        total, weighted, top = sums
        keys, values = gathered(tile)
        scores = dot(keys, q_cols[...]) * score_scale
        if masked:
            key_at = tile * span + lax.broadcasted_iota(jnp.int32, (span, rows), 0)
            row_at = place * BLOCK + lax.rem(
                lax.broadcasted_iota(jnp.int32, (span, rows), 1), BLOCK
            )
            visible = key_at <= row_at
            scores = jnp.where(visible, scores, -jnp.inf)
        highest = jnp.maximum(top, jnp.max(scores, axis=0, keepdims=True))
        shrink = jnp.exp2(top - highest)
        exponent = jnp.exp2(scores - highest)
        prob_grad = dot(values, g_cols[...])
        exp_store[tile] = exponent
        prob_store[tile] = prob_grad
        top_store[tile] = highest
        total = total * shrink + folded(exponent)
        weighted = weighted * shrink + folded(exponent * prob_grad)
        return (total, weighted, highest)

    empty = jnp.zeros((8, rows), jnp.float32)
    start = forward(tiles - 1, (empty, empty, jnp.full((1, rows), -1e30, jnp.float32)), True)
    total, weighted, top = lax.fori_loop(
        0, tiles - 1, lambda tile, sums: forward(tile, sums, False), start
    )
    inverse = 1.0 / jnp.sum(total, axis=0, keepdims=True)
    row_delta = jnp.sum(weighted, axis=0, keepdims=True) * inverse

    @pl.loop(0, tiles)
    def _(tile):
        keys, _ = gathered(tile)
        factor = jnp.exp2(top_store[tile] - top) * inverse
        probs = exp_store[tile] * factor
        score_grad = (probs * (prob_store[tile] - row_delta)).astype(jnp.bfloat16)
        value_grad = dot(probs.astype(jnp.bfloat16), g_rows[...]).astype(jnp.bfloat16)
        key_grad = dot(score_grad, q_rows[...]).astype(jnp.bfloat16)
        dq_cols[...] += dot(keys.T, score_grad)
        near_grad = jnp.where(is_first, key_grad, value_grad)
        far_grad = jnp.where(is_first, value_grad, key_grad)
        for step in range(TILE_BLOCKS):
            slot = order_ref[tile * TILE_BLOCKS + step]
            near_grad_ref[slot] = near_grad[step * BLOCK : (step + 1) * BLOCK]
            far_grad_ref[slot] = far_grad[step * BLOCK : (step + 1) * BLOCK]

    @pl.loop(tiles * TILE_BLOCKS, blocks)
    def _(place_at):
        slot = order_ref[place_at]
        near_grad_ref[slot] = jnp.zeros((BLOCK, HD), jnp.bfloat16)
        far_grad_ref[slot] = jnp.zeros((BLOCK, HD), jnp.bfloat16)

    for head in range(QH):
        part = pl.ds(head * HD, HD)
        dq_ref[:, part] = (dq_cols[:, part].T * (1.0 / math.sqrt(HD))).astype(jnp.bfloat16)


def attention_backward(order, place, core, near, far, columns_and_rows):
    rows = columns_and_rows[0].shape[1]
    tiles = near.shape[0] // TILE_BLOCKS
    span = TILE_BLOCKS * BLOCK
    smem = pl.BlockSpec(memory_space=pltpu.SMEM)
    vmem = pl.BlockSpec(memory_space=pltpu.VMEM)
    return pl.pallas_call(
        attention_kernel,
        out_shape=(
            jax.ShapeDtypeStruct((rows // QH, QH * HD), jnp.bfloat16),
            jax.ShapeDtypeStruct(near.shape, jnp.bfloat16),
            jax.ShapeDtypeStruct(far.shape, jnp.bfloat16),
        ),
        in_specs=[smem] * 3 + [vmem] * 6,
        out_specs=(vmem, vmem, vmem),
        scratch_shapes=[
            pltpu.VMEM((tiles, span, rows), jnp.float32),
            pltpu.VMEM((tiles, span, rows), jnp.float32),
            pltpu.VMEM((tiles, 1, rows), jnp.float32),
            pltpu.VMEM((HD, rows), jnp.float32),
        ],
        compiler_params=pltpu.CompilerParams(vmem_limit_bytes=56 * 1024 * 1024),
        name="attention_backward",
    )(order, place, core, near, far, *columns_and_rows)


def local_call(kernel, shapes, scalars, arrays, name, scratch=()):
    smem = pl.BlockSpec(memory_space=pltpu.SMEM)
    vmem = pl.BlockSpec(memory_space=pltpu.VMEM)
    return pl.pallas_call(
        kernel,
        out_shape=shapes,
        in_specs=[smem] * len(scalars) + [vmem] * len(arrays),
        out_specs=jax.tree.map(lambda _: vmem, shapes),
        scratch_shapes=scratch,
        compiler_params=pltpu.CompilerParams(vmem_limit_bytes=32 * 1024 * 1024),
        name=name,
    )(*scalars, *arrays)


def copies_kernel(core_ref, weight_ref, out_ref):
    start = pl.multiple_of(core_ref[0] * HD, HD)
    half = weight_ref[:, pl.ds(start, HD)]
    for copy in range(out_ref.shape[0]):
        out_ref[copy] = half


def query_kernel(q_ref, g_ref, q_cols, g_cols, q_rows, g_rows):
    for head in range(QH):
        part = pl.ds(head * HD, HD)
        q_cols[:, part] = q_ref[:, part].T
        g_cols[:, part] = g_ref[:, part].T
        q_rows[part, :] = q_ref[:, part]
        g_rows[part, :] = g_ref[:, part]


def project_kernel(core_ref, levels_ref, own_ref, far_ref, weight_ref, cos_ref, sin_ref, out_ref):
    core = core_ref[0]
    weight = weight_ref[...]
    for distance, x_ref in enumerate((own_ref, far_ref)):
        at = core if distance == 0 else 1 - core
        raw = dot(x_ref[...], weight)
        turned = raw * cos_ref[at] + pltpu.roll(raw, HD // 2, 1) * sin_ref[at]
        largest = jnp.max(jnp.abs(turned), axis=0, keepdims=True)
        level_step = (largest + EPSILON) / levels_ref[distance]
        quantized = (level_step * softstep(turned / level_step)).astype(jnp.bfloat16)
        for copy in range(out_ref.shape[0]):
            out_ref[copy, at] = quantized


def settle_kernel(arrived_ref, cos_ref, sin_ref, out_ref):
    for at in range(2):
        grads = arrived_ref[0, at].astype(jnp.float32)
        for source in range(1, arrived_ref.shape[0]):
            grads += arrived_ref[source, at].astype(jnp.float32)
        turned = grads * cos_ref[at] - pltpu.roll(grads, HD // 2, 1) * sin_ref[at]
        turned = turned.astype(jnp.bfloat16)
        for copy in range(out_ref.shape[0]):
            out_ref[copy, at] = turned


def turn_kernel(parity_ref, x_ref, keep_ref, *rest):
    parity = parity_ref[0]
    for group in range(keep_ref.shape[0] // BLOCK):
        rows = slice(group * BLOCK, (group + 1) * BLOCK)
        for out_ref, half in zip((keep_ref, *rest), (parity, 1 - parity)):
            start = pl.multiple_of((2 * group + half) * BLOCK, BLOCK)
            out_ref[rows, :] = x_ref[:, pl.ds(start, BLOCK)].T


def turned_halves(parity, x_rows, count, name):
    tokens, width = x_rows.shape
    shape = jax.ShapeDtypeStruct((width // 2, tokens), x_rows.dtype)
    return local_call(turn_kernel, (shape,) * count, (parity,), (x_rows,), name)


def share_kernel(core_ref, *rest):
    core = core_ref[0]
    own_ref, own_far_ref, next_ref, next_far_ref, grads_ref, next_grads_ref, out_ref = rest
    quads, groups, piece, _ = out_ref.shape
    own = jnp.concatenate([grads_ref[core], grads_ref[1 - core]], axis=0)
    beside = jnp.concatenate([next_grads_ref[core], next_grads_ref[1 - core]], axis=0)
    for group in range(groups):
        rows = slice(group * BLOCK, (group + 1) * BLOCK)
        share = dot(jnp.concatenate([own_ref[rows, :], own_far_ref[rows, :]], axis=1), own)
        share += dot(jnp.concatenate([next_ref[rows, :], next_far_ref[rows, :]], axis=1), beside)
        share = share.astype(out_ref.dtype)
        for quad in range(quads):
            out_ref[quad, group] = share[quad * piece : (quad + 1) * piece]


def total_kernel(parts_ref, out_ref):
    total = parts_ref[0].astype(jnp.float32)
    for source in range(1, parts_ref.shape[0]):
        total += parts_ref[source].astype(jnp.float32)
    total = total.astype(out_ref.dtype)
    for copy in range(out_ref.shape[0]):
        out_ref[copy] = total


def assemble_kernel(grad_scale, parts_ref, out_ref):
    _, quads, _, _, piece, _ = parts_ref.shape
    for quad in range(quads):
        for parity in range(2):
            for core in range(2):
                low = parts_ref[0, quad, parity, core].astype(jnp.float32)
                high = parts_ref[1, quad, parity, core].astype(jnp.float32)
                row = parity * BLOCK + quad * piece
                out_ref[row : row + piece, core * HD : (core + 1) * HD] = (
                    low + high
                ) * grad_scale


def body(hidden_in, queries, out_grad, kv_weight, block_pos, precision):
    score_scale = 1.0 / math.sqrt(HD)
    tokens = hidden_in.shape[1]
    width = hidden_in.shape[2]
    seq_count = lax.axis_size("seq")
    dp_count = lax.axis_size("dp")
    half_count = seq_count // 2
    columns = half_count // 2
    grad_scale = 1.0 / math.sqrt(dp_count * seq_count * tokens)
    self_index = lax.axis_index("seq")
    core_index = lax.rem(self_index, 2)
    core = core_index.reshape(1).astype(jnp.int32)
    is_first = core_index == 0
    quads = columns // 2
    parity = lax.rem(lax.div(self_index, 2), 2).reshape(1).astype(jnp.int32)
    quad_groups = [
        [start * half_count + 4 * quad + side for quad in range(quads)]
        for start in range(2)
        for side in range(4)
    ]
    same_core = [[2 * chip + side for chip in range(half_count)] for side in range(2)]
    swap = [(source, source ^ 1) for source in range(seq_count)]
    beside = [(source, source ^ 2) for source in range(seq_count)]

    def swapped(value):
        return lax.ppermute(value, "seq", swap)

    def passed(value):
        return lax.ppermute(value, "seq", beside)

    def exchanged(value, axis, groups=None):
        return lax.all_to_all(value, axis, 0, 0, axis_index_groups=groups)

    x_rows = hidden_in[0]
    places = block_pos[0]
    place = lax.dynamic_slice_in_dim(places, self_index, 1)
    slots = jnp.arange(seq_count, dtype=jnp.int32)
    order = jnp.sum(
        jnp.where(places[None, :] == slots[:, None], slots[None, :], 0), axis=1
    ).astype(jnp.int32)

    with jax.named_scope("rotation"):
        pair_places = lax.dynamic_slice_in_dim(places, self_index - core_index, 2)
        pair_pos = pair_places[:, None] * BLOCK + jnp.arange(tokens, dtype=jnp.int32)[None, :]
        freq = frequencies(HD)
        angles = pair_pos.astype(jnp.float32)[:, :, None] * jnp.concatenate([freq, freq])
        lane = jnp.arange(HD, dtype=jnp.int32)
        cosine = jnp.where(is_first, jnp.cos(angles), 1.0)
        sine_part = jnp.where(
            is_first, jnp.sin(angles) * jnp.where(lane < HD // 2, -1.0, 1.0), 0.0
        )
        back_scale = jnp.where(is_first, score_scale, 1.0)
        back_cosine = cosine * back_scale
        back_sine = sine_part * back_scale
        pair_bits = jnp.concatenate([precision[0], swapped(precision[0])])
        bits_here = jnp.where(is_first, pair_bits[:, 0], pair_bits[:, 1])
        levels = (lax.shift_left(jnp.ones_like(bits_here), bits_here - 1) - 1).astype(jnp.float32)
        x_far = swapped(x_rows)
        own_half, given_half = turned_halves(parity, x_rows, 2, "own_halves")
        next_half = passed(given_half)
        (far_half,) = turned_halves(parity, x_far, 1, "far_half")
    with jax.named_scope("weight_gather"):
        copies = local_call(
            copies_kernel,
            jax.ShapeDtypeStruct((dp_count, kv_weight.shape[0], HD), kv_weight.dtype),
            (core,),
            (kv_weight,),
            "weight_copies",
        )
        near_weight = exchanged(copies, "dp").reshape(width, HD)
        (
            near_weight, order, cosine, sine_part, back_cosine, back_sine, levels, x_far,
            own_half, next_half, far_half,
        ) = lax.optimization_barrier(
            (
                near_weight, order, cosine, sine_part, back_cosine, back_sine, levels, x_far,
                own_half, next_half, far_half,
            )
        )
    with jax.named_scope("projection"):
        stacked = local_call(
            project_kernel,
            jax.ShapeDtypeStruct((half_count, 2, tokens, HD), jnp.bfloat16),
            (core, levels),
            (x_rows, x_far, near_weight, cosine, sine_part),
            "projection",
        )
    with jax.named_scope("kv_gather"):
        near = exchanged(stacked, "seq", same_core).reshape(seq_count, tokens, HD)
        columns_shape = jax.ShapeDtypeStruct((HD, QH * tokens), jnp.bfloat16)
        rows_shape = jax.ShapeDtypeStruct((QH * tokens, HD), jnp.bfloat16)
        columns_and_rows = local_call(
            query_kernel,
            (columns_shape, columns_shape, rows_shape, rows_shape),
            (),
            (queries[0], out_grad[0]),
            "query_columns",
        )
        near, *columns_and_rows = lax.optimization_barrier((near, *columns_and_rows))
        far = swapped(near)
    with jax.named_scope("attention"):
        query_grad, near_grad, far_grad = attention_backward(
            order, place, core, near, far, columns_and_rows
        )
    with jax.named_scope("kv_reduce"):
        pair = near_grad.astype(jnp.float32) + swapped(far_grad).astype(jnp.float32)
        pair = pair.astype(jnp.bfloat16).reshape(half_count, 2, tokens, HD)
        pair, next_half, near_weight = lax.optimization_barrier((pair, next_half, near_weight))
        arrived = exchanged(pair, "seq", same_core)
        next_far_half = swapped(next_half)
        far_weight = swapped(near_weight)
        arrived, next_far_half, far_weight = lax.optimization_barrier(
            (arrived, next_far_half, far_weight)
        )
    with jax.named_scope("projection_grad"):
        settled = local_call(
            settle_kernel,
            jax.ShapeDtypeStruct((1, 2, tokens, HD), jnp.bfloat16),
            (),
            (arrived, back_cosine, back_sine),
            "projection_grad",
        )
    with jax.named_scope("weight_grad"):
        piece = BLOCK // quads
        share = local_call(
            share_kernel,
            jax.ShapeDtypeStruct((quads, dp_count, piece, HD), jnp.bfloat16),
            (core,),
            (own_half, far_half, next_half, next_far_half, settled[0], passed(settled[0])),
            "weight_share",
        )
        quad_parts = exchanged(share, "seq", quad_groups)
        (quad_share,) = local_call(
            total_kernel,
            (jax.ShapeDtypeStruct((1, dp_count, piece, HD), jnp.bfloat16),),
            (),
            (quad_parts,),
            "quad_share",
        )
        share_parts = exchanged(quad_share[0], "dp")
        group_share = local_call(
            total_kernel,
            jax.ShapeDtypeStruct((seq_count, piece, HD), jnp.bfloat16),
            (),
            (share_parts,),
            "group_share",
        )
        gathered = exchanged(group_share, "seq")
        weight_grad = local_call(
            functools.partial(assemble_kernel, grad_scale),
            jax.ShapeDtypeStruct((width // dp_count, 2 * HD), jnp.float32),
            (),
            (gathered.reshape(2, quads, 2, 2, piece, HD),),
            "weight_grad",
        )
    with jax.named_scope("input_grad"):
        both = settled[0]
        own = jnp.where(is_first, both[0], both[1])
        other = swapped(jnp.where(is_first, both[1], both[0]))
        proj_grad = jnp.concatenate(
            [jnp.where(is_first, own, other), jnp.where(is_first, other, own)], axis=1
        )
        input_grad = (dot_cols(own, near_weight) + dot_cols(other, far_weight)).astype(
            jnp.bfloat16
        )
    return (query_grad[None], proj_grad[None], input_grad[None], weight_grad)


def solution(mesh):
    in_specs = (
        P("dp", "seq", None),
        P("dp", "seq", None),
        P("dp", "seq", None),
        P("dp", None),
        P("dp", None),
        P("dp", "seq", None),
    )
    out_specs = (P("dp", "seq", None), P("dp", "seq", None), P("dp", "seq", None), P("dp", None))
    return jax.shard_map(body, mesh=mesh, in_specs=in_specs, out_specs=out_specs, check_vma=False)
```

```python
import functools
import math

import jax
import jax.numpy as jnp
from jax import lax
from jax.experimental import pallas as pl
from jax.experimental.pallas import tpu as pltpu
from jax.sharding import PartitionSpec as P

QH = 8
HD = 128
BLOCK = 128
TILE_BLOCKS = 4

EPSILON = 1e-06
LOG2E = math.log2(math.e)


def frequencies(size):
    expo = jnp.arange(0, size, 2).astype(jnp.float32) / size
    base = 1.0 / jnp.power(jnp.float32(500000.0), expo)
    wavelen = 2.0 * math.pi / base
    mixing = (8192.0 / wavelen - 1.0) / 3.0
    blended = (1.0 - mixing) * base / 8.0 + mixing * base
    return jnp.where(wavelen < 2048.0, base, jnp.where(wavelen > 8192.0, base / 8.0, blended))


def softstep(scaled):
    return scaled - jnp.sin(2.0 * math.pi * (scaled - jnp.round(scaled))) / (2.0 * math.pi)


def dot_cols(left, right):
    return lax.dot_general(
        left, right, (((1,), (1,)), ((), ())), preferred_element_type=jnp.float32
    )


def dot(left, right):
    return jnp.dot(left, right, preferred_element_type=jnp.float32)


def tile_of(plan_ref, core_ref, near_ref, far_ref, tile):
    slots = [plan_ref[tile * TILE_BLOCKS + step] for step in range(TILE_BLOCKS)]
    near = jnp.concatenate([near_ref[slot] for slot in slots], axis=0)
    far = jnp.concatenate([far_ref[slot] for slot in slots], axis=0)
    is_first = core_ref[0] == 0
    return jnp.where(is_first, near, far), jnp.where(is_first, far, near)


def tile_counts(plan_ref, blocks, group):
    below = plan_ref[2 * blocks + 2 + group]
    seen = below + 1 - group
    return lax.div(below, TILE_BLOCKS), lax.div(seen + TILE_BLOCKS - 1, TILE_BLOCKS)


def visible_in(plan_ref, blocks, group, tile, rows):
    offsets = lax.broadcasted_iota(jnp.int32, (BLOCK, 1), 0)
    key_at = jnp.concatenate(
        [
            plan_ref[blocks + tile * TILE_BLOCKS + step] * BLOCK + offsets
            for step in range(TILE_BLOCKS)
        ],
        axis=0,
    )
    token = lax.rem(lax.broadcasted_iota(jnp.int32, (1, rows), 1), BLOCK)
    return key_at <= plan_ref[2 * blocks + group] * BLOCK + token


SCORE_SCALE = LOG2E / math.sqrt(HD)


def totals_kernel(plan_ref, core_ref, near_ref, far_ref, *rest):
    query_refs, out_ref = rest[:-1], rest[-1]
    blocks = near_ref.shape[0]
    rows = QH * BLOCK
    span = TILE_BLOCKS * BLOCK

    def folded(values):
        return jnp.sum(values.reshape(span // 8, 8, rows), axis=0)

    for group in range(2):
        q_cols, g_cols = query_refs[2 * group], query_refs[2 * group + 1]

        def step(tile, sums, masked, q_cols=q_cols, g_cols=g_cols, group=group):
            total, weighted, top = sums
            keys, values = tile_of(plan_ref, core_ref, near_ref, far_ref, tile)
            scores = dot(keys, q_cols[...]) * SCORE_SCALE
            if masked:
                visible = visible_in(plan_ref, blocks, group, tile, rows)
                scores = jnp.where(visible, scores, -jnp.inf)
            highest = jnp.maximum(top, jnp.max(scores, axis=0, keepdims=True))
            shrink = jnp.exp2(top - highest)
            exponent = jnp.exp2(scores - highest)
            prob_grad = dot(values, g_cols[...])
            total = total * shrink + folded(exponent)
            weighted = weighted * shrink + folded(exponent * prob_grad)
            return (total, weighted, highest)

        full, tiles = tile_counts(plan_ref, blocks, group)
        empty = jnp.zeros((8, rows), jnp.float32)
        sums = (empty, empty, jnp.full((1, rows), -1e30, jnp.float32))
        sums = lax.fori_loop(0, full, functools.partial(step, masked=False), sums)
        total, weighted, top = lax.fori_loop(
            full, tiles, functools.partial(step, masked=True), sums
        )
        out_ref[group, 0:1, :] = top
        out_ref[group, 1:2, :] = jnp.sum(total, axis=0, keepdims=True)
        out_ref[group, 2:3, :] = jnp.sum(weighted, axis=0, keepdims=True)


def grads_kernel(plan_ref, core_ref, near_ref, far_ref, own_ref, other_ref, *rest):
    query_refs, (dq_ref, dq_sent_ref, near_grad_ref, far_grad_ref) = rest[:8], rest[8:12]
    key_sums, value_sums, dq_cols = rest[12:]
    blocks = near_ref.shape[0]
    rows = QH * BLOCK
    is_first = core_ref[0] == 0
    key_sums[...] = jnp.zeros_like(key_sums)
    value_sums[...] = jnp.zeros_like(value_sums)

    for group, out_ref in enumerate((dq_ref, dq_sent_ref)):
        q_cols, g_cols, q_rows, g_rows = query_refs[4 * group : 4 * group + 4]
        here, there = own_ref[group], other_ref[1 - group]
        top = jnp.maximum(here[0:1], there[0:1])
        here_part, there_part = jnp.exp2(here[0:1] - top), jnp.exp2(there[0:1] - top)
        total = here[1:2] * here_part + there[1:2] * there_part
        row_delta = (here[2:3] * here_part + there[2:3] * there_part) / total
        log_total = top + jnp.log(total) * LOG2E
        dq_cols[...] = jnp.zeros_like(dq_cols)

        def step(
            tile, carry, masked, group=group, q_cols=q_cols, g_cols=g_cols, q_rows=q_rows,
            g_rows=g_rows, row_delta=row_delta, log_total=log_total,
        ):
            keys, values = tile_of(plan_ref, core_ref, near_ref, far_ref, tile)
            probs = jnp.exp2(dot(keys, q_cols[...]) * SCORE_SCALE - log_total)
            if masked:
                probs = jnp.where(visible_in(plan_ref, blocks, group, tile, rows), probs, 0.0)
            prob_grad = dot(values, g_cols[...])
            score_grad = (probs * (prob_grad - row_delta)).astype(jnp.bfloat16)
            value_sums[tile] += dot(probs.astype(jnp.bfloat16), g_rows[...])
            key_sums[tile] += dot(score_grad, q_rows[...])
            dq_cols[...] += dot(keys.T, score_grad)
            return carry

        full, tiles = tile_counts(plan_ref, blocks, group)
        lax.fori_loop(0, full, functools.partial(step, masked=False), 0)
        lax.fori_loop(full, tiles, functools.partial(step, masked=True), 0)
        for head in range(QH):
            part = pl.ds(head * HD, HD)
            out_ref[:, part] = (dq_cols[:, part].T * (1.0 / math.sqrt(HD))).astype(out_ref.dtype)

    @pl.loop(0, blocks // TILE_BLOCKS)
    def _(tile):
        key_grad = key_sums[tile].astype(jnp.bfloat16)
        value_grad = value_sums[tile].astype(jnp.bfloat16)
        near_grad = jnp.where(is_first, key_grad, value_grad)
        far_grad = jnp.where(is_first, value_grad, key_grad)
        for step in range(TILE_BLOCKS):
            slot = plan_ref[tile * TILE_BLOCKS + step]
            near_grad_ref[slot] = near_grad[step * BLOCK : (step + 1) * BLOCK]
            far_grad_ref[slot] = far_grad[step * BLOCK : (step + 1) * BLOCK]


def copies_kernel(core_ref, weight_ref, out_ref):
    start = pl.multiple_of(core_ref[0] * HD, HD)
    half = weight_ref[:, pl.ds(start, HD)]
    for copy in range(out_ref.shape[0]):
        out_ref[copy] = half


def query_kernel(q_ref, g_ref, q_cols, g_cols, q_rows, g_rows):
    for head in range(QH):
        part = pl.ds(head * HD, HD)
        q_cols[:, part] = q_ref[:, part].T
        g_cols[:, part] = g_ref[:, part].T
        q_rows[part, :] = q_ref[:, part]
        g_rows[part, :] = g_ref[:, part]


def local_call(kernel, shapes, scalars, arrays, name, scratch=(), limit=32):
    smem = pl.BlockSpec(memory_space=pltpu.SMEM)
    vmem = pl.BlockSpec(memory_space=pltpu.VMEM)
    return pl.pallas_call(
        kernel,
        out_shape=shapes,
        in_specs=[smem] * len(scalars) + [vmem] * len(arrays),
        out_specs=jax.tree.map(lambda _: vmem, shapes),
        scratch_shapes=scratch,
        compiler_params=pltpu.CompilerParams(vmem_limit_bytes=limit * 1024 * 1024),
        name=name,
    )(*scalars, *arrays)


def project_kernel(core_ref, levels_ref, own_ref, far_ref, weight_ref, cos_ref, sin_ref, out_ref):
    core = core_ref[0]
    weight = weight_ref[...]
    for distance, x_ref in enumerate((own_ref, far_ref)):
        at = core if distance == 0 else 1 - core
        raw = dot(x_ref[...], weight)
        turned = raw * cos_ref[at] + pltpu.roll(raw, HD // 2, 1) * sin_ref[at]
        largest = jnp.max(jnp.abs(turned), axis=0, keepdims=True)
        level_step = (largest + EPSILON) / levels_ref[distance]
        quantized = (level_step * softstep(turned / level_step)).astype(jnp.bfloat16)
        for copy in range(out_ref.shape[0]):
            out_ref[copy, at] = quantized


def settle_kernel(arrived_ref, cos_ref, sin_ref, out_ref):
    for at in range(2):
        grads = arrived_ref[0, at].astype(jnp.float32)
        for source in range(1, arrived_ref.shape[0]):
            grads += arrived_ref[source, at].astype(jnp.float32)
        turned = grads * cos_ref[at] - pltpu.roll(grads, HD // 2, 1) * sin_ref[at]
        turned = turned.astype(jnp.bfloat16)
        for copy in range(out_ref.shape[0]):
            out_ref[copy, at] = turned


def turn_kernel(parity_ref, x_ref, keep_ref, *rest):
    parity = parity_ref[0]
    for group in range(keep_ref.shape[0] // BLOCK):
        rows = slice(group * BLOCK, (group + 1) * BLOCK)
        for out_ref, half in zip((keep_ref, *rest), (parity, 1 - parity)):
            start = pl.multiple_of((2 * group + half) * BLOCK, BLOCK)
            out_ref[rows, :] = x_ref[:, pl.ds(start, BLOCK)].T


def turned_halves(parity, x_rows, count, name):
    tokens, width = x_rows.shape
    shape = jax.ShapeDtypeStruct((width // 2, tokens), x_rows.dtype)
    return local_call(turn_kernel, (shape,) * count, (parity,), (x_rows,), name)


def share_kernel(core_ref, *rest):
    core = core_ref[0]
    own_ref, own_far_ref, next_ref, next_far_ref, grads_ref, next_grads_ref, out_ref = rest
    quads, groups, piece, _ = out_ref.shape
    own = jnp.concatenate([grads_ref[core], grads_ref[1 - core]], axis=0)
    beside = jnp.concatenate([next_grads_ref[core], next_grads_ref[1 - core]], axis=0)
    for group in range(groups):
        rows = slice(group * BLOCK, (group + 1) * BLOCK)
        share = dot(jnp.concatenate([own_ref[rows, :], own_far_ref[rows, :]], axis=1), own)
        share += dot(jnp.concatenate([next_ref[rows, :], next_far_ref[rows, :]], axis=1), beside)
        share = share.astype(out_ref.dtype)
        for quad in range(quads):
            out_ref[quad, group] = share[quad * piece : (quad + 1) * piece]


def total_kernel(parts_ref, out_ref):
    total = parts_ref[0].astype(jnp.float32)
    for source in range(1, parts_ref.shape[0]):
        total += parts_ref[source].astype(jnp.float32)
    total = total.astype(out_ref.dtype)
    for copy in range(out_ref.shape[0]):
        out_ref[copy] = total


def assemble_kernel(grad_scale, parts_ref, out_ref):
    _, quads, _, _, piece, _ = parts_ref.shape
    for quad in range(quads):
        for parity in range(2):
            for core in range(2):
                low = parts_ref[0, quad, parity, core].astype(jnp.float32)
                high = parts_ref[1, quad, parity, core].astype(jnp.float32)
                row = parity * BLOCK + quad * piece
                out_ref[row : row + piece, core * HD : (core + 1) * HD] = (
                    low + high
                ) * grad_scale


def body(hidden_in, queries, out_grad, kv_weight, block_pos, precision):
    score_scale = 1.0 / math.sqrt(HD)
    tokens = hidden_in.shape[1]
    width = hidden_in.shape[2]
    seq_count = lax.axis_size("seq")
    dp_count = lax.axis_size("dp")
    half_count = seq_count // 2
    columns = half_count // 2
    grad_scale = 1.0 / math.sqrt(dp_count * seq_count * tokens)
    self_index = lax.axis_index("seq")
    core_index = lax.rem(self_index, 2)
    core = core_index.reshape(1).astype(jnp.int32)
    is_first = core_index == 0
    quads = columns // 2
    parity = lax.rem(lax.div(self_index, 2), 2).reshape(1).astype(jnp.int32)
    quad_groups = [
        [start * half_count + 4 * quad + side for quad in range(quads)]
        for start in range(2)
        for side in range(4)
    ]
    column_groups = [
        [start * half_count + 2 * column + side for column in range(columns)]
        for start in range(2)
        for side in range(2)
    ]
    run = math.gcd(dp_count, 4)
    runs = [[start + step for step in range(run)] for start in range(0, dp_count, run)]
    strides = [[start + step for step in range(0, dp_count, run)] for start in range(run)]
    swap = [(source, source ^ 1) for source in range(seq_count)]
    cross = [(source, (source + half_count) % seq_count) for source in range(seq_count)]
    beside = [(source, source ^ 2) for source in range(seq_count)]

    def swapped(value):
        return lax.ppermute(value, "seq", swap)

    def crossed(value):
        return lax.ppermute(value, "seq", cross)

    def moved(value, steps):
        pairs = []
        for group in range(dp_count):
            for member in range(seq_count):
                high = member // half_count
                place_y = (high * run + group % run + steps) % (2 * run)
                target_group = group // run * run + place_y % run
                target = place_y // run * half_count + member % half_count
                pairs.append((group * seq_count + member, target_group * seq_count + target))
        return lax.ppermute(value, ("dp", "seq"), pairs)

    def passed(value):
        return lax.ppermute(value, "seq", beside)

    def exchanged(value, axis, groups=None):
        return lax.all_to_all(value, axis, 0, 0, axis_index_groups=groups)

    x_rows = hidden_in[0]
    places = block_pos[0]
    half_places = lax.dynamic_slice_in_dim(
        places, lax.div(self_index, half_count) * half_count, half_count
    )
    own_place = lax.dynamic_slice_in_dim(places, self_index, 1)
    cross_place = lax.dynamic_slice_in_dim(
        places, lax.rem(self_index + half_count, seq_count), 1
    )
    slots = jnp.arange(half_count, dtype=jnp.int32)
    below = (half_places[None, :] < half_places[:, None]).astype(jnp.int32)
    ranked = jnp.sum(below, axis=1)[None, :] == slots[:, None]
    order = jnp.sum(jnp.where(ranked, slots[None, :], 0), axis=1)
    ranked_places = jnp.sum(jnp.where(ranked, half_places[None, :], 0), axis=1)
    group_places = jnp.concatenate([own_place, cross_place])
    seen = jnp.sum((half_places[None, :] < group_places[:, None]).astype(jnp.int32), axis=1)
    plan = jnp.concatenate([order, ranked_places, group_places, seen]).astype(jnp.int32)

    with jax.named_scope("rotation"):
        pair_places = lax.dynamic_slice_in_dim(places, self_index - core_index, 2)
        pair_pos = pair_places[:, None] * BLOCK + jnp.arange(tokens, dtype=jnp.int32)[None, :]
        freq = frequencies(HD)
        angles = pair_pos.astype(jnp.float32)[:, :, None] * jnp.concatenate([freq, freq])
        lane = jnp.arange(HD, dtype=jnp.int32)
        cosine = jnp.where(is_first, jnp.cos(angles), 1.0)
        sine_part = jnp.where(
            is_first, jnp.sin(angles) * jnp.where(lane < HD // 2, -1.0, 1.0), 0.0
        )
        back_scale = jnp.where(is_first, score_scale, 1.0)
        back_cosine = cosine * back_scale
        back_sine = sine_part * back_scale
        pair_bits = jnp.concatenate([precision[0], swapped(precision[0])])
        bits_here = jnp.where(is_first, pair_bits[:, 0], pair_bits[:, 1])
        levels = (lax.shift_left(jnp.ones_like(bits_here), bits_here - 1) - 1).astype(jnp.float32)
        x_far = swapped(x_rows)
        own_half, given_half = turned_halves(parity, x_rows, 2, "own_halves")
        next_half = passed(given_half)
        (far_half,) = turned_halves(parity, x_far, 1, "far_half")
    with jax.named_scope("weight_gather"):
        copies = local_call(
            copies_kernel,
            jax.ShapeDtypeStruct((run, kv_weight.shape[0], HD), kv_weight.dtype),
            (core,),
            (kv_weight,),
            "weight_copies",
        )
        run_weight = exchanged(copies, "dp", runs)
        run_weight, q_start, g_start = lax.optimization_barrier(
            (run_weight, queries[0], out_grad[0])
        )
        q_middle, g_middle = moved(q_start, run // 2), moved(g_start, -(run // 2))
        copies = jnp.broadcast_to(run_weight[None], (dp_count // run, *run_weight.shape))
        copies = lax.optimization_barrier(copies)
        near_weight = exchanged(copies, "dp", strides).reshape(width, HD)
        (
            near_weight, q_middle, g_middle, plan, cosine, sine_part, back_cosine, back_sine, levels, x_far,
            own_half, next_half, far_half,
        ) = lax.optimization_barrier(
            (
                near_weight, q_middle, g_middle, plan, cosine, sine_part, back_cosine, back_sine, levels, x_far,
                own_half, next_half, far_half,
            )
        )
    with jax.named_scope("projection"):
        stacked = local_call(
            project_kernel,
            jax.ShapeDtypeStruct((columns, 2, tokens, HD), jnp.bfloat16),
            (core, levels),
            (x_rows, x_far, near_weight, cosine, sine_part),
            "projection",
        )
    with jax.named_scope("kv_gather"):
        near = exchanged(stacked, "seq", column_groups).reshape(half_count, tokens, HD)
        q_cross, g_cross = moved(q_middle, run // 2), moved(g_middle, -(run // 2))
        columns_shape = jax.ShapeDtypeStruct((HD, QH * tokens), jnp.bfloat16)
        rows_shape = jax.ShapeDtypeStruct((QH * tokens, HD), jnp.bfloat16)
        query_shapes = (columns_shape, columns_shape, rows_shape, rows_shape)
        own_forms = local_call(
            query_kernel, query_shapes, (), (queries[0], out_grad[0]), "own_query_forms"
        )
        cross_forms = local_call(
            query_kernel, query_shapes, (), (q_cross, g_cross), "cross_query_forms"
        )
        near, own_forms, cross_forms = lax.optimization_barrier((near, own_forms, cross_forms))
        far = swapped(near)
    with jax.named_scope("attention"):
        totals = local_call(
            totals_kernel,
            jax.ShapeDtypeStruct((2, 3, QH * tokens), jnp.float32),
            (plan, core),
            (near, far, *own_forms[:2], *cross_forms[:2]),
            "attention_totals",
            (),
            48,
        )
        sum_tiles = (half_count // TILE_BLOCKS, TILE_BLOCKS * BLOCK, HD)
        dq_own, dq_sent, near_grad, far_grad = local_call(
            grads_kernel,
            (
                jax.ShapeDtypeStruct((tokens, QH * HD), jnp.float32),
                jax.ShapeDtypeStruct((tokens, QH * HD), jnp.bfloat16),
                jax.ShapeDtypeStruct(near.shape, jnp.bfloat16),
                jax.ShapeDtypeStruct(near.shape, jnp.bfloat16),
            ),
            (plan, core),
            (near, far, totals, crossed(totals), *own_forms, *cross_forms),
            "attention_grads",
            (
                pltpu.VMEM(sum_tiles, jnp.float32),
                pltpu.VMEM(sum_tiles, jnp.float32),
                pltpu.VMEM((HD, QH * tokens), jnp.float32),
            ),
            48,
        )
    with jax.named_scope("kv_reduce"):
        pair = near_grad.astype(jnp.float32) + swapped(far_grad).astype(jnp.float32)
        pair = pair.astype(jnp.bfloat16).reshape(columns, 2, tokens, HD)
        pair, next_half, near_weight, dq_sent = lax.optimization_barrier(
            (pair, next_half, near_weight, dq_sent)
        )
        arrived = exchanged(pair, "seq", column_groups)
        next_far_half = swapped(next_half)
        far_weight = swapped(near_weight)
        arrived, next_far_half, far_weight = lax.optimization_barrier(
            (arrived, next_far_half, far_weight)
        )
    with jax.named_scope("query_grad"):
        query_grad = (dq_own + crossed(dq_sent).astype(jnp.float32)).astype(jnp.bfloat16)
    with jax.named_scope("projection_grad"):
        settled = local_call(
            settle_kernel,
            jax.ShapeDtypeStruct((1, 2, tokens, HD), jnp.bfloat16),
            (),
            (arrived, back_cosine, back_sine),
            "projection_grad",
        )
    with jax.named_scope("weight_grad"):
        piece = BLOCK // quads
        share = local_call(
            share_kernel,
            jax.ShapeDtypeStruct((quads, dp_count, piece, HD), jnp.bfloat16),
            (core,),
            (own_half, far_half, next_half, next_far_half, settled[0], passed(settled[0])),
            "weight_share",
        )
        quad_parts = exchanged(share, "seq", quad_groups)
        (quad_share,) = local_call(
            total_kernel,
            (jax.ShapeDtypeStruct((1, dp_count, piece, HD), jnp.bfloat16),),
            (),
            (quad_parts,),
            "quad_share",
        )
        share_parts = exchanged(quad_share[0], "dp")
        group_share = local_call(
            total_kernel,
            jax.ShapeDtypeStruct((seq_count, piece, HD), jnp.bfloat16),
            (),
            (share_parts,),
            "group_share",
        )
        gathered = exchanged(group_share, "seq")
        weight_grad = local_call(
            functools.partial(assemble_kernel, grad_scale),
            jax.ShapeDtypeStruct((width // dp_count, 2 * HD), jnp.float32),
            (),
            (gathered.reshape(2, quads, 2, 2, piece, HD),),
            "weight_grad",
        )
    with jax.named_scope("input_grad"):
        both = settled[0]
        own = jnp.where(is_first, both[0], both[1])
        other = swapped(jnp.where(is_first, both[1], both[0]))
        proj_grad = jnp.concatenate(
            [jnp.where(is_first, own, other), jnp.where(is_first, other, own)], axis=1
        )
        input_grad = (dot_cols(own, near_weight) + dot_cols(other, far_weight)).astype(
            jnp.bfloat16
        )
    return (query_grad[None], proj_grad[None], input_grad[None], weight_grad)


def solution(mesh):
    in_specs = (
        P("dp", "seq", None),
        P("dp", "seq", None),
        P("dp", "seq", None),
        P("dp", None),
        P("dp", None),
        P("dp", "seq", None),
    )
    out_specs = (P("dp", "seq", None), P("dp", "seq", None), P("dp", "seq", None), P("dp", None))
    return jax.shard_map(body, mesh=mesh, in_specs=in_specs, out_specs=out_specs, check_vma=False)
```

```python
import functools
import math

import jax
import jax.numpy as jnp
import numpy as np
from jax import lax
from jax.experimental import pallas as pl
from jax.experimental.pallas import tpu as pltpu
from jax.sharding import PartitionSpec as P

QH = 8
HD = 128
BLOCK = 128
TILE_BLOCKS = 4

EPSILON = 1e-06
LOG2E = math.log2(math.e)


def frequencies(size):
    expo = np.arange(0, size, 2).astype(np.float32) / np.float32(size)
    base = np.float32(1.0) / np.power(np.float32(500000.0), expo)
    wavelen = np.float32(2.0 * math.pi) / base
    mixing = (np.float32(8192.0) / wavelen - np.float32(1.0)) / np.float32(3.0)
    blended = (1.0 - mixing) * base / 8.0 + mixing * base
    slow = np.where(wavelen > 8192.0, base / 8.0, blended)
    return np.where(wavelen < 2048.0, base, slow).astype(np.float32)


def softstep(scaled):
    return scaled - jnp.sin(2.0 * math.pi * (scaled - jnp.round(scaled))) / (2.0 * math.pi)


def dot_cols(left, right):
    return lax.dot_general(
        left, right, (((1,), (1,)), ((), ())), preferred_element_type=jnp.float32
    )


def dot(left, right):
    return jnp.dot(left, right, preferred_element_type=jnp.float32)


def plan_kernel(index_ref, places_ref, plan_ref, slot_at):
    blocks = slot_at.shape[0]
    half = blocks // 2
    me = index_ref[0]
    start = lax.div(me, half) * half
    for place in range(blocks):
        slot_at[place] = -1
    for slot in range(half):
        slot_at[places_ref[start + slot]] = slot
    own = places_ref[me]
    cross = places_ref[lax.rem(me + half, blocks)]

    def visit(place, counts):
        rank, below_own, below_cross = counts
        slot = slot_at[place]
        found = slot >= 0

        @pl.when(found)
        def _():
            plan_ref[rank] = slot
            plan_ref[half + rank] = place

        one = jnp.where(found, 1, 0)
        return (
            rank + one,
            below_own + jnp.where(place < own, one, 0),
            below_cross + jnp.where(place < cross, one, 0),
        )

    _, below_own, below_cross = lax.fori_loop(0, blocks, visit, (0, 0, 0))
    plan_ref[2 * half] = own
    plan_ref[2 * half + 1] = cross
    plan_ref[2 * half + 2] = below_own
    plan_ref[2 * half + 3] = below_cross


def tile_of(plan_ref, core_ref, near_ref, far_ref, tile):
    slots = [plan_ref[tile * TILE_BLOCKS + step] for step in range(TILE_BLOCKS)]
    near = jnp.concatenate([near_ref[slot] for slot in slots], axis=0)
    far = jnp.concatenate([far_ref[slot] for slot in slots], axis=0)
    is_first = core_ref[0] == 0
    return jnp.where(is_first, near, far), jnp.where(is_first, far, near)


def tile_counts(plan_ref, blocks, group):
    below = plan_ref[2 * blocks + 2 + group]
    seen = below + 1 - group
    return lax.div(below, TILE_BLOCKS), lax.div(seen + TILE_BLOCKS - 1, TILE_BLOCKS)


def visible_in(plan_ref, blocks, group, tile, rows):
    offsets = lax.broadcasted_iota(jnp.int32, (BLOCK, 1), 0)
    key_at = jnp.concatenate(
        [
            plan_ref[blocks + tile * TILE_BLOCKS + step] * BLOCK + offsets
            for step in range(TILE_BLOCKS)
        ],
        axis=0,
    )
    token = lax.rem(lax.broadcasted_iota(jnp.int32, (1, rows), 1), BLOCK)
    return key_at <= plan_ref[2 * blocks + group] * BLOCK + token


SCORE_SCALE = LOG2E / math.sqrt(HD)


def totals_kernel(plan_ref, core_ref, near_ref, far_ref, *rest):
    query_refs, out_ref = rest[:-1], rest[-1]
    blocks = near_ref.shape[0]
    rows = QH * BLOCK
    span = TILE_BLOCKS * BLOCK

    def folded(values):
        return jnp.sum(values.reshape(span // 8, 8, rows), axis=0)

    for group in range(2):
        q_cols, g_cols = query_refs[2 * group], query_refs[2 * group + 1]

        def step(tile, sums, masked, q_cols=q_cols, g_cols=g_cols, group=group):
            total, weighted, top = sums
            keys, values = tile_of(plan_ref, core_ref, near_ref, far_ref, tile)
            scores = dot(keys, q_cols[...]) * SCORE_SCALE
            if masked:
                visible = visible_in(plan_ref, blocks, group, tile, rows)
                scores = jnp.where(visible, scores, -jnp.inf)
            highest = jnp.maximum(top, jnp.max(scores, axis=0, keepdims=True))
            shrink = jnp.exp2(top - highest)
            exponent = jnp.exp2(scores - highest)
            prob_grad = dot(values, g_cols[...])
            total = total * shrink + folded(exponent)
            weighted = weighted * shrink + folded(exponent * prob_grad)
            return (total, weighted, highest)

        full, tiles = tile_counts(plan_ref, blocks, group)
        empty = jnp.zeros((8, rows), jnp.float32)
        sums = (empty, empty, jnp.full((1, rows), -1e30, jnp.float32))
        sums = lax.fori_loop(0, full, functools.partial(step, masked=False), sums)
        total, weighted, top = lax.fori_loop(
            full, tiles, functools.partial(step, masked=True), sums
        )
        out_ref[group, 0:1, :] = top
        out_ref[group, 1:2, :] = jnp.sum(total, axis=0, keepdims=True)
        out_ref[group, 2:3, :] = jnp.sum(weighted, axis=0, keepdims=True)


def grads_kernel(plan_ref, core_ref, near_ref, far_ref, own_ref, other_ref, *rest):
    query_refs, (dq_ref, dq_sent_ref, near_grad_ref, far_grad_ref) = rest[:8], rest[8:12]
    key_sums, value_sums, dq_cols = rest[12:]
    blocks = near_ref.shape[0]
    rows = QH * BLOCK
    is_first = core_ref[0] == 0
    key_sums[...] = jnp.zeros_like(key_sums)
    value_sums[...] = jnp.zeros_like(value_sums)

    for group, out_ref in enumerate((dq_ref, dq_sent_ref)):
        q_cols, g_cols, q_rows, g_rows = query_refs[4 * group : 4 * group + 4]
        here, there = own_ref[group], other_ref[1 - group]
        top = jnp.maximum(here[0:1], there[0:1])
        here_part, there_part = jnp.exp2(here[0:1] - top), jnp.exp2(there[0:1] - top)
        total = here[1:2] * here_part + there[1:2] * there_part
        row_delta = (here[2:3] * here_part + there[2:3] * there_part) / total
        log_total = top + jnp.log(total) * LOG2E
        dq_cols[...] = jnp.zeros_like(dq_cols)

        def step(
            tile, carry, masked, group=group, q_cols=q_cols, g_cols=g_cols, q_rows=q_rows,
            g_rows=g_rows, row_delta=row_delta, log_total=log_total,
        ):
            keys, values = tile_of(plan_ref, core_ref, near_ref, far_ref, tile)
            probs = jnp.exp2(dot(keys, q_cols[...]) * SCORE_SCALE - log_total)
            if masked:
                probs = jnp.where(visible_in(plan_ref, blocks, group, tile, rows), probs, 0.0)
            prob_grad = dot(values, g_cols[...])
            score_grad = (probs * (prob_grad - row_delta)).astype(jnp.bfloat16)
            value_sums[tile] += dot(probs.astype(jnp.bfloat16), g_rows[...])
            key_sums[tile] += dot(score_grad, q_rows[...])
            dq_cols[...] += dot(keys.T, score_grad)
            return carry

        full, tiles = tile_counts(plan_ref, blocks, group)
        lax.fori_loop(0, full, functools.partial(step, masked=False), 0)
        lax.fori_loop(full, tiles, functools.partial(step, masked=True), 0)
        for head in range(QH):
            part = pl.ds(head * HD, HD)
            out_ref[:, part] = (dq_cols[:, part].T * (1.0 / math.sqrt(HD))).astype(out_ref.dtype)

    @pl.loop(0, blocks // TILE_BLOCKS)
    def _(tile):
        key_grad = key_sums[tile].astype(jnp.bfloat16)
        value_grad = value_sums[tile].astype(jnp.bfloat16)
        near_grad = jnp.where(is_first, key_grad, value_grad)
        far_grad = jnp.where(is_first, value_grad, key_grad)
        for step in range(TILE_BLOCKS):
            slot = plan_ref[tile * TILE_BLOCKS + step]
            near_grad_ref[slot] = near_grad[step * BLOCK : (step + 1) * BLOCK]
            far_grad_ref[slot] = far_grad[step * BLOCK : (step + 1) * BLOCK]


def copies_kernel(core_ref, weight_ref, out_ref):
    start = pl.multiple_of(core_ref[0] * HD, HD)
    half = weight_ref[:, pl.ds(start, HD)]
    for copy in range(out_ref.shape[0]):
        out_ref[copy] = half


def query_kernel(q_ref, g_ref, q_cols, g_cols, q_rows, g_rows):
    for head in range(QH):
        part = pl.ds(head * HD, HD)
        q_cols[:, part] = q_ref[:, part].T
        g_cols[:, part] = g_ref[:, part].T
        q_rows[part, :] = q_ref[:, part]
        g_rows[part, :] = g_ref[:, part]


def local_call(kernel, shapes, scalars, arrays, name, scratch=(), limit=32):
    smem = pl.BlockSpec(memory_space=pltpu.SMEM)
    vmem = pl.BlockSpec(memory_space=pltpu.VMEM)
    return pl.pallas_call(
        kernel,
        out_shape=shapes,
        in_specs=[smem] * len(scalars) + [vmem] * len(arrays),
        out_specs=jax.tree.map(lambda _: vmem, shapes),
        scratch_shapes=scratch,
        compiler_params=pltpu.CompilerParams(vmem_limit_bytes=limit * 1024 * 1024),
        name=name,
    )(*scalars, *arrays)


def turning(core_ref, cos_ref, sin_ref, at):
    is_first = core_ref[0] == 0
    first_half = lax.broadcasted_iota(jnp.int32, (1, HD), 1) < HD // 2
    sine_part = jnp.where(first_half, -sin_ref[at], sin_ref[at])
    return jnp.where(is_first, cos_ref[at], 1.0), jnp.where(is_first, sine_part, 0.0)


def project_kernel(
    core_ref, own_bits_ref, far_bits_ref, own_ref, far_ref, weight_ref, cos_ref, sin_ref, out_ref
):
    core = core_ref[0]
    weight = weight_ref[...]
    for x_ref, bits_ref, at in ((own_ref, own_bits_ref, core), (far_ref, far_bits_ref, 1 - core)):
        raw = dot(x_ref[...], weight)
        cosine, sine_part = turning(core_ref, cos_ref, sin_ref, at)
        turned = raw * cosine + pltpu.roll(raw, HD // 2, 1) * sine_part
        largest = jnp.max(jnp.abs(turned), axis=0, keepdims=True)
        levels = (lax.shift_left(jnp.int32(1), bits_ref[core] - 1) - 1).astype(jnp.float32)
        level_step = (largest + EPSILON) / levels
        quantized = (level_step * softstep(turned / level_step)).astype(jnp.bfloat16)
        for copy in range(out_ref.shape[0]):
            out_ref[copy, at] = quantized


def settle_kernel(core_ref, arrived_ref, cos_ref, sin_ref, out_ref):
    scale = jnp.where(core_ref[0] == 0, 1.0 / math.sqrt(HD), 1.0)
    for at in range(2):
        grads = arrived_ref[0, at].astype(jnp.float32)
        for source in range(1, arrived_ref.shape[0]):
            grads += arrived_ref[source, at].astype(jnp.float32)
        cosine, sine_part = turning(core_ref, cos_ref, sin_ref, at)
        grads = grads * scale
        turned = grads * cosine - pltpu.roll(grads, HD // 2, 1) * sine_part
        out_ref[0, at] = turned.astype(jnp.bfloat16)


def turn_kernel(parity_ref, x_ref, keep_ref, *rest):
    parity = parity_ref[0]
    for group in range(keep_ref.shape[0] // BLOCK):
        rows = slice(group * BLOCK, (group + 1) * BLOCK)
        for out_ref, half in zip((keep_ref, *rest), (parity, 1 - parity)):
            start = pl.multiple_of((2 * group + half) * BLOCK, BLOCK)
            out_ref[rows, :] = x_ref[:, pl.ds(start, BLOCK)].T


def turned_halves(parity, x_rows, count, name):
    tokens, width = x_rows.shape
    shape = jax.ShapeDtypeStruct((width // 2, tokens), x_rows.dtype)
    return local_call(turn_kernel, (shape,) * count, (parity,), (x_rows,), name)


def share_kernel(core_ref, *rest):
    core = core_ref[0]
    own_ref, own_far_ref, next_ref, next_far_ref, grads_ref, next_grads_ref, out_ref = rest
    quads, groups, piece, _ = out_ref.shape
    own = jnp.concatenate([grads_ref[core], grads_ref[1 - core]], axis=0)
    beside = jnp.concatenate([next_grads_ref[core], next_grads_ref[1 - core]], axis=0)
    for group in range(groups):
        rows = slice(group * BLOCK, (group + 1) * BLOCK)
        share = dot(jnp.concatenate([own_ref[rows, :], own_far_ref[rows, :]], axis=1), own)
        share += dot(jnp.concatenate([next_ref[rows, :], next_far_ref[rows, :]], axis=1), beside)
        share = share.astype(out_ref.dtype)
        for quad in range(quads):
            out_ref[quad, group] = share[quad * piece : (quad + 1) * piece]


def total_kernel(parts_ref, out_ref):
    total = parts_ref[0].astype(jnp.float32)
    for source in range(1, parts_ref.shape[0]):
        total += parts_ref[source].astype(jnp.float32)
    total = total.astype(out_ref.dtype)
    for copy in range(out_ref.shape[0]):
        out_ref[copy] = total


def assemble_kernel(grad_scale, parts_ref, out_ref):
    _, quads, _, _, piece, _ = parts_ref.shape
    for quad in range(quads):
        for parity in range(2):
            for core in range(2):
                low = parts_ref[0, quad, parity, core].astype(jnp.float32)
                high = parts_ref[1, quad, parity, core].astype(jnp.float32)
                row = parity * BLOCK + quad * piece
                out_ref[row : row + piece, core * HD : (core + 1) * HD] = (
                    low + high
                ) * grad_scale


def body(hidden_in, queries, out_grad, kv_weight, block_pos, precision):
    tokens = hidden_in.shape[1]
    width = hidden_in.shape[2]
    seq_count = lax.axis_size("seq")
    dp_count = lax.axis_size("dp")
    half_count = seq_count // 2
    columns = half_count // 2
    grad_scale = 1.0 / math.sqrt(dp_count * seq_count * tokens)
    self_index = lax.axis_index("seq")
    core_index = lax.rem(self_index, 2)
    core = core_index.reshape(1).astype(jnp.int32)
    is_first = core_index == 0
    quads = columns // 2
    parity = lax.rem(lax.div(self_index, 2), 2).reshape(1).astype(jnp.int32)
    quad_groups = [
        [start * half_count + 4 * quad + side for quad in range(quads)]
        for start in range(2)
        for side in range(4)
    ]
    column_groups = [
        [start * half_count + 2 * column + side for column in range(columns)]
        for start in range(2)
        for side in range(2)
    ]
    run = math.gcd(dp_count, 4)
    runs = [[start + step for step in range(run)] for start in range(0, dp_count, run)]
    strides = [[start + step for step in range(0, dp_count, run)] for start in range(run)]
    swap = [(source, source ^ 1) for source in range(seq_count)]
    cross = [(source, (source + half_count) % seq_count) for source in range(seq_count)]
    beside = [(source, source ^ 2) for source in range(seq_count)]

    def swapped(value):
        return lax.ppermute(value, "seq", swap)

    def crossed(value):
        return lax.ppermute(value, "seq", cross)

    def moved(value, steps):
        pairs = []
        for group in range(dp_count):
            for member in range(seq_count):
                high = member // half_count
                place_y = (high * run + group % run + steps) % (2 * run)
                target_group = group // run * run + place_y % run
                target = place_y // run * half_count + member % half_count
                pairs.append((group * seq_count + member, target_group * seq_count + target))
        return lax.ppermute(value, ("dp", "seq"), pairs)

    def passed(value):
        return lax.ppermute(value, "seq", beside)

    def exchanged(value, axis, groups=None):
        return lax.all_to_all(value, axis, 0, 0, axis_index_groups=groups)

    x_rows = hidden_in[0]
    places = block_pos[0]
    index = self_index.reshape(1).astype(jnp.int32)
    smem = pl.BlockSpec(memory_space=pltpu.SMEM)

    with jax.named_scope("rotation"):
        pair_places = lax.dynamic_slice_in_dim(places, self_index - core_index, 2)
        pair_pos = pair_places[:, None] * BLOCK + jnp.arange(tokens, dtype=jnp.int32)[None, :]
        freq = frequencies(HD)
        angles = pair_pos.astype(jnp.float32)[:, :, None] * np.concatenate([freq, freq])
        cosine = jnp.cos(angles)
        sine_part = jnp.sin(angles)
        plan = pl.pallas_call(
            plan_kernel,
            out_shape=jax.ShapeDtypeStruct((2 * half_count + 4,), jnp.int32),
            in_specs=[smem, smem],
            out_specs=smem,
            scratch_shapes=[pltpu.SMEM((seq_count,), jnp.int32)],
            name="block_plan",
        )(index, places)
        x_far = swapped(x_rows)
        own_half, given_half = turned_halves(parity, x_rows, 2, "own_halves")
        next_half = passed(given_half)
        (far_half,) = turned_halves(parity, x_far, 1, "far_half")
    with jax.named_scope("weight_gather"):
        copies = local_call(
            copies_kernel,
            jax.ShapeDtypeStruct((run, kv_weight.shape[0], HD), kv_weight.dtype),
            (core,),
            (kv_weight,),
            "weight_copies",
        )
        run_weight = exchanged(copies, "dp", runs)
        run_weight, q_start, g_start, own_bits = lax.optimization_barrier(
            (run_weight, queries[0], out_grad[0], precision.reshape(2))
        )
        far_bits = swapped(own_bits)
        q_middle, g_middle = moved(q_start, run // 2), moved(g_start, -(run // 2))
        copies = jnp.broadcast_to(run_weight[None], (dp_count // run, *run_weight.shape))
        copies = lax.optimization_barrier(copies)
        near_weight = exchanged(copies, "dp", strides).reshape(width, HD)
        (
            near_weight, q_middle, g_middle, plan, cosine, sine_part, far_bits, x_far, own_half,
            next_half, far_half,
        ) = lax.optimization_barrier(
            (
                near_weight, q_middle, g_middle, plan, cosine, sine_part, far_bits, x_far,
                own_half, next_half, far_half,
            )
        )
    with jax.named_scope("projection"):
        stacked = local_call(
            project_kernel,
            jax.ShapeDtypeStruct((columns, 2, tokens, HD), jnp.bfloat16),
            (core, own_bits, far_bits),
            (x_rows, x_far, near_weight, cosine, sine_part),
            "projection",
        )
    with jax.named_scope("kv_gather"):
        stacked, late_weight, late_half = lax.optimization_barrier(
            (stacked, near_weight, next_half)
        )
        near = exchanged(stacked, "seq", column_groups).reshape(half_count, tokens, HD)
        next_far_half = swapped(late_half)
        far_weight = swapped(late_weight)
        q_cross, g_cross = moved(q_middle, run // 2), moved(g_middle, -(run // 2))
        columns_shape = jax.ShapeDtypeStruct((HD, QH * tokens), jnp.bfloat16)
        rows_shape = jax.ShapeDtypeStruct((QH * tokens, HD), jnp.bfloat16)
        query_shapes = (columns_shape, columns_shape, rows_shape, rows_shape)
        own_forms = local_call(
            query_kernel, query_shapes, (), (queries[0], out_grad[0]), "own_query_forms"
        )
        cross_forms = local_call(
            query_kernel, query_shapes, (), (q_cross, g_cross), "cross_query_forms"
        )
        near, own_forms, cross_forms, next_far_half, far_weight = lax.optimization_barrier(
            (near, own_forms, cross_forms, next_far_half, far_weight)
        )
        far = swapped(near)
    with jax.named_scope("attention"):
        totals = local_call(
            totals_kernel,
            jax.ShapeDtypeStruct((2, 3, QH * tokens), jnp.float32),
            (plan, core),
            (near, far, *own_forms[:2], *cross_forms[:2]),
            "attention_totals",
            (),
            48,
        )
        sum_tiles = (half_count // TILE_BLOCKS, TILE_BLOCKS * BLOCK, HD)
        dq_own, dq_sent, near_grad, far_grad = local_call(
            grads_kernel,
            (
                jax.ShapeDtypeStruct((tokens, QH * HD), jnp.float32),
                jax.ShapeDtypeStruct((tokens, QH * HD), jnp.bfloat16),
                jax.ShapeDtypeStruct(near.shape, jnp.bfloat16),
                jax.ShapeDtypeStruct(near.shape, jnp.bfloat16),
            ),
            (plan, core),
            (near, far, totals, crossed(totals), *own_forms, *cross_forms),
            "attention_grads",
            (
                pltpu.VMEM(sum_tiles, jnp.float32),
                pltpu.VMEM(sum_tiles, jnp.float32),
                pltpu.VMEM((HD, QH * tokens), jnp.float32),
            ),
            48,
        )
    with jax.named_scope("kv_reduce"):
        pair = near_grad.astype(jnp.float32) + swapped(far_grad).astype(jnp.float32)
        pair = pair.astype(jnp.bfloat16).reshape(columns, 2, tokens, HD)
        arrived = exchanged(pair, "seq", column_groups)
        arrived, dq_middle = lax.optimization_barrier((arrived, moved(dq_sent, run // 2)))
    with jax.named_scope("query_grad"):
        dq_back = moved(dq_middle, run // 2)
        query_grad = (dq_own + dq_back.astype(jnp.float32)).astype(jnp.bfloat16)
    with jax.named_scope("projection_grad"):
        settled = local_call(
            settle_kernel,
            jax.ShapeDtypeStruct((1, 2, tokens, HD), jnp.bfloat16),
            (core,),
            (arrived, cosine, sine_part),
            "projection_grad",
        )
    with jax.named_scope("weight_grad"):
        piece = BLOCK // quads
        share = local_call(
            share_kernel,
            jax.ShapeDtypeStruct((quads, dp_count, piece, HD), jnp.bfloat16),
            (core,),
            (own_half, far_half, next_half, next_far_half, settled[0], passed(settled[0])),
            "weight_share",
        )
        quad_parts = exchanged(share, "seq", quad_groups)
        (quad_share,) = local_call(
            total_kernel,
            (jax.ShapeDtypeStruct((1, dp_count, piece, HD), jnp.bfloat16),),
            (),
            (quad_parts,),
            "quad_share",
        )
        share_parts = exchanged(quad_share[0], "dp")
        group_share = local_call(
            total_kernel,
            jax.ShapeDtypeStruct((seq_count, piece, HD), jnp.bfloat16),
            (),
            (share_parts,),
            "group_share",
        )
        gathered = exchanged(group_share, "seq")
        weight_grad = local_call(
            functools.partial(assemble_kernel, grad_scale),
            jax.ShapeDtypeStruct((width // dp_count, 2 * HD), jnp.float32),
            (),
            (gathered.reshape(2, quads, 2, 2, piece, HD),),
            "weight_grad",
        )
    with jax.named_scope("input_grad"):
        both = settled[0]
        own = jnp.where(is_first, both[0], both[1])
        other = swapped(jnp.where(is_first, both[1], both[0]))
        proj_grad = jnp.concatenate(
            [jnp.where(is_first, own, other), jnp.where(is_first, other, own)], axis=1
        )
        input_grad = (dot_cols(own, near_weight) + dot_cols(other, far_weight)).astype(
            jnp.bfloat16
        )
    return (query_grad[None], proj_grad[None], input_grad[None], weight_grad)


def solution(mesh):
    in_specs = (
        P("dp", "seq", None),
        P("dp", "seq", None),
        P("dp", "seq", None),
        P("dp", None),
        P("dp", None),
        P("dp", "seq", None),
    )
    out_specs = (P("dp", "seq", None), P("dp", "seq", None), P("dp", "seq", None), P("dp", None))
    return jax.shard_map(body, mesh=mesh, in_specs=in_specs, out_specs=out_specs, check_vma=False)
```

```python
import functools
import math

import jax
import jax.numpy as jnp
import numpy as np
from jax import lax
from jax.experimental import pallas as pl
from jax.experimental.pallas import tpu as pltpu
from jax.sharding import PartitionSpec as P

QH = 8
HD = 128
BLOCK = 128
TILE_BLOCKS = 4

EPSILON = 1e-06
LOG2E = math.log2(math.e)


def frequencies(size):
    expo = np.arange(0, size, 2).astype(np.float32) / np.float32(size)
    base = np.float32(1.0) / np.power(np.float32(500000.0), expo)
    wavelen = np.float32(2.0 * math.pi) / base
    mixing = (np.float32(8192.0) / wavelen - np.float32(1.0)) / np.float32(3.0)
    blended = (1.0 - mixing) * base / 8.0 + mixing * base
    slow = np.where(wavelen > 8192.0, base / 8.0, blended)
    return np.where(wavelen < 2048.0, base, slow).astype(np.float32)


def softstep(scaled):
    return scaled - jnp.sin(2.0 * math.pi * (scaled - jnp.round(scaled))) / (2.0 * math.pi)


def dot_cols(left, right):
    return lax.dot_general(
        left, right, (((1,), (1,)), ((), ())), preferred_element_type=jnp.float32
    )


def dot(left, right):
    return jnp.dot(left, right, preferred_element_type=jnp.float32)


def plan_kernel(index_ref, places_ref, plan_ref, slot_at):
    blocks = slot_at.shape[0]
    half = blocks // 2
    me = index_ref[0]
    start = lax.div(me, half) * half
    for place in range(blocks):
        slot_at[place] = -1
    for slot in range(half):
        slot_at[places_ref[start + slot]] = slot
    own = places_ref[me]
    cross = places_ref[lax.rem(me + half, blocks)]

    def visit(place, counts):
        rank, below_own, below_cross = counts
        slot = slot_at[place]
        found = slot >= 0

        @pl.when(found)
        def _():
            plan_ref[rank] = slot
            plan_ref[half + rank] = place

        one = jnp.where(found, 1, 0)
        return (
            rank + one,
            below_own + jnp.where(place < own, one, 0),
            below_cross + jnp.where(place < cross, one, 0),
        )

    _, below_own, below_cross = lax.fori_loop(0, blocks, visit, (0, 0, 0))
    plan_ref[2 * half] = own
    plan_ref[2 * half + 1] = cross
    plan_ref[2 * half + 2] = below_own
    plan_ref[2 * half + 3] = below_cross


def tile_of(plan_ref, core_ref, near_ref, far_ref, tile):
    slots = [plan_ref[tile * TILE_BLOCKS + step] for step in range(TILE_BLOCKS)]
    near = jnp.concatenate([near_ref[slot] for slot in slots], axis=0)
    far = jnp.concatenate([far_ref[slot] for slot in slots], axis=0)
    is_first = core_ref[0] == 0
    return jnp.where(is_first, near, far), jnp.where(is_first, far, near)


def tile_counts(plan_ref, blocks, group):
    below = plan_ref[2 * blocks + 2 + group]
    seen = below + 1 - group
    return lax.div(below, TILE_BLOCKS), lax.div(seen + TILE_BLOCKS - 1, TILE_BLOCKS)


def visible_in(plan_ref, blocks, group, tile, rows):
    offsets = lax.broadcasted_iota(jnp.int32, (BLOCK, 1), 0)
    key_at = jnp.concatenate(
        [
            plan_ref[blocks + tile * TILE_BLOCKS + step] * BLOCK + offsets
            for step in range(TILE_BLOCKS)
        ],
        axis=0,
    )
    token = lax.rem(lax.broadcasted_iota(jnp.int32, (1, rows), 1), BLOCK)
    return key_at <= plan_ref[2 * blocks + group] * BLOCK + token


SCORE_SCALE = LOG2E / math.sqrt(HD)


def totals_kernel(plan_ref, core_ref, near_ref, far_ref, *rest):
    query_refs, out_ref = rest[:-1], rest[-1]
    blocks = near_ref.shape[0]
    rows = QH * BLOCK
    span = TILE_BLOCKS * BLOCK

    def folded(values):
        return jnp.sum(values.reshape(span // 8, 8, rows), axis=0)

    for group in range(2):
        q_cols, g_cols = query_refs[2 * group], query_refs[2 * group + 1]

        def step(tile, sums, masked, q_cols=q_cols, g_cols=g_cols, group=group):
            total, weighted, top = sums
            keys, values = tile_of(plan_ref, core_ref, near_ref, far_ref, tile)
            scores = dot(keys, q_cols[...]) * SCORE_SCALE
            if masked:
                visible = visible_in(plan_ref, blocks, group, tile, rows)
                scores = jnp.where(visible, scores, -jnp.inf)
            highest = jnp.maximum(top, jnp.max(scores, axis=0, keepdims=True))
            shrink = jnp.exp2(top - highest)
            exponent = jnp.exp2(scores - highest)
            prob_grad = dot(values, g_cols[...])
            total = total * shrink + folded(exponent)
            weighted = weighted * shrink + folded(exponent * prob_grad)
            return (total, weighted, highest)

        full, tiles = tile_counts(plan_ref, blocks, group)
        empty = jnp.zeros((8, rows), jnp.float32)
        sums = (empty, empty, jnp.full((1, rows), -1e30, jnp.float32))
        sums = lax.fori_loop(0, full, functools.partial(step, masked=False), sums)
        total, weighted, top = lax.fori_loop(
            full, tiles, functools.partial(step, masked=True), sums
        )
        out_ref[group, 0:1, :] = top
        out_ref[group, 1:2, :] = jnp.sum(total, axis=0, keepdims=True)
        out_ref[group, 2:3, :] = jnp.sum(weighted, axis=0, keepdims=True)


def grads_kernel(plan_ref, core_ref, near_ref, far_ref, own_ref, other_ref, *rest):
    query_refs, (dq_ref, dq_sent_ref, near_grad_ref, far_grad_ref) = rest[:8], rest[8:12]
    key_sums, value_sums, dq_cols = rest[12:]
    blocks = near_ref.shape[0]
    rows = QH * BLOCK
    is_first = core_ref[0] == 0
    key_sums[...] = jnp.zeros_like(key_sums)
    value_sums[...] = jnp.zeros_like(value_sums)

    for group, out_ref in enumerate((dq_ref, dq_sent_ref)):
        q_cols, g_cols, q_rows, g_rows = query_refs[4 * group : 4 * group + 4]
        here, there = own_ref[group], other_ref[1 - group]
        top = jnp.maximum(here[0:1], there[0:1])
        here_part, there_part = jnp.exp2(here[0:1] - top), jnp.exp2(there[0:1] - top)
        total = here[1:2] * here_part + there[1:2] * there_part
        row_delta = (here[2:3] * here_part + there[2:3] * there_part) / total
        log_total = top + jnp.log(total) * LOG2E
        dq_cols[...] = jnp.zeros_like(dq_cols)

        def step(
            tile, carry, masked, group=group, q_cols=q_cols, g_cols=g_cols, q_rows=q_rows,
            g_rows=g_rows, row_delta=row_delta, log_total=log_total,
        ):
            keys, values = tile_of(plan_ref, core_ref, near_ref, far_ref, tile)
            probs = jnp.exp2(dot(keys, q_cols[...]) * SCORE_SCALE - log_total)
            if masked:
                probs = jnp.where(visible_in(plan_ref, blocks, group, tile, rows), probs, 0.0)
            prob_grad = dot(values, g_cols[...])
            score_grad = (probs * (prob_grad - row_delta)).astype(jnp.bfloat16)
            value_sums[tile] += dot(probs.astype(jnp.bfloat16), g_rows[...])
            key_sums[tile] += dot(score_grad, q_rows[...])
            dq_cols[...] += dot(keys.T, score_grad)
            return carry

        full, tiles = tile_counts(plan_ref, blocks, group)
        lax.fori_loop(0, full, functools.partial(step, masked=False), 0)
        lax.fori_loop(full, tiles, functools.partial(step, masked=True), 0)
        for head in range(QH):
            part = pl.ds(head * HD, HD)
            out_ref[:, part] = (dq_cols[:, part].T * (1.0 / math.sqrt(HD))).astype(out_ref.dtype)

    @pl.loop(0, blocks // TILE_BLOCKS)
    def _(tile):
        key_grad = key_sums[tile].astype(jnp.bfloat16)
        value_grad = value_sums[tile].astype(jnp.bfloat16)
        near_grad = jnp.where(is_first, key_grad, value_grad)
        far_grad = jnp.where(is_first, value_grad, key_grad)
        for step in range(TILE_BLOCKS):
            slot = plan_ref[tile * TILE_BLOCKS + step]
            near_grad_ref[slot] = near_grad[step * BLOCK : (step + 1) * BLOCK]
            far_grad_ref[slot] = far_grad[step * BLOCK : (step + 1) * BLOCK]


def copies_kernel(core_ref, weight_ref, out_ref):
    start = pl.multiple_of(core_ref[0] * HD, HD)
    half = weight_ref[:, pl.ds(start, HD)]
    for copy in range(out_ref.shape[0]):
        out_ref[copy] = half


def query_kernel(q_ref, g_ref, q_cols, g_cols, q_rows, g_rows):
    for head in range(QH):
        part = pl.ds(head * HD, HD)
        q_cols[:, part] = q_ref[:, part].T
        g_cols[:, part] = g_ref[:, part].T
        q_rows[part, :] = q_ref[:, part]
        g_rows[part, :] = g_ref[:, part]


def local_call(kernel, shapes, scalars, arrays, name, scratch=(), limit=32):
    smem = pl.BlockSpec(memory_space=pltpu.SMEM)
    vmem = pl.BlockSpec(memory_space=pltpu.VMEM)
    return pl.pallas_call(
        kernel,
        out_shape=shapes,
        in_specs=[smem] * len(scalars) + [vmem] * len(arrays),
        out_specs=jax.tree.map(lambda _: vmem, shapes),
        scratch_shapes=scratch,
        compiler_params=pltpu.CompilerParams(vmem_limit_bytes=limit * 1024 * 1024),
        name=name,
    )(*scalars, *arrays)


def turning(core_ref, cos_ref, sin_ref, at):
    is_first = core_ref[0] == 0
    first_half = lax.broadcasted_iota(jnp.int32, (1, HD), 1) < HD // 2
    sine_part = jnp.where(first_half, -sin_ref[at], sin_ref[at])
    return jnp.where(is_first, cos_ref[at], 1.0), jnp.where(is_first, sine_part, 0.0)


def project_kernel(
    core_ref, own_bits_ref, far_bits_ref, own_ref, far_ref, weight_ref, cos_ref, sin_ref, out_ref
):
    core = core_ref[0]
    weight = weight_ref[...]
    for x_ref, bits_ref, at in ((own_ref, own_bits_ref, core), (far_ref, far_bits_ref, 1 - core)):
        raw = dot(x_ref[...], weight)
        cosine, sine_part = turning(core_ref, cos_ref, sin_ref, at)
        turned = raw * cosine + pltpu.roll(raw, HD // 2, 1) * sine_part
        largest = jnp.max(jnp.abs(turned), axis=0, keepdims=True)
        levels = (lax.shift_left(jnp.int32(1), bits_ref[core] - 1) - 1).astype(jnp.float32)
        level_step = (largest + EPSILON) / levels
        quantized = (level_step * softstep(turned / level_step)).astype(jnp.bfloat16)
        for copy in range(out_ref.shape[0]):
            out_ref[copy, at] = quantized


def settle_kernel(core_ref, arrived_ref, cos_ref, sin_ref, out_ref):
    scale = jnp.where(core_ref[0] == 0, 1.0 / math.sqrt(HD), 1.0)
    for at in range(2):
        grads = arrived_ref[0, at].astype(jnp.float32)
        for source in range(1, arrived_ref.shape[0]):
            grads += arrived_ref[source, at].astype(jnp.float32)
        cosine, sine_part = turning(core_ref, cos_ref, sin_ref, at)
        grads = grads * scale
        turned = grads * cosine - pltpu.roll(grads, HD // 2, 1) * sine_part
        out_ref[0, at] = turned.astype(jnp.bfloat16)


def turn_kernel(parity_ref, x_ref, keep_ref, *rest):
    parity = parity_ref[0]
    for group in range(keep_ref.shape[0] // BLOCK):
        rows = slice(group * BLOCK, (group + 1) * BLOCK)
        for out_ref, half in zip((keep_ref, *rest), (parity, 1 - parity)):
            start = pl.multiple_of((2 * group + half) * BLOCK, BLOCK)
            out_ref[rows, :] = x_ref[:, pl.ds(start, BLOCK)].T


def turned_halves(parity, x_rows, count, name):
    tokens, width = x_rows.shape
    shape = jax.ShapeDtypeStruct((width // 2, tokens), x_rows.dtype)
    return local_call(turn_kernel, (shape,) * count, (parity,), (x_rows,), name)


def share_kernel(core_ref, *rest):
    core = core_ref[0]
    own_ref, own_far_ref, next_ref, next_far_ref, grads_ref, next_grads_ref, out_ref = rest
    quads, groups, piece, _ = out_ref.shape
    own = jnp.concatenate([grads_ref[core], grads_ref[1 - core]], axis=0)
    beside = jnp.concatenate([next_grads_ref[core], next_grads_ref[1 - core]], axis=0)
    for group in range(groups):
        rows = slice(group * BLOCK, (group + 1) * BLOCK)
        share = dot(jnp.concatenate([own_ref[rows, :], own_far_ref[rows, :]], axis=1), own)
        share += dot(jnp.concatenate([next_ref[rows, :], next_far_ref[rows, :]], axis=1), beside)
        share = share.astype(out_ref.dtype)
        for quad in range(quads):
            out_ref[quad, group] = share[quad * piece : (quad + 1) * piece]


def total_kernel(parts_ref, out_ref):
    total = parts_ref[0].astype(jnp.float32)
    for source in range(1, parts_ref.shape[0]):
        total += parts_ref[source].astype(jnp.float32)
    total = total.astype(out_ref.dtype)
    for copy in range(out_ref.shape[0]):
        out_ref[copy] = total


def assemble_kernel(grad_scale, parts_ref, out_ref):
    _, quads, _, _, piece, _ = parts_ref.shape
    for quad in range(quads):
        for parity in range(2):
            for core in range(2):
                low = parts_ref[0, quad, parity, core].astype(jnp.float32)
                high = parts_ref[1, quad, parity, core].astype(jnp.float32)
                row = parity * BLOCK + quad * piece
                out_ref[row : row + piece, core * HD : (core + 1) * HD] = (
                    low + high
                ) * grad_scale


def body(hidden_in, queries, out_grad, kv_weight, block_pos, precision):
    tokens = hidden_in.shape[1]
    width = hidden_in.shape[2]
    seq_count = lax.axis_size("seq")
    dp_count = lax.axis_size("dp")
    half_count = seq_count // 2
    columns = half_count // 2
    grad_scale = 1.0 / math.sqrt(dp_count * seq_count * tokens)
    self_index = lax.axis_index("seq")
    core_index = lax.rem(self_index, 2)
    core = core_index.reshape(1).astype(jnp.int32)
    is_first = core_index == 0
    quads = columns // 2
    parity = lax.rem(lax.div(self_index, 2), 2).reshape(1).astype(jnp.int32)
    quad_groups = [
        [start * half_count + 4 * quad + side for quad in range(quads)]
        for start in range(2)
        for side in range(4)
    ]
    column_groups = [
        [start * half_count + 2 * column + side for column in range(columns)]
        for start in range(2)
        for side in range(2)
    ]
    run = math.gcd(dp_count, 4)
    runs = [[start + step for step in range(run)] for start in range(0, dp_count, run)]
    strides = [[start + step for step in range(0, dp_count, run)] for start in range(run)]
    swap = [(source, source ^ 1) for source in range(seq_count)]
    cross = [(source, (source + half_count) % seq_count) for source in range(seq_count)]
    beside = [(source, source ^ 2) for source in range(seq_count)]

    def swapped(value):
        return lax.ppermute(value, "seq", swap)

    def crossed(value):
        return lax.ppermute(value, "seq", cross)

    def moved(value, steps):
        pairs = []
        for group in range(dp_count):
            for member in range(seq_count):
                high = member // half_count
                place_y = (high * run + group % run + steps) % (2 * run)
                target_group = group // run * run + place_y % run
                target = place_y // run * half_count + member % half_count
                pairs.append((group * seq_count + member, target_group * seq_count + target))
        return lax.ppermute(value, ("dp", "seq"), pairs)

    def passed(value):
        return lax.ppermute(value, "seq", beside)

    def exchanged(value, axis, groups=None):
        return lax.all_to_all(value, axis, 0, 0, axis_index_groups=groups)

    x_rows = hidden_in[0]
    places = block_pos[0]
    index = self_index.reshape(1).astype(jnp.int32)
    smem = pl.BlockSpec(memory_space=pltpu.SMEM)

    with jax.named_scope("rotation"):
        pair_places = lax.dynamic_slice_in_dim(places, self_index - core_index, 2)
        pair_pos = pair_places[:, None] * BLOCK + jnp.arange(tokens, dtype=jnp.int32)[None, :]
        freq = frequencies(HD)
        angles = pair_pos.astype(jnp.float32)[:, :, None] * np.concatenate([freq, freq])
        cosine = jnp.cos(angles)
        sine_part = jnp.sin(angles)
        plan = pl.pallas_call(
            plan_kernel,
            out_shape=jax.ShapeDtypeStruct((2 * half_count + 4,), jnp.int32),
            in_specs=[smem, smem],
            out_specs=smem,
            scratch_shapes=[pltpu.SMEM((seq_count,), jnp.int32)],
            name="block_plan",
        )(index, places)
        x_far = swapped(x_rows)
    with jax.named_scope("weight_gather"):
        copies = local_call(
            copies_kernel,
            jax.ShapeDtypeStruct((run, kv_weight.shape[0], HD), kv_weight.dtype),
            (core,),
            (kv_weight,),
            "weight_copies",
        )
        run_weight = exchanged(copies, "dp", runs)
        run_weight, q_start, g_start, own_bits = lax.optimization_barrier(
            (run_weight, queries[0], out_grad[0], precision.reshape(2))
        )
        far_bits = swapped(own_bits)
        q_middle, g_middle = moved(q_start, run // 2), moved(g_start, -(run // 2))
        copies = jnp.broadcast_to(run_weight[None], (dp_count // run, *run_weight.shape))
        copies = lax.optimization_barrier(copies)
        near_weight = exchanged(copies, "dp", strides).reshape(width, HD)
        near_weight, q_middle, g_middle, plan, cosine, sine_part, far_bits, x_far = (
            lax.optimization_barrier(
                (near_weight, q_middle, g_middle, plan, cosine, sine_part, far_bits, x_far)
            )
        )
    with jax.named_scope("projection"):
        stacked = local_call(
            project_kernel,
            jax.ShapeDtypeStruct((columns, 2, tokens, HD), jnp.bfloat16),
            (core, own_bits, far_bits),
            (x_rows, x_far, near_weight, cosine, sine_part),
            "projection",
        )
    with jax.named_scope("kv_gather"):
        stacked, x_late, x_far_late, late_weight = lax.optimization_barrier(
            (stacked, x_rows, x_far, near_weight)
        )
        far_weight = swapped(late_weight)
        near = exchanged(stacked, "seq", column_groups).reshape(half_count, tokens, HD)
        own_half, given_half = turned_halves(parity, x_late, 2, "own_halves")
        (far_half,) = turned_halves(parity, x_far_late, 1, "far_half")
        q_cross, g_cross = moved(q_middle, run // 2), moved(g_middle, -(run // 2))
        columns_shape = jax.ShapeDtypeStruct((HD, QH * tokens), jnp.bfloat16)
        rows_shape = jax.ShapeDtypeStruct((QH * tokens, HD), jnp.bfloat16)
        query_shapes = (columns_shape, columns_shape, rows_shape, rows_shape)
        own_forms = local_call(
            query_kernel, query_shapes, (), (queries[0], out_grad[0]), "own_query_forms"
        )
        cross_forms = local_call(
            query_kernel, query_shapes, (), (q_cross, g_cross), "cross_query_forms"
        )
        near, own_forms, cross_forms, own_half, given_half, far_half, far_weight = (
            lax.optimization_barrier(
                (near, own_forms, cross_forms, own_half, given_half, far_half, far_weight)
            )
        )
        far = swapped(near)
    with jax.named_scope("attention"):
        totals = local_call(
            totals_kernel,
            jax.ShapeDtypeStruct((2, 3, QH * tokens), jnp.float32),
            (plan, core),
            (near, far, *own_forms[:2], *cross_forms[:2]),
            "attention_totals",
            (),
            48,
        )
        totals, given_half = lax.optimization_barrier((totals, given_half))
        other_totals = crossed(totals)
        next_half = passed(given_half)
        sum_tiles = (half_count // TILE_BLOCKS, TILE_BLOCKS * BLOCK, HD)
        dq_own, dq_sent, near_grad, far_grad = local_call(
            grads_kernel,
            (
                jax.ShapeDtypeStruct((tokens, QH * HD), jnp.float32),
                jax.ShapeDtypeStruct((tokens, QH * HD), jnp.bfloat16),
                jax.ShapeDtypeStruct(near.shape, jnp.bfloat16),
                jax.ShapeDtypeStruct(near.shape, jnp.bfloat16),
            ),
            (plan, core),
            (near, far, totals, other_totals, *own_forms, *cross_forms),
            "attention_grads",
            (
                pltpu.VMEM(sum_tiles, jnp.float32),
                pltpu.VMEM(sum_tiles, jnp.float32),
                pltpu.VMEM((HD, QH * tokens), jnp.float32),
            ),
            48,
        )
    with jax.named_scope("kv_reduce"):
        near_grad, far_grad, next_half = lax.optimization_barrier(
            (near_grad, far_grad, next_half)
        )
        pair = near_grad.astype(jnp.float32) + swapped(far_grad).astype(jnp.float32)
        pair = pair.astype(jnp.bfloat16).reshape(columns, 2, tokens, HD)
        pair, next_half, dq_sent = lax.optimization_barrier((pair, next_half, dq_sent))
        arrived = exchanged(pair, "seq", column_groups)
        next_far_half = swapped(next_half)
        dq_middle = moved(dq_sent, run // 2)
    with jax.named_scope("projection_grad"):
        settled = local_call(
            settle_kernel,
            jax.ShapeDtypeStruct((1, 2, tokens, HD), jnp.bfloat16),
            (core,),
            (arrived, cosine, sine_part),
            "projection_grad",
        )
    with jax.named_scope("weight_grad"):
        next_grads, next_far_half, dq_middle = lax.optimization_barrier(
            (passed(settled[0]), next_far_half, dq_middle)
        )
        piece = BLOCK // quads
        share = local_call(
            share_kernel,
            jax.ShapeDtypeStruct((quads, dp_count, piece, HD), jnp.bfloat16),
            (core,),
            (own_half, far_half, next_half, next_far_half, settled[0], next_grads),
            "weight_share",
        )
        quad_parts = exchanged(share, "seq", quad_groups)
        dq_back = moved(dq_middle, run // 2)
        quad_parts, dq_back = lax.optimization_barrier((quad_parts, dq_back))
        (quad_share,) = local_call(
            total_kernel,
            (jax.ShapeDtypeStruct((1, dp_count, piece, HD), jnp.bfloat16),),
            (),
            (quad_parts,),
            "quad_share",
        )
        share_parts = exchanged(quad_share[0], "dp")
        group_share = local_call(
            total_kernel,
            jax.ShapeDtypeStruct((seq_count, piece, HD), jnp.bfloat16),
            (),
            (share_parts,),
            "group_share",
        )
        gathered = exchanged(group_share, "seq")
        weight_grad = local_call(
            functools.partial(assemble_kernel, grad_scale),
            jax.ShapeDtypeStruct((width // dp_count, 2 * HD), jnp.float32),
            (),
            (gathered.reshape(2, quads, 2, 2, piece, HD),),
            "weight_grad",
        )
    with jax.named_scope("query_grad"):
        query_grad = (dq_own + dq_back.astype(jnp.float32)).astype(jnp.bfloat16)
    with jax.named_scope("input_grad"):
        both = settled[0]
        own = jnp.where(is_first, both[0], both[1])
        other = swapped(jnp.where(is_first, both[1], both[0]))
        proj_grad = jnp.concatenate(
            [jnp.where(is_first, own, other), jnp.where(is_first, other, own)], axis=1
        )
        input_grad = (dot_cols(own, near_weight) + dot_cols(other, far_weight)).astype(
            jnp.bfloat16
        )
    return (query_grad[None], proj_grad[None], input_grad[None], weight_grad)


def solution(mesh):
    in_specs = (
        P("dp", "seq", None),
        P("dp", "seq", None),
        P("dp", "seq", None),
        P("dp", None),
        P("dp", None),
        P("dp", "seq", None),
    )
    out_specs = (P("dp", "seq", None), P("dp", "seq", None), P("dp", "seq", None), P("dp", None))
    return jax.shard_map(body, mesh=mesh, in_specs=in_specs, out_specs=out_specs, check_vma=False)
```

```python
import functools
import math

import jax
import jax.numpy as jnp
import numpy as np
from jax import lax
from jax.experimental import pallas as pl
from jax.experimental.pallas import tpu as pltpu
from jax.sharding import PartitionSpec as P

QH = 8
HD = 128
BLOCK = 128
TILE_BLOCKS = 4

EPSILON = 1e-06
LOG2E = math.log2(math.e)


def frequencies(size):
    expo = np.arange(0, size, 2).astype(np.float32) / np.float32(size)
    base = np.float32(1.0) / np.power(np.float32(500000.0), expo)
    wavelen = np.float32(2.0 * math.pi) / base
    mixing = (np.float32(8192.0) / wavelen - np.float32(1.0)) / np.float32(3.0)
    blended = (1.0 - mixing) * base / 8.0 + mixing * base
    slow = np.where(wavelen > 8192.0, base / 8.0, blended)
    return np.where(wavelen < 2048.0, base, slow).astype(np.float32)


def softstep(scaled):
    return scaled - jnp.sin(2.0 * math.pi * (scaled - jnp.round(scaled))) / (2.0 * math.pi)


def dot_cols(left, right):
    return lax.dot_general(
        left, right, (((1,), (1,)), ((), ())), preferred_element_type=jnp.float32
    )


def dot(left, right):
    return jnp.dot(left, right, preferred_element_type=jnp.float32)


def plan_kernel(index_ref, places_ref, plan_ref, slot_at):
    blocks = slot_at.shape[0]
    half = blocks // 2
    me = index_ref[0]
    start = lax.div(me, half) * half
    for place in range(blocks):
        slot_at[place] = -1
    for slot in range(half):
        slot_at[places_ref[start + slot]] = slot
    own = places_ref[me]
    cross = places_ref[lax.rem(me + half, blocks)]

    def visit(place, counts):
        rank, below_own, below_cross = counts
        slot = slot_at[place]
        found = slot >= 0

        @pl.when(found)
        def _():
            plan_ref[rank] = slot
            plan_ref[half + rank] = place

        one = jnp.where(found, 1, 0)
        return (
            rank + one,
            below_own + jnp.where(place < own, one, 0),
            below_cross + jnp.where(place < cross, one, 0),
        )

    _, below_own, below_cross = lax.fori_loop(0, blocks, visit, (0, 0, 0))
    plan_ref[2 * half] = own
    plan_ref[2 * half + 1] = cross
    plan_ref[2 * half + 2] = below_own
    plan_ref[2 * half + 3] = below_cross


def tile_of(plan_ref, core_ref, near_ref, far_ref, tile):
    slots = [plan_ref[tile * TILE_BLOCKS + step] for step in range(TILE_BLOCKS)]
    near = jnp.concatenate([near_ref[slot] for slot in slots], axis=0)
    far = jnp.concatenate([far_ref[slot] for slot in slots], axis=0)
    is_first = core_ref[0] == 0
    return jnp.where(is_first, near, far), jnp.where(is_first, far, near)


def tile_counts(plan_ref, blocks, group):
    below = plan_ref[2 * blocks + 2 + group]
    seen = below + 1 - group
    return lax.div(below, TILE_BLOCKS), lax.div(seen + TILE_BLOCKS - 1, TILE_BLOCKS)


def visible_in(plan_ref, blocks, group, tile, rows):
    offsets = lax.broadcasted_iota(jnp.int32, (BLOCK, 1), 0)
    key_at = jnp.concatenate(
        [
            plan_ref[blocks + tile * TILE_BLOCKS + step] * BLOCK + offsets
            for step in range(TILE_BLOCKS)
        ],
        axis=0,
    )
    token = lax.rem(lax.broadcasted_iota(jnp.int32, (1, rows), 1), BLOCK)
    return key_at <= plan_ref[2 * blocks + group] * BLOCK + token


SCORE_SCALE = LOG2E / math.sqrt(HD)


def totals_kernel(plan_ref, core_ref, near_ref, far_ref, *rest):
    query_refs, out_ref = rest[:-1], rest[-1]
    blocks = near_ref.shape[0]
    rows = QH * BLOCK
    span = TILE_BLOCKS * BLOCK

    def folded(values):
        return jnp.sum(values.reshape(span // 8, 8, rows), axis=0)

    for group in range(2):
        q_cols, g_cols = query_refs[2 * group], query_refs[2 * group + 1]

        def step(tile, sums, masked, q_cols=q_cols, g_cols=g_cols, group=group):
            total, weighted, top = sums
            keys, values = tile_of(plan_ref, core_ref, near_ref, far_ref, tile)
            scores = dot(keys, q_cols[...]) * SCORE_SCALE
            if masked:
                visible = visible_in(plan_ref, blocks, group, tile, rows)
                scores = jnp.where(visible, scores, -jnp.inf)
            highest = jnp.maximum(top, jnp.max(scores, axis=0, keepdims=True))
            shrink = jnp.exp2(top - highest)
            exponent = jnp.exp2(scores - highest)
            prob_grad = dot(values, g_cols[...])
            total = total * shrink + folded(exponent)
            weighted = weighted * shrink + folded(exponent * prob_grad)
            return (total, weighted, highest)

        full, tiles = tile_counts(plan_ref, blocks, group)
        empty = jnp.zeros((8, rows), jnp.float32)
        sums = (empty, empty, jnp.full((1, rows), -1e30, jnp.float32))
        sums = lax.fori_loop(0, full, functools.partial(step, masked=False), sums)
        total, weighted, top = lax.fori_loop(
            full, tiles, functools.partial(step, masked=True), sums
        )
        out_ref[group, 0:1, :] = top
        out_ref[group, 1:2, :] = jnp.sum(total, axis=0, keepdims=True)
        out_ref[group, 2:3, :] = jnp.sum(weighted, axis=0, keepdims=True)


def grads_kernel(plan_ref, core_ref, near_ref, far_ref, own_ref, other_ref, *rest):
    query_refs, (dq_ref, dq_sent_ref, near_grad_ref, far_grad_ref) = rest[:8], rest[8:12]
    key_sums, value_sums, dq_cols = rest[12:]
    blocks = near_ref.shape[0]
    rows = QH * BLOCK
    is_first = core_ref[0] == 0
    key_sums[...] = jnp.zeros_like(key_sums)
    value_sums[...] = jnp.zeros_like(value_sums)

    for group, out_ref in enumerate((dq_ref, dq_sent_ref)):
        q_cols, g_cols, q_rows, g_rows = query_refs[4 * group : 4 * group + 4]
        here, there = own_ref[group], other_ref[1 - group]
        top = jnp.maximum(here[0:1], there[0:1])
        here_part, there_part = jnp.exp2(here[0:1] - top), jnp.exp2(there[0:1] - top)
        total = here[1:2] * here_part + there[1:2] * there_part
        row_delta = (here[2:3] * here_part + there[2:3] * there_part) / total
        log_total = top + jnp.log(total) * LOG2E
        dq_cols[...] = jnp.zeros_like(dq_cols)

        def step(
            tile, carry, masked, group=group, q_cols=q_cols, g_cols=g_cols, q_rows=q_rows,
            g_rows=g_rows, row_delta=row_delta, log_total=log_total,
        ):
            keys, values = tile_of(plan_ref, core_ref, near_ref, far_ref, tile)
            probs = jnp.exp2(dot(keys, q_cols[...]) * SCORE_SCALE - log_total)
            if masked:
                probs = jnp.where(visible_in(plan_ref, blocks, group, tile, rows), probs, 0.0)
            prob_grad = dot(values, g_cols[...])
            score_grad = (probs * (prob_grad - row_delta)).astype(jnp.bfloat16)
            value_sums[tile] += dot(probs.astype(jnp.bfloat16), g_rows[...])
            key_sums[tile] += dot(score_grad, q_rows[...])
            dq_cols[...] += dot(keys.T, score_grad)
            return carry

        full, tiles = tile_counts(plan_ref, blocks, group)
        lax.fori_loop(0, full, functools.partial(step, masked=False), 0)
        lax.fori_loop(full, tiles, functools.partial(step, masked=True), 0)
        for head in range(QH):
            part = pl.ds(head * HD, HD)
            out_ref[:, part] = (dq_cols[:, part].T * (1.0 / math.sqrt(HD))).astype(out_ref.dtype)

    @pl.loop(0, blocks // TILE_BLOCKS)
    def _(tile):
        key_grad = key_sums[tile].astype(jnp.bfloat16)
        value_grad = value_sums[tile].astype(jnp.bfloat16)
        near_grad = jnp.where(is_first, key_grad, value_grad)
        far_grad = jnp.where(is_first, value_grad, key_grad)
        for step in range(TILE_BLOCKS):
            slot = plan_ref[tile * TILE_BLOCKS + step]
            near_grad_ref[slot] = near_grad[step * BLOCK : (step + 1) * BLOCK]
            far_grad_ref[slot] = far_grad[step * BLOCK : (step + 1) * BLOCK]


def copies_kernel(core_ref, weight_ref, out_ref):
    start = pl.multiple_of(core_ref[0] * HD, HD)
    half = weight_ref[:, pl.ds(start, HD)]
    for copy in range(out_ref.shape[0]):
        out_ref[copy] = half


def query_kernel(q_ref, g_ref, q_cols, g_cols, q_rows, g_rows):
    for head in range(QH):
        part = pl.ds(head * HD, HD)
        q_cols[:, part] = q_ref[:, part].T
        g_cols[:, part] = g_ref[:, part].T
        q_rows[part, :] = q_ref[:, part]
        g_rows[part, :] = g_ref[:, part]


def local_call(kernel, shapes, scalars, arrays, name, scratch=(), limit=32):
    smem = pl.BlockSpec(memory_space=pltpu.SMEM)
    vmem = pl.BlockSpec(memory_space=pltpu.VMEM)
    return pl.pallas_call(
        kernel,
        out_shape=shapes,
        in_specs=[smem] * len(scalars) + [vmem] * len(arrays),
        out_specs=jax.tree.map(lambda _: vmem, shapes),
        scratch_shapes=scratch,
        compiler_params=pltpu.CompilerParams(vmem_limit_bytes=limit * 1024 * 1024),
        name=name,
    )(*scalars, *arrays)


def turning(core_ref, cos_ref, sin_ref, at):
    is_first = core_ref[0] == 0
    first_half = lax.broadcasted_iota(jnp.int32, (1, HD), 1) < HD // 2
    sine_part = jnp.where(first_half, -sin_ref[at], sin_ref[at])
    return jnp.where(is_first, cos_ref[at], 1.0), jnp.where(is_first, sine_part, 0.0)


def project_kernel(
    core_ref, own_bits_ref, far_bits_ref, own_ref, far_ref, weight_ref, cos_ref, sin_ref, out_ref
):
    core = core_ref[0]
    weight = weight_ref[...]
    for x_ref, bits_ref, at in ((own_ref, own_bits_ref, core), (far_ref, far_bits_ref, 1 - core)):
        raw = dot(x_ref[...], weight)
        cosine, sine_part = turning(core_ref, cos_ref, sin_ref, at)
        turned = raw * cosine + pltpu.roll(raw, HD // 2, 1) * sine_part
        largest = jnp.max(jnp.abs(turned), axis=0, keepdims=True)
        levels = (lax.shift_left(jnp.int32(1), bits_ref[core] - 1) - 1).astype(jnp.float32)
        level_step = (largest + EPSILON) / levels
        quantized = (level_step * softstep(turned / level_step)).astype(jnp.bfloat16)
        for copy in range(out_ref.shape[0]):
            out_ref[copy, at] = quantized


def settle_kernel(core_ref, arrived_ref, cos_ref, sin_ref, out_ref):
    scale = jnp.where(core_ref[0] == 0, 1.0 / math.sqrt(HD), 1.0)
    for at in range(2):
        grads = arrived_ref[0, at].astype(jnp.float32)
        for source in range(1, arrived_ref.shape[0]):
            grads += arrived_ref[source, at].astype(jnp.float32)
        cosine, sine_part = turning(core_ref, cos_ref, sin_ref, at)
        grads = grads * scale
        turned = grads * cosine - pltpu.roll(grads, HD // 2, 1) * sine_part
        out_ref[0, at] = turned.astype(jnp.bfloat16)


def turn_kernel(parity_ref, x_ref, keep_ref, *rest):
    parity = parity_ref[0]
    for group in range(keep_ref.shape[0] // BLOCK):
        rows = slice(group * BLOCK, (group + 1) * BLOCK)
        for out_ref, half in zip((keep_ref, *rest), (parity, 1 - parity)):
            start = pl.multiple_of((2 * group + half) * BLOCK, BLOCK)
            out_ref[rows, :] = x_ref[:, pl.ds(start, BLOCK)].T


def turned_halves(parity, x_rows, count, name):
    tokens, width = x_rows.shape
    shape = jax.ShapeDtypeStruct((width // 2, tokens), x_rows.dtype)
    return local_call(turn_kernel, (shape,) * count, (parity,), (x_rows,), name)


def share_kernel(core_ref, *rest):
    core = core_ref[0]
    own_ref, own_far_ref, next_ref, next_far_ref, grads_ref, next_grads_ref, out_ref = rest
    quads, groups, piece, _ = out_ref.shape
    own = jnp.concatenate([grads_ref[core], grads_ref[1 - core]], axis=0)
    beside = jnp.concatenate([next_grads_ref[core], next_grads_ref[1 - core]], axis=0)
    for group in range(groups):
        rows = slice(group * BLOCK, (group + 1) * BLOCK)
        share = dot(jnp.concatenate([own_ref[rows, :], own_far_ref[rows, :]], axis=1), own)
        share += dot(jnp.concatenate([next_ref[rows, :], next_far_ref[rows, :]], axis=1), beside)
        share = share.astype(out_ref.dtype)
        for quad in range(quads):
            out_ref[quad, group] = share[quad * piece : (quad + 1) * piece]


def sum_kernel(here_ref, there_ref, out_ref):
    total = here_ref[...].astype(jnp.float32) + there_ref[...].astype(jnp.float32)
    for copy in range(out_ref.shape[0]):
        out_ref[copy] = total.astype(out_ref.dtype)


def total_kernel(parts_ref, out_ref):
    total = parts_ref[0].astype(jnp.float32)
    for source in range(1, parts_ref.shape[0]):
        total += parts_ref[source].astype(jnp.float32)
    total = total.astype(out_ref.dtype)
    for copy in range(out_ref.shape[0]):
        out_ref[copy] = total


def assemble_kernel(grad_scale, core_ref, near_ref, far_ref, out_ref):
    columns, piece, _ = near_ref.shape
    is_first = core_ref[0] == 0
    for column in range(columns):
        row = column % 2 * BLOCK + column // 2 * piece
        near = near_ref[column].astype(jnp.float32) * grad_scale
        far = far_ref[column].astype(jnp.float32) * grad_scale
        out_ref[row : row + piece, :HD] = jnp.where(is_first, near, far)
        out_ref[row : row + piece, HD:] = jnp.where(is_first, far, near)


def body(hidden_in, queries, out_grad, kv_weight, block_pos, precision):
    tokens = hidden_in.shape[1]
    width = hidden_in.shape[2]
    seq_count = lax.axis_size("seq")
    dp_count = lax.axis_size("dp")
    half_count = seq_count // 2
    columns = half_count // 2
    grad_scale = 1.0 / math.sqrt(dp_count * seq_count * tokens)
    self_index = lax.axis_index("seq")
    core_index = lax.rem(self_index, 2)
    core = core_index.reshape(1).astype(jnp.int32)
    is_first = core_index == 0
    quads = columns // 2
    parity = lax.rem(lax.div(self_index, 2), 2).reshape(1).astype(jnp.int32)
    quad_groups = [
        [start * half_count + 4 * quad + side for quad in range(quads)]
        for start in range(2)
        for side in range(4)
    ]
    column_groups = [
        [start * half_count + 2 * column + side for column in range(columns)]
        for start in range(2)
        for side in range(2)
    ]
    run = math.gcd(dp_count, 4)
    runs = [[start + step for step in range(run)] for start in range(0, dp_count, run)]
    strides = [[start + step for step in range(0, dp_count, run)] for start in range(run)]
    swap = [(source, source ^ 1) for source in range(seq_count)]
    cross = [(source, (source + half_count) % seq_count) for source in range(seq_count)]
    beside = [(source, source ^ 2) for source in range(seq_count)]

    def swapped(value):
        return lax.ppermute(value, "seq", swap)

    def crossed(value):
        return lax.ppermute(value, "seq", cross)

    def moved(value, steps):
        pairs = []
        for group in range(dp_count):
            for member in range(seq_count):
                high = member // half_count
                place_y = (high * run + group % run + steps) % (2 * run)
                target_group = group // run * run + place_y % run
                target = place_y // run * half_count + member % half_count
                pairs.append((group * seq_count + member, target_group * seq_count + target))
        return lax.ppermute(value, ("dp", "seq"), pairs)

    def passed(value):
        return lax.ppermute(value, "seq", beside)

    def exchanged(value, axis, groups=None):
        return lax.all_to_all(value, axis, 0, 0, axis_index_groups=groups)

    x_rows = hidden_in[0]
    places = block_pos[0]
    index = self_index.reshape(1).astype(jnp.int32)
    smem = pl.BlockSpec(memory_space=pltpu.SMEM)

    with jax.named_scope("rotation"):
        pair_places = lax.dynamic_slice_in_dim(places, self_index - core_index, 2)
        pair_pos = pair_places[:, None] * BLOCK + jnp.arange(tokens, dtype=jnp.int32)[None, :]
        freq = frequencies(HD)
        angles = pair_pos.astype(jnp.float32)[:, :, None] * np.concatenate([freq, freq])
        cosine = jnp.cos(angles)
        sine_part = jnp.sin(angles)
        plan = pl.pallas_call(
            plan_kernel,
            out_shape=jax.ShapeDtypeStruct((2 * half_count + 4,), jnp.int32),
            in_specs=[smem, smem],
            out_specs=smem,
            scratch_shapes=[pltpu.SMEM((seq_count,), jnp.int32)],
            name="block_plan",
        )(index, places)
        x_far = swapped(x_rows)
    with jax.named_scope("weight_gather"):
        copies = local_call(
            copies_kernel,
            jax.ShapeDtypeStruct((run, kv_weight.shape[0], HD), kv_weight.dtype),
            (core,),
            (kv_weight,),
            "weight_copies",
        )
        run_weight = exchanged(copies, "dp", runs)
        run_weight, q_start, g_start, own_bits = lax.optimization_barrier(
            (run_weight, queries[0], out_grad[0], precision.reshape(2))
        )
        far_bits = swapped(own_bits)
        q_middle, g_middle = moved(q_start, run // 2), moved(g_start, -(run // 2))
        copies = jnp.broadcast_to(run_weight[None], (dp_count // run, *run_weight.shape))
        copies = lax.optimization_barrier(copies)
        near_weight = exchanged(copies, "dp", strides).reshape(width, HD)
        near_weight, q_middle, g_middle, plan, cosine, sine_part, far_bits, x_far = (
            lax.optimization_barrier(
                (near_weight, q_middle, g_middle, plan, cosine, sine_part, far_bits, x_far)
            )
        )
    with jax.named_scope("projection"):
        stacked = local_call(
            project_kernel,
            jax.ShapeDtypeStruct((columns, 2, tokens, HD), jnp.bfloat16),
            (core, own_bits, far_bits),
            (x_rows, x_far, near_weight, cosine, sine_part),
            "projection",
        )
    with jax.named_scope("kv_gather"):
        stacked, x_late, x_far_late, late_weight = lax.optimization_barrier(
            (stacked, x_rows, x_far, near_weight)
        )
        far_weight = swapped(late_weight)
        near = exchanged(stacked, "seq", column_groups).reshape(half_count, tokens, HD)
        own_half, given_half = turned_halves(parity, x_late, 2, "own_halves")
        (far_half,) = turned_halves(parity, x_far_late, 1, "far_half")
        next_half = passed(given_half)
        q_cross, g_cross = moved(q_middle, run // 2), moved(g_middle, -(run // 2))
        columns_shape = jax.ShapeDtypeStruct((HD, QH * tokens), jnp.bfloat16)
        rows_shape = jax.ShapeDtypeStruct((QH * tokens, HD), jnp.bfloat16)
        query_shapes = (columns_shape, columns_shape, rows_shape, rows_shape)
        own_forms = local_call(
            query_kernel, query_shapes, (), (queries[0], out_grad[0]), "own_query_forms"
        )
        cross_forms = local_call(
            query_kernel, query_shapes, (), (q_cross, g_cross), "cross_query_forms"
        )
        near, own_forms, cross_forms, own_half, next_half, far_half, far_weight = (
            lax.optimization_barrier(
                (near, own_forms, cross_forms, own_half, next_half, far_half, far_weight)
            )
        )
        far = swapped(near)
    with jax.named_scope("attention"):
        totals = local_call(
            totals_kernel,
            jax.ShapeDtypeStruct((2, 3, QH * tokens), jnp.float32),
            (plan, core),
            (near, far, *own_forms[:2], *cross_forms[:2]),
            "attention_totals",
            (),
            48,
        )
        other_totals = crossed(totals)
        sum_tiles = (half_count // TILE_BLOCKS, TILE_BLOCKS * BLOCK, HD)
        dq_own, dq_sent, near_grad, far_grad = local_call(
            grads_kernel,
            (
                jax.ShapeDtypeStruct((tokens, QH * HD), jnp.float32),
                jax.ShapeDtypeStruct((tokens, QH * HD), jnp.bfloat16),
                jax.ShapeDtypeStruct(near.shape, jnp.bfloat16),
                jax.ShapeDtypeStruct(near.shape, jnp.bfloat16),
            ),
            (plan, core),
            (near, far, totals, other_totals, *own_forms, *cross_forms),
            "attention_grads",
            (
                pltpu.VMEM(sum_tiles, jnp.float32),
                pltpu.VMEM(sum_tiles, jnp.float32),
                pltpu.VMEM((HD, QH * tokens), jnp.float32),
            ),
            48,
        )
    with jax.named_scope("kv_reduce"):
        pair = near_grad.astype(jnp.float32) + swapped(far_grad).astype(jnp.float32)
        pair = pair.astype(jnp.bfloat16).reshape(columns, 2, tokens, HD)
        pair, next_half, dq_sent = lax.optimization_barrier((pair, next_half, dq_sent))
        arrived = exchanged(pair, "seq", column_groups)
        next_far_half = swapped(next_half)
        dq_middle = moved(dq_sent, run // 2)
    with jax.named_scope("projection_grad"):
        settled = local_call(
            settle_kernel,
            jax.ShapeDtypeStruct((1, 2, tokens, HD), jnp.bfloat16),
            (core,),
            (arrived, cosine, sine_part),
            "projection_grad",
        )
    with jax.named_scope("weight_grad"):
        next_grads, next_far_half, dq_middle = lax.optimization_barrier(
            (passed(settled[0]), next_far_half, dq_middle)
        )
        piece = BLOCK // quads
        share = local_call(
            share_kernel,
            jax.ShapeDtypeStruct((quads, dp_count, piece, HD), jnp.bfloat16),
            (core,),
            (own_half, far_half, next_half, next_far_half, settled[0], next_grads),
            "weight_share",
        )
        quad_parts = exchanged(share, "seq", quad_groups)
        dq_back = moved(dq_middle, run // 2)
        quad_parts, dq_back = lax.optimization_barrier((quad_parts, dq_back))
        (quad_share,) = local_call(
            total_kernel,
            (jax.ShapeDtypeStruct((1, dp_count, piece, HD), jnp.bfloat16),),
            (),
            (quad_parts,),
            "quad_share",
        )
        share_parts = exchanged(quad_share[0], "dp")
        (group_share,) = local_call(
            total_kernel,
            (jax.ShapeDtypeStruct((1, piece, HD), jnp.bfloat16),),
            (),
            (share_parts,),
            "group_share",
        )
        whole_share = local_call(
            sum_kernel,
            jax.ShapeDtypeStruct((columns, piece, HD), jnp.bfloat16),
            (),
            (group_share[0], crossed(group_share[0])),
            "whole_share",
        )
        near_parts = exchanged(whole_share, "seq", column_groups)
        weight_grad = local_call(
            functools.partial(assemble_kernel, grad_scale),
            jax.ShapeDtypeStruct((width // dp_count, 2 * HD), jnp.float32),
            (core,),
            (near_parts, swapped(near_parts)),
            "weight_grad",
        )
    with jax.named_scope("query_grad"):
        query_grad = (dq_own + dq_back.astype(jnp.float32)).astype(jnp.bfloat16)
    with jax.named_scope("input_grad"):
        both = settled[0]
        own = jnp.where(is_first, both[0], both[1])
        other = swapped(jnp.where(is_first, both[1], both[0]))
        proj_grad = jnp.concatenate(
            [jnp.where(is_first, own, other), jnp.where(is_first, other, own)], axis=1
        )
        input_grad = (dot_cols(own, near_weight) + dot_cols(other, far_weight)).astype(
            jnp.bfloat16
        )
    return (query_grad[None], proj_grad[None], input_grad[None], weight_grad)


def solution(mesh):
    in_specs = (
        P("dp", "seq", None),
        P("dp", "seq", None),
        P("dp", "seq", None),
        P("dp", None),
        P("dp", None),
        P("dp", "seq", None),
    )
    out_specs = (P("dp", "seq", None), P("dp", "seq", None), P("dp", "seq", None), P("dp", None))
    return jax.shard_map(body, mesh=mesh, in_specs=in_specs, out_specs=out_specs, check_vma=False)
```

```python
import functools
import math

import jax
import jax.numpy as jnp
import numpy as np
from jax import lax
from jax.experimental import pallas as pl
from jax.experimental.pallas import tpu as pltpu
from jax.sharding import PartitionSpec as P

QH = 8
HD = 128
BLOCK = 128
TILE_BLOCKS = 4

EPSILON = 1e-06
LOG2E = math.log2(math.e)


def frequencies(size):
    expo = np.arange(0, size, 2).astype(np.float32) / np.float32(size)
    base = np.float32(1.0) / np.power(np.float32(500000.0), expo)
    wavelen = np.float32(2.0 * math.pi) / base
    mixing = (np.float32(8192.0) / wavelen - np.float32(1.0)) / np.float32(3.0)
    blended = (1.0 - mixing) * base / 8.0 + mixing * base
    slow = np.where(wavelen > 8192.0, base / 8.0, blended)
    return np.where(wavelen < 2048.0, base, slow).astype(np.float32)


def softstep(scaled):
    return scaled - jnp.sin(2.0 * math.pi * (scaled - jnp.round(scaled))) / (2.0 * math.pi)


def dot_cols(left, right):
    return lax.dot_general(
        left, right, (((1,), (1,)), ((), ())), preferred_element_type=jnp.float32
    )


def dot(left, right):
    return jnp.dot(left, right, preferred_element_type=jnp.float32)


def plan_kernel(index_ref, places_ref, plan_ref, slot_at):
    blocks = slot_at.shape[0]
    half = blocks // 2
    me = index_ref[0]
    start = lax.div(me, half) * half
    for place in range(blocks):
        slot_at[place] = -1
    for slot in range(half):
        slot_at[places_ref[start + slot]] = slot
    own = places_ref[me]
    cross = places_ref[lax.rem(me + half, blocks)]

    def visit(place, counts):
        rank, below_own, below_cross = counts
        slot = slot_at[place]
        found = slot >= 0

        @pl.when(found)
        def _():
            plan_ref[rank] = slot
            plan_ref[half + rank] = place

        one = jnp.where(found, 1, 0)
        return (
            rank + one,
            below_own + jnp.where(place < own, one, 0),
            below_cross + jnp.where(place < cross, one, 0),
        )

    _, below_own, below_cross = lax.fori_loop(0, blocks, visit, (0, 0, 0))
    plan_ref[2 * half] = own
    plan_ref[2 * half + 1] = cross
    plan_ref[2 * half + 2] = below_own
    plan_ref[2 * half + 3] = below_cross


def tile_of(plan_ref, core_ref, near_ref, far_ref, tile):
    slots = [plan_ref[tile * TILE_BLOCKS + step] for step in range(TILE_BLOCKS)]
    near = jnp.concatenate([near_ref[slot] for slot in slots], axis=0)
    far = jnp.concatenate([far_ref[slot] for slot in slots], axis=0)
    is_first = core_ref[0] == 0
    return jnp.where(is_first, near, far), jnp.where(is_first, far, near)


def tile_counts(plan_ref, blocks, group):
    below = plan_ref[2 * blocks + 2 + group]
    seen = below + 1 - group
    return lax.div(below, TILE_BLOCKS), lax.div(seen + TILE_BLOCKS - 1, TILE_BLOCKS)


def visible_in(plan_ref, blocks, group, tile, rows):
    offsets = lax.broadcasted_iota(jnp.int32, (BLOCK, 1), 0)
    key_at = jnp.concatenate(
        [
            plan_ref[blocks + tile * TILE_BLOCKS + step] * BLOCK + offsets
            for step in range(TILE_BLOCKS)
        ],
        axis=0,
    )
    token = lax.rem(lax.broadcasted_iota(jnp.int32, (1, rows), 1), BLOCK)
    return key_at <= plan_ref[2 * blocks + group] * BLOCK + token


SCORE_SCALE = LOG2E / math.sqrt(HD)


def totals_kernel(plan_ref, core_ref, near_ref, far_ref, *rest):
    query_refs, out_ref = rest[:-1], rest[-1]
    blocks = near_ref.shape[0]
    rows = QH * BLOCK
    span = TILE_BLOCKS * BLOCK

    def folded(values):
        return jnp.sum(values.reshape(span // 8, 8, rows), axis=0)

    for group in range(2):
        q_cols, g_cols = query_refs[2 * group], query_refs[2 * group + 1]

        def step(tile, sums, masked, q_cols=q_cols, g_cols=g_cols, group=group):
            total, weighted, top = sums
            keys, values = tile_of(plan_ref, core_ref, near_ref, far_ref, tile)
            scores = dot(keys, q_cols[...]) * SCORE_SCALE
            if masked:
                visible = visible_in(plan_ref, blocks, group, tile, rows)
                scores = jnp.where(visible, scores, -jnp.inf)
            highest = jnp.maximum(top, jnp.max(scores, axis=0, keepdims=True))
            shrink = jnp.exp2(top - highest)
            exponent = jnp.exp2(scores - highest)
            prob_grad = dot(values, g_cols[...])
            total = total * shrink + folded(exponent)
            weighted = weighted * shrink + folded(exponent * prob_grad)
            return (total, weighted, highest)

        full, tiles = tile_counts(plan_ref, blocks, group)
        empty = jnp.zeros((8, rows), jnp.float32)
        sums = (empty, empty, jnp.full((1, rows), -1e30, jnp.float32))
        sums = lax.fori_loop(0, full, functools.partial(step, masked=False), sums)
        total, weighted, top = lax.fori_loop(
            full, tiles, functools.partial(step, masked=True), sums
        )
        out_ref[group, 0:1, :] = top
        out_ref[group, 1:2, :] = jnp.sum(total, axis=0, keepdims=True)
        out_ref[group, 2:3, :] = jnp.sum(weighted, axis=0, keepdims=True)


def grads_kernel(plan_ref, core_ref, near_ref, far_ref, own_ref, other_ref, *rest):
    query_refs, (dq_ref, dq_sent_ref, near_grad_ref, far_grad_ref) = rest[:8], rest[8:12]
    key_sums, value_sums, dq_cols = rest[12:]
    blocks = near_ref.shape[0]
    rows = QH * BLOCK
    is_first = core_ref[0] == 0
    key_sums[...] = jnp.zeros_like(key_sums)
    value_sums[...] = jnp.zeros_like(value_sums)

    for group, out_ref in enumerate((dq_ref, dq_sent_ref)):
        q_cols, g_cols, q_rows, g_rows = query_refs[4 * group : 4 * group + 4]
        here, there = own_ref[group], other_ref[1 - group]
        top = jnp.maximum(here[0:1], there[0:1])
        here_part, there_part = jnp.exp2(here[0:1] - top), jnp.exp2(there[0:1] - top)
        total = here[1:2] * here_part + there[1:2] * there_part
        row_delta = (here[2:3] * here_part + there[2:3] * there_part) / total
        log_total = top + jnp.log(total) * LOG2E
        dq_cols[...] = jnp.zeros_like(dq_cols)

        def step(
            tile, carry, masked, group=group, q_cols=q_cols, g_cols=g_cols, q_rows=q_rows,
            g_rows=g_rows, row_delta=row_delta, log_total=log_total,
        ):
            keys, values = tile_of(plan_ref, core_ref, near_ref, far_ref, tile)
            probs = jnp.exp2(dot(keys, q_cols[...]) * SCORE_SCALE - log_total)
            if masked:
                probs = jnp.where(visible_in(plan_ref, blocks, group, tile, rows), probs, 0.0)
            prob_grad = dot(values, g_cols[...])
            score_grad = (probs * (prob_grad - row_delta)).astype(jnp.bfloat16)
            value_sums[tile] += dot(probs.astype(jnp.bfloat16), g_rows[...])
            key_sums[tile] += dot(score_grad, q_rows[...])
            dq_cols[...] += dot(keys.T, score_grad)
            return carry

        full, tiles = tile_counts(plan_ref, blocks, group)
        lax.fori_loop(0, full, functools.partial(step, masked=False), 0)
        lax.fori_loop(full, tiles, functools.partial(step, masked=True), 0)
        for head in range(QH):
            part = pl.ds(head * HD, HD)
            out_ref[:, part] = (dq_cols[:, part].T * (1.0 / math.sqrt(HD))).astype(out_ref.dtype)

    @pl.loop(0, blocks // TILE_BLOCKS)
    def _(tile):
        key_grad = key_sums[tile].astype(jnp.bfloat16)
        value_grad = value_sums[tile].astype(jnp.bfloat16)
        near_grad = jnp.where(is_first, key_grad, value_grad)
        far_grad = jnp.where(is_first, value_grad, key_grad)
        for step in range(TILE_BLOCKS):
            slot = plan_ref[tile * TILE_BLOCKS + step]
            near_grad_ref[slot] = near_grad[step * BLOCK : (step + 1) * BLOCK]
            far_grad_ref[slot] = far_grad[step * BLOCK : (step + 1) * BLOCK]


def copies_kernel(core_ref, weight_ref, out_ref):
    start = pl.multiple_of(core_ref[0] * HD, HD)
    half = weight_ref[:, pl.ds(start, HD)]
    for copy in range(out_ref.shape[0]):
        out_ref[copy] = half


def query_kernel(q_ref, g_ref, q_cols, g_cols, q_rows, g_rows):
    for head in range(QH):
        part = pl.ds(head * HD, HD)
        q_cols[:, part] = q_ref[:, part].T
        g_cols[:, part] = g_ref[:, part].T
        q_rows[part, :] = q_ref[:, part]
        g_rows[part, :] = g_ref[:, part]


def local_call(kernel, shapes, scalars, arrays, name, scratch=(), limit=32):
    smem = pl.BlockSpec(memory_space=pltpu.SMEM)
    vmem = pl.BlockSpec(memory_space=pltpu.VMEM)
    return pl.pallas_call(
        kernel,
        out_shape=shapes,
        in_specs=[smem] * len(scalars) + [vmem] * len(arrays),
        out_specs=jax.tree.map(lambda _: vmem, shapes),
        scratch_shapes=scratch,
        compiler_params=pltpu.CompilerParams(vmem_limit_bytes=limit * 1024 * 1024),
        name=name,
    )(*scalars, *arrays)


def turning(core_ref, cos_ref, sin_ref, at):
    is_first = core_ref[0] == 0
    first_half = lax.broadcasted_iota(jnp.int32, (1, HD), 1) < HD // 2
    sine_part = jnp.where(first_half, -sin_ref[at], sin_ref[at])
    return jnp.where(is_first, cos_ref[at], 1.0), jnp.where(is_first, sine_part, 0.0)


def project_kernel(
    core_ref, own_bits_ref, far_bits_ref, own_ref, far_ref, weight_ref, cos_ref, sin_ref, out_ref
):
    core = core_ref[0]
    weight = weight_ref[...]
    for x_ref, bits_ref, at in ((own_ref, own_bits_ref, core), (far_ref, far_bits_ref, 1 - core)):
        raw = dot(x_ref[...], weight)
        cosine, sine_part = turning(core_ref, cos_ref, sin_ref, at)
        turned = raw * cosine + pltpu.roll(raw, HD // 2, 1) * sine_part
        largest = jnp.max(jnp.abs(turned), axis=0, keepdims=True)
        levels = (lax.shift_left(jnp.int32(1), bits_ref[core] - 1) - 1).astype(jnp.float32)
        level_step = (largest + EPSILON) / levels
        quantized = (level_step * softstep(turned / level_step)).astype(jnp.bfloat16)
        for copy in range(out_ref.shape[0]):
            out_ref[copy, at] = quantized


def settle_kernel(core_ref, arrived_ref, cos_ref, sin_ref, out_ref):
    scale = jnp.where(core_ref[0] == 0, 1.0 / math.sqrt(HD), 1.0)
    for at in range(2):
        grads = arrived_ref[0, at].astype(jnp.float32)
        for source in range(1, arrived_ref.shape[0]):
            grads += arrived_ref[source, at].astype(jnp.float32)
        cosine, sine_part = turning(core_ref, cos_ref, sin_ref, at)
        grads = grads * scale
        turned = grads * cosine - pltpu.roll(grads, HD // 2, 1) * sine_part
        out_ref[0, at] = turned.astype(jnp.bfloat16)


def turn_kernel(parity_ref, x_ref, keep_ref, *rest):
    parity = parity_ref[0]
    for group in range(keep_ref.shape[0] // BLOCK):
        rows = slice(group * BLOCK, (group + 1) * BLOCK)
        for out_ref, half in zip((keep_ref, *rest), (parity, 1 - parity)):
            start = pl.multiple_of((2 * group + half) * BLOCK, BLOCK)
            out_ref[rows, :] = x_ref[:, pl.ds(start, BLOCK)].T


def turned_halves(parity, x_rows, count, name):
    tokens, width = x_rows.shape
    shape = jax.ShapeDtypeStruct((width // 2, tokens), x_rows.dtype)
    return local_call(turn_kernel, (shape,) * count, (parity,), (x_rows,), name)


def share_kernel(core_ref, *rest):
    core = core_ref[0]
    own_ref, own_far_ref, next_ref, next_far_ref, grads_ref, next_grads_ref, out_ref = rest
    quads, groups, piece, _ = out_ref.shape
    own = jnp.concatenate([grads_ref[core], grads_ref[1 - core]], axis=0)
    beside = jnp.concatenate([next_grads_ref[core], next_grads_ref[1 - core]], axis=0)
    for group in range(groups):
        rows = slice(group * BLOCK, (group + 1) * BLOCK)
        share = dot(jnp.concatenate([own_ref[rows, :], own_far_ref[rows, :]], axis=1), own)
        share += dot(jnp.concatenate([next_ref[rows, :], next_far_ref[rows, :]], axis=1), beside)
        share = share.astype(out_ref.dtype)
        for quad in range(quads):
            out_ref[quad, group] = share[quad * piece : (quad + 1) * piece]


def total_kernel(parts_ref, out_ref):
    total = parts_ref[0].astype(jnp.float32)
    for source in range(1, parts_ref.shape[0]):
        total += parts_ref[source].astype(jnp.float32)
    total = total.astype(out_ref.dtype)
    for copy in range(out_ref.shape[0]):
        out_ref[copy] = total


def assemble_kernel(grad_scale, parts_ref, out_ref):
    _, quads, _, _, piece, _ = parts_ref.shape
    for quad in range(quads):
        for parity in range(2):
            for core in range(2):
                low = parts_ref[0, quad, parity, core].astype(jnp.float32)
                high = parts_ref[1, quad, parity, core].astype(jnp.float32)
                row = parity * BLOCK + quad * piece
                out_ref[row : row + piece, core * HD : (core + 1) * HD] = (
                    low + high
                ) * grad_scale


def body(hidden_in, queries, out_grad, kv_weight, block_pos, precision):
    tokens = hidden_in.shape[1]
    width = hidden_in.shape[2]
    seq_count = lax.axis_size("seq")
    dp_count = lax.axis_size("dp")
    half_count = seq_count // 2
    columns = half_count // 2
    grad_scale = 1.0 / math.sqrt(dp_count * seq_count * tokens)
    self_index = lax.axis_index("seq")
    core_index = lax.rem(self_index, 2)
    core = core_index.reshape(1).astype(jnp.int32)
    is_first = core_index == 0
    quads = columns // 2
    parity = lax.rem(lax.div(self_index, 2), 2).reshape(1).astype(jnp.int32)
    quad_groups = [
        [start * half_count + 4 * quad + side for quad in range(quads)]
        for start in range(2)
        for side in range(4)
    ]
    column_groups = [
        [start * half_count + 2 * column + side for column in range(columns)]
        for start in range(2)
        for side in range(2)
    ]
    run = math.gcd(dp_count, 4)
    runs = [[start + step for step in range(run)] for start in range(0, dp_count, run)]
    strides = [[start + step for step in range(0, dp_count, run)] for start in range(run)]
    swap = [(source, source ^ 1) for source in range(seq_count)]
    cross = [(source, (source + half_count) % seq_count) for source in range(seq_count)]
    beside = [(source, source ^ 2) for source in range(seq_count)]

    def swapped(value):
        return lax.ppermute(value, "seq", swap)

    def crossed(value):
        return lax.ppermute(value, "seq", cross)

    def moved(value, steps):
        pairs = []
        for group in range(dp_count):
            for member in range(seq_count):
                high = member // half_count
                place_y = (high * run + group % run + steps) % (2 * run)
                target_group = group // run * run + place_y % run
                target = place_y // run * half_count + member % half_count
                pairs.append((group * seq_count + member, target_group * seq_count + target))
        return lax.ppermute(value, ("dp", "seq"), pairs)

    def passed(value):
        return lax.ppermute(value, "seq", beside)

    def exchanged(value, axis, groups=None):
        return lax.all_to_all(value, axis, 0, 0, axis_index_groups=groups)

    x_rows = hidden_in[0]
    places = block_pos[0]
    index = self_index.reshape(1).astype(jnp.int32)
    smem = pl.BlockSpec(memory_space=pltpu.SMEM)

    with jax.named_scope("rotation"):
        pair_places = lax.dynamic_slice_in_dim(places, self_index - core_index, 2)
        pair_pos = pair_places[:, None] * BLOCK + jnp.arange(tokens, dtype=jnp.int32)[None, :]
        freq = frequencies(HD)
        angles = pair_pos.astype(jnp.float32)[:, :, None] * np.concatenate([freq, freq])
        cosine = jnp.cos(angles)
        sine_part = jnp.sin(angles)
        plan = pl.pallas_call(
            plan_kernel,
            out_shape=jax.ShapeDtypeStruct((2 * half_count + 4,), jnp.int32),
            in_specs=[smem, smem],
            out_specs=smem,
            scratch_shapes=[pltpu.SMEM((seq_count,), jnp.int32)],
            name="block_plan",
        )(index, places)
        x_far = swapped(x_rows)
    with jax.named_scope("weight_gather"):
        copies = local_call(
            copies_kernel,
            jax.ShapeDtypeStruct((run, kv_weight.shape[0], HD), kv_weight.dtype),
            (core,),
            (kv_weight,),
            "weight_copies",
        )
        run_weight = exchanged(copies, "dp", runs)
        run_weight, q_start, g_start, own_bits = lax.optimization_barrier(
            (run_weight, queries[0], out_grad[0], precision.reshape(2))
        )
        far_bits = swapped(own_bits)
        q_middle, g_middle = moved(q_start, run // 2), moved(g_start, -(run // 2))
        copies = jnp.broadcast_to(run_weight[None], (dp_count // run, *run_weight.shape))
        copies = lax.optimization_barrier(copies)
        near_weight = exchanged(copies, "dp", strides).reshape(width, HD)
        near_weight, plan, cosine, sine_part, far_bits, x_far = lax.optimization_barrier(
            (near_weight, plan, cosine, sine_part, far_bits, x_far)
        )
    with jax.named_scope("projection"):
        stacked = local_call(
            project_kernel,
            jax.ShapeDtypeStruct((columns, 2, tokens, HD), jnp.bfloat16),
            (core, own_bits, far_bits),
            (x_rows, x_far, near_weight, cosine, sine_part),
            "projection",
        )
    with jax.named_scope("kv_gather"):
        stacked, x_late, x_far_late, late_weight, q_middle, g_middle = lax.optimization_barrier(
            (stacked, x_rows, x_far, near_weight, q_middle, g_middle)
        )
        far_weight = swapped(late_weight)
        near = exchanged(stacked, "seq", column_groups).reshape(half_count, tokens, HD)
        own_half, given_half = turned_halves(parity, x_late, 2, "own_halves")
        (far_half,) = turned_halves(parity, x_far_late, 1, "far_half")
        q_cross, g_cross = moved(q_middle, run // 2), moved(g_middle, -(run // 2))
        columns_shape = jax.ShapeDtypeStruct((HD, QH * tokens), jnp.bfloat16)
        rows_shape = jax.ShapeDtypeStruct((QH * tokens, HD), jnp.bfloat16)
        query_shapes = (columns_shape, columns_shape, rows_shape, rows_shape)
        own_forms = local_call(
            query_kernel, query_shapes, (), (queries[0], out_grad[0]), "own_query_forms"
        )
        cross_forms = local_call(
            query_kernel, query_shapes, (), (q_cross, g_cross), "cross_query_forms"
        )
        near, own_forms, cross_forms, own_half, given_half, far_half, far_weight = (
            lax.optimization_barrier(
                (near, own_forms, cross_forms, own_half, given_half, far_half, far_weight)
            )
        )
        far = swapped(near)
    with jax.named_scope("attention"):
        totals = local_call(
            totals_kernel,
            jax.ShapeDtypeStruct((2, 3, QH * tokens), jnp.float32),
            (plan, core),
            (near, far, *own_forms[:2], *cross_forms[:2]),
            "attention_totals",
            (),
            48,
        )
        totals, given_half = lax.optimization_barrier((totals, given_half))
        other_totals = crossed(totals)
        next_half = passed(given_half)
        sum_tiles = (half_count // TILE_BLOCKS, TILE_BLOCKS * BLOCK, HD)
        dq_own, dq_sent, near_grad, far_grad = local_call(
            grads_kernel,
            (
                jax.ShapeDtypeStruct((tokens, QH * HD), jnp.float32),
                jax.ShapeDtypeStruct((tokens, QH * HD), jnp.bfloat16),
                jax.ShapeDtypeStruct(near.shape, jnp.bfloat16),
                jax.ShapeDtypeStruct(near.shape, jnp.bfloat16),
            ),
            (plan, core),
            (near, far, totals, other_totals, *own_forms, *cross_forms),
            "attention_grads",
            (
                pltpu.VMEM(sum_tiles, jnp.float32),
                pltpu.VMEM(sum_tiles, jnp.float32),
                pltpu.VMEM((HD, QH * tokens), jnp.float32),
            ),
            48,
        )
    with jax.named_scope("kv_reduce"):
        near_grad, far_grad, next_half = lax.optimization_barrier(
            (near_grad, far_grad, next_half)
        )
        pair = near_grad.astype(jnp.float32) + swapped(far_grad).astype(jnp.float32)
        pair = pair.astype(jnp.bfloat16).reshape(columns, 2, tokens, HD)
        pair, next_half, dq_sent = lax.optimization_barrier((pair, next_half, dq_sent))
        arrived = exchanged(pair, "seq", column_groups)
        next_far_half = swapped(next_half)
        dq_middle = moved(dq_sent, run // 2)
    with jax.named_scope("projection_grad"):
        settled = local_call(
            settle_kernel,
            jax.ShapeDtypeStruct((1, 2, tokens, HD), jnp.bfloat16),
            (core,),
            (arrived, cosine, sine_part),
            "projection_grad",
        )
    with jax.named_scope("weight_grad"):
        next_grads, next_far_half, dq_middle = lax.optimization_barrier(
            (passed(settled[0]), next_far_half, dq_middle)
        )
        piece = BLOCK // quads
        share = local_call(
            share_kernel,
            jax.ShapeDtypeStruct((quads, dp_count, piece, HD), jnp.bfloat16),
            (core,),
            (own_half, far_half, next_half, next_far_half, settled[0], next_grads),
            "weight_share",
        )
        quad_parts = exchanged(share, "seq", quad_groups)
        dq_back = moved(dq_middle, run // 2)
        quad_parts, dq_back = lax.optimization_barrier((quad_parts, dq_back))
        (quad_share,) = local_call(
            total_kernel,
            (jax.ShapeDtypeStruct((1, dp_count, piece, HD), jnp.bfloat16),),
            (),
            (quad_parts,),
            "quad_share",
        )
        share_parts = exchanged(quad_share[0], "dp")
        group_share = local_call(
            total_kernel,
            jax.ShapeDtypeStruct((seq_count, piece, HD), jnp.bfloat16),
            (),
            (share_parts,),
            "group_share",
        )
        gathered = exchanged(group_share, "seq")
        weight_grad = local_call(
            functools.partial(assemble_kernel, grad_scale),
            jax.ShapeDtypeStruct((width // dp_count, 2 * HD), jnp.float32),
            (),
            (gathered.reshape(2, quads, 2, 2, piece, HD),),
            "weight_grad",
        )
    with jax.named_scope("query_grad"):
        query_grad = (dq_own + dq_back.astype(jnp.float32)).astype(jnp.bfloat16)
    with jax.named_scope("input_grad"):
        both = settled[0]
        own = jnp.where(is_first, both[0], both[1])
        other = swapped(jnp.where(is_first, both[1], both[0]))
        proj_grad = jnp.concatenate(
            [jnp.where(is_first, own, other), jnp.where(is_first, other, own)], axis=1
        )
        input_grad = (dot_cols(own, near_weight) + dot_cols(other, far_weight)).astype(
            jnp.bfloat16
        )
    return (query_grad[None], proj_grad[None], input_grad[None], weight_grad)


def solution(mesh):
    in_specs = (
        P("dp", "seq", None),
        P("dp", "seq", None),
        P("dp", "seq", None),
        P("dp", None),
        P("dp", None),
        P("dp", "seq", None),
    )
    out_specs = (P("dp", "seq", None), P("dp", "seq", None), P("dp", "seq", None), P("dp", None))
    return jax.shard_map(body, mesh=mesh, in_specs=in_specs, out_specs=out_specs, check_vma=False)
```

```python
import functools
import math

import jax
import jax.numpy as jnp
import numpy as np
from jax import lax
from jax.experimental import pallas as pl
from jax.experimental.pallas import tpu as pltpu
from jax.sharding import PartitionSpec as P

QH = 8
HD = 128
BLOCK = 128
TILE_BLOCKS = 4

EPSILON = 1e-06
LOG2E = math.log2(math.e)


def frequencies(size):
    expo = np.arange(0, size, 2).astype(np.float32) / np.float32(size)
    base = np.float32(1.0) / np.power(np.float32(500000.0), expo)
    wavelen = np.float32(2.0 * math.pi) / base
    mixing = (np.float32(8192.0) / wavelen - np.float32(1.0)) / np.float32(3.0)
    blended = (1.0 - mixing) * base / 8.0 + mixing * base
    slow = np.where(wavelen > 8192.0, base / 8.0, blended)
    return np.where(wavelen < 2048.0, base, slow).astype(np.float32)


def softstep(scaled):
    return scaled - jnp.sin(2.0 * math.pi * (scaled - jnp.round(scaled))) / (2.0 * math.pi)


def dot_cols(left, right):
    return lax.dot_general(
        left, right, (((1,), (1,)), ((), ())), preferred_element_type=jnp.float32
    )


def dot(left, right):
    return jnp.dot(left, right, preferred_element_type=jnp.float32)


def plan_kernel(index_ref, places_ref, plan_ref, slot_at):
    blocks = slot_at.shape[0]
    half = blocks // 2
    me = index_ref[0]
    start = lax.div(me, half) * half
    for place in range(blocks):
        slot_at[place] = -1
    for slot in range(half):
        slot_at[places_ref[start + slot]] = slot
    own = places_ref[me]
    cross = places_ref[lax.rem(me + half, blocks)]

    def visit(place, counts):
        rank, below_own, below_cross = counts
        slot = slot_at[place]
        found = slot >= 0

        @pl.when(found)
        def _():
            plan_ref[rank] = slot
            plan_ref[half + rank] = place

        one = jnp.where(found, 1, 0)
        return (
            rank + one,
            below_own + jnp.where(place < own, one, 0),
            below_cross + jnp.where(place < cross, one, 0),
        )

    _, below_own, below_cross = lax.fori_loop(0, blocks, visit, (0, 0, 0))
    plan_ref[2 * half] = own
    plan_ref[2 * half + 1] = cross
    plan_ref[2 * half + 2] = below_own
    plan_ref[2 * half + 3] = below_cross


def tile_of(plan_ref, core_ref, near_ref, far_ref, tile):
    slots = [plan_ref[tile * TILE_BLOCKS + step] for step in range(TILE_BLOCKS)]
    near = jnp.concatenate([near_ref[slot] for slot in slots], axis=0)
    far = jnp.concatenate([far_ref[slot] for slot in slots], axis=0)
    is_first = core_ref[0] == 0
    return jnp.where(is_first, near, far), jnp.where(is_first, far, near)


def tile_counts(plan_ref, blocks, group):
    below = plan_ref[2 * blocks + 2 + group]
    seen = below + 1 - group
    return lax.div(below, TILE_BLOCKS), lax.div(seen + TILE_BLOCKS - 1, TILE_BLOCKS)


def visible_in(plan_ref, blocks, group, tile, rows):
    offsets = lax.broadcasted_iota(jnp.int32, (BLOCK, 1), 0)
    key_at = jnp.concatenate(
        [
            plan_ref[blocks + tile * TILE_BLOCKS + step] * BLOCK + offsets
            for step in range(TILE_BLOCKS)
        ],
        axis=0,
    )
    token = lax.rem(lax.broadcasted_iota(jnp.int32, (1, rows), 1), BLOCK)
    return key_at <= plan_ref[2 * blocks + group] * BLOCK + token


SCORE_SCALE = LOG2E / math.sqrt(HD)


def totals_kernel(plan_ref, core_ref, near_ref, far_ref, *rest):
    query_refs, out_ref = rest[:-1], rest[-1]
    blocks = near_ref.shape[0]
    rows = QH * BLOCK
    span = TILE_BLOCKS * BLOCK

    def folded(values):
        return jnp.sum(values.reshape(span // 8, 8, rows), axis=0)

    for group in range(2):
        q_cols, g_cols = query_refs[2 * group], query_refs[2 * group + 1]

        def step(tile, sums, masked, q_cols=q_cols, g_cols=g_cols, group=group):
            total, weighted, top = sums
            keys, values = tile_of(plan_ref, core_ref, near_ref, far_ref, tile)
            scores = dot(keys, q_cols[...]) * SCORE_SCALE
            if masked:
                visible = visible_in(plan_ref, blocks, group, tile, rows)
                scores = jnp.where(visible, scores, -jnp.inf)
            highest = jnp.maximum(top, jnp.max(scores, axis=0, keepdims=True))
            shrink = jnp.exp2(top - highest)
            exponent = jnp.exp2(scores - highest)
            prob_grad = dot(values, g_cols[...])
            total = total * shrink + folded(exponent)
            weighted = weighted * shrink + folded(exponent * prob_grad)
            return (total, weighted, highest)

        full, tiles = tile_counts(plan_ref, blocks, group)
        empty = jnp.zeros((8, rows), jnp.float32)
        sums = (empty, empty, jnp.full((1, rows), -1e30, jnp.float32))
        sums = lax.fori_loop(0, full, functools.partial(step, masked=False), sums)
        total, weighted, top = lax.fori_loop(
            full, tiles, functools.partial(step, masked=True), sums
        )
        out_ref[group, 0:1, :] = top
        out_ref[group, 1:2, :] = jnp.sum(total, axis=0, keepdims=True)
        out_ref[group, 2:3, :] = jnp.sum(weighted, axis=0, keepdims=True)


def grads_kernel(plan_ref, core_ref, near_ref, far_ref, own_ref, other_ref, *rest):
    query_refs, (dq_ref, dq_sent_ref, near_grad_ref, far_grad_ref) = rest[:8], rest[8:12]
    key_sums, value_sums, dq_cols = rest[12:]
    blocks = near_ref.shape[0]
    rows = QH * BLOCK
    is_first = core_ref[0] == 0
    key_sums[...] = jnp.zeros_like(key_sums)
    value_sums[...] = jnp.zeros_like(value_sums)

    for group, out_ref in enumerate((dq_ref, dq_sent_ref)):
        q_cols, g_cols, q_rows, g_rows = query_refs[4 * group : 4 * group + 4]
        here, there = own_ref[group], other_ref[1 - group]
        top = jnp.maximum(here[0:1], there[0:1])
        here_part, there_part = jnp.exp2(here[0:1] - top), jnp.exp2(there[0:1] - top)
        total = here[1:2] * here_part + there[1:2] * there_part
        row_delta = (here[2:3] * here_part + there[2:3] * there_part) / total
        log_total = top + jnp.log(total) * LOG2E
        dq_cols[...] = jnp.zeros_like(dq_cols)

        def step(
            tile, carry, masked, group=group, q_cols=q_cols, g_cols=g_cols, q_rows=q_rows,
            g_rows=g_rows, row_delta=row_delta, log_total=log_total,
        ):
            keys, values = tile_of(plan_ref, core_ref, near_ref, far_ref, tile)
            probs = jnp.exp2(dot(keys, q_cols[...]) * SCORE_SCALE - log_total)
            if masked:
                probs = jnp.where(visible_in(plan_ref, blocks, group, tile, rows), probs, 0.0)
            prob_grad = dot(values, g_cols[...])
            score_grad = (probs * (prob_grad - row_delta)).astype(jnp.bfloat16)
            value_sums[tile] += dot(probs.astype(jnp.bfloat16), g_rows[...])
            key_sums[tile] += dot(score_grad, q_rows[...])
            dq_cols[...] += dot(keys.T, score_grad)
            return carry

        full, tiles = tile_counts(plan_ref, blocks, group)
        lax.fori_loop(0, full, functools.partial(step, masked=False), 0)
        lax.fori_loop(full, tiles, functools.partial(step, masked=True), 0)
        for head in range(QH):
            part = pl.ds(head * HD, HD)
            out_ref[:, part] = (dq_cols[:, part].T * (1.0 / math.sqrt(HD))).astype(out_ref.dtype)

    @pl.loop(0, blocks // TILE_BLOCKS)
    def _(tile):
        key_grad = key_sums[tile].astype(jnp.bfloat16)
        value_grad = value_sums[tile].astype(jnp.bfloat16)
        near_grad = jnp.where(is_first, key_grad, value_grad)
        far_grad = jnp.where(is_first, value_grad, key_grad)
        for step in range(TILE_BLOCKS):
            slot = plan_ref[tile * TILE_BLOCKS + step]
            near_grad_ref[slot] = near_grad[step * BLOCK : (step + 1) * BLOCK]
            far_grad_ref[slot] = far_grad[step * BLOCK : (step + 1) * BLOCK]


def copies_kernel(core_ref, weight_ref, out_ref):
    start = pl.multiple_of(core_ref[0] * HD, HD)
    half = weight_ref[:, pl.ds(start, HD)]
    for copy in range(out_ref.shape[0]):
        out_ref[copy] = half


def query_kernel(q_ref, g_ref, q_cols, g_cols, q_rows, g_rows):
    for head in range(QH):
        part = pl.ds(head * HD, HD)
        q_cols[:, part] = q_ref[:, part].T
        g_cols[:, part] = g_ref[:, part].T
        q_rows[part, :] = q_ref[:, part]
        g_rows[part, :] = g_ref[:, part]


def local_call(kernel, shapes, scalars, arrays, name, scratch=(), limit=32):
    smem = pl.BlockSpec(memory_space=pltpu.SMEM)
    vmem = pl.BlockSpec(memory_space=pltpu.VMEM)
    return pl.pallas_call(
        kernel,
        out_shape=shapes,
        in_specs=[smem] * len(scalars) + [vmem] * len(arrays),
        out_specs=jax.tree.map(lambda _: vmem, shapes),
        scratch_shapes=scratch,
        compiler_params=pltpu.CompilerParams(vmem_limit_bytes=limit * 1024 * 1024),
        name=name,
    )(*scalars, *arrays)


def turning(core_ref, cos_ref, sin_ref, at):
    is_first = core_ref[0] == 0
    first_half = lax.broadcasted_iota(jnp.int32, (1, HD), 1) < HD // 2
    sine_part = jnp.where(first_half, -sin_ref[at], sin_ref[at])
    return jnp.where(is_first, cos_ref[at], 1.0), jnp.where(is_first, sine_part, 0.0)


def project_kernel(
    core_ref, own_bits_ref, far_bits_ref, own_ref, far_ref, weight_ref, cos_ref, sin_ref, out_ref
):
    core = core_ref[0]
    weight = weight_ref[...]
    for x_ref, bits_ref, at in ((own_ref, own_bits_ref, core), (far_ref, far_bits_ref, 1 - core)):
        raw = dot(x_ref[...], weight)
        cosine, sine_part = turning(core_ref, cos_ref, sin_ref, at)
        turned = raw * cosine + pltpu.roll(raw, HD // 2, 1) * sine_part
        largest = jnp.max(jnp.abs(turned), axis=0, keepdims=True)
        levels = (lax.shift_left(jnp.int32(1), bits_ref[core] - 1) - 1).astype(jnp.float32)
        level_step = (largest + EPSILON) / levels
        quantized = (level_step * softstep(turned / level_step)).astype(jnp.bfloat16)
        for copy in range(out_ref.shape[0]):
            out_ref[copy, at] = quantized


def settle_kernel(core_ref, arrived_ref, cos_ref, sin_ref, out_ref):
    scale = jnp.where(core_ref[0] == 0, 1.0 / math.sqrt(HD), 1.0)
    for at in range(2):
        grads = arrived_ref[0, at].astype(jnp.float32)
        for source in range(1, arrived_ref.shape[0]):
            grads += arrived_ref[source, at].astype(jnp.float32)
        cosine, sine_part = turning(core_ref, cos_ref, sin_ref, at)
        grads = grads * scale
        turned = grads * cosine - pltpu.roll(grads, HD // 2, 1) * sine_part
        out_ref[0, at] = turned.astype(jnp.bfloat16)


def turn_kernel(parity_ref, x_ref, keep_ref, *rest):
    parity = parity_ref[0]
    for group in range(keep_ref.shape[0] // BLOCK):
        rows = slice(group * BLOCK, (group + 1) * BLOCK)
        for out_ref, half in zip((keep_ref, *rest), (parity, 1 - parity)):
            start = pl.multiple_of((2 * group + half) * BLOCK, BLOCK)
            out_ref[rows, :] = x_ref[:, pl.ds(start, BLOCK)].T


def turned_halves(parity, x_rows, count, name):
    tokens, width = x_rows.shape
    shape = jax.ShapeDtypeStruct((width // 2, tokens), x_rows.dtype)
    return local_call(turn_kernel, (shape,) * count, (parity,), (x_rows,), name)


def share_kernel(core_ref, *rest):
    core = core_ref[0]
    own_ref, own_far_ref, next_ref, next_far_ref, grads_ref, next_grads_ref, out_ref = rest
    quads, groups, piece, _ = out_ref.shape
    own = jnp.concatenate([grads_ref[core], grads_ref[1 - core]], axis=0)
    beside = jnp.concatenate([next_grads_ref[core], next_grads_ref[1 - core]], axis=0)
    for group in range(groups):
        rows = slice(group * BLOCK, (group + 1) * BLOCK)
        share = dot(jnp.concatenate([own_ref[rows, :], own_far_ref[rows, :]], axis=1), own)
        share += dot(jnp.concatenate([next_ref[rows, :], next_far_ref[rows, :]], axis=1), beside)
        share = share.astype(out_ref.dtype)
        for quad in range(quads):
            out_ref[quad, group] = share[quad * piece : (quad + 1) * piece]


def total_kernel(parts_ref, out_ref):
    total = parts_ref[0].astype(jnp.float32)
    for source in range(1, parts_ref.shape[0]):
        total += parts_ref[source].astype(jnp.float32)
    total = total.astype(out_ref.dtype)
    for copy in range(out_ref.shape[0]):
        out_ref[copy] = total


def assemble_kernel(grad_scale, parts_ref, out_ref):
    _, quads, _, _, piece, _ = parts_ref.shape
    for quad in range(quads):
        for parity in range(2):
            for core in range(2):
                low = parts_ref[0, quad, parity, core].astype(jnp.float32)
                high = parts_ref[1, quad, parity, core].astype(jnp.float32)
                row = parity * BLOCK + quad * piece
                out_ref[row : row + piece, core * HD : (core + 1) * HD] = (
                    low + high
                ) * grad_scale


def body(hidden_in, queries, out_grad, kv_weight, block_pos, precision):
    tokens = hidden_in.shape[1]
    width = hidden_in.shape[2]
    seq_count = lax.axis_size("seq")
    dp_count = lax.axis_size("dp")
    half_count = seq_count // 2
    columns = half_count // 2
    grad_scale = 1.0 / math.sqrt(dp_count * seq_count * tokens)
    self_index = lax.axis_index("seq")
    core_index = lax.rem(self_index, 2)
    core = core_index.reshape(1).astype(jnp.int32)
    is_first = core_index == 0
    quads = columns // 2
    parity = lax.rem(lax.div(self_index, 2), 2).reshape(1).astype(jnp.int32)
    quad_groups = [
        [start * half_count + 4 * quad + side for quad in range(quads)]
        for start in range(2)
        for side in range(4)
    ]
    column_groups = [
        [start * half_count + 2 * column + side for column in range(columns)]
        for start in range(2)
        for side in range(2)
    ]
    run = math.gcd(dp_count, 4)
    runs = [[start + step for step in range(run)] for start in range(0, dp_count, run)]
    strides = [[start + step for step in range(0, dp_count, run)] for start in range(run)]
    swap = [(source, source ^ 1) for source in range(seq_count)]
    cross = [(source, (source + half_count) % seq_count) for source in range(seq_count)]
    beside = [(source, source ^ 2) for source in range(seq_count)]

    def swapped(value):
        return lax.ppermute(value, "seq", swap)

    def crossed(value):
        return lax.ppermute(value, "seq", cross)

    def moved(value, steps):
        pairs = []
        for group in range(dp_count):
            for member in range(seq_count):
                high = member // half_count
                place_y = (high * run + group % run + steps) % (2 * run)
                target_group = group // run * run + place_y % run
                target = place_y // run * half_count + member % half_count
                pairs.append((group * seq_count + member, target_group * seq_count + target))
        return lax.ppermute(value, ("dp", "seq"), pairs)

    def passed(value):
        return lax.ppermute(value, "seq", beside)

    def exchanged(value, axis, groups=None):
        return lax.all_to_all(value, axis, 0, 0, axis_index_groups=groups)

    x_rows = hidden_in[0]
    places = block_pos[0]
    index = self_index.reshape(1).astype(jnp.int32)
    smem = pl.BlockSpec(memory_space=pltpu.SMEM)

    with jax.named_scope("rotation"):
        pair_places = lax.dynamic_slice_in_dim(places, self_index - core_index, 2)
        pair_pos = pair_places[:, None] * BLOCK + jnp.arange(tokens, dtype=jnp.int32)[None, :]
        freq = frequencies(HD)
        angles = pair_pos.astype(jnp.float32)[:, :, None] * np.concatenate([freq, freq])
        cosine = jnp.cos(angles)
        sine_part = jnp.sin(angles)
        plan = pl.pallas_call(
            plan_kernel,
            out_shape=jax.ShapeDtypeStruct((2 * half_count + 4,), jnp.int32),
            in_specs=[smem, smem],
            out_specs=smem,
            scratch_shapes=[pltpu.SMEM((seq_count,), jnp.int32)],
            name="block_plan",
        )(index, places)
        x_far = swapped(x_rows)
    with jax.named_scope("weight_gather"):
        copies = local_call(
            copies_kernel,
            jax.ShapeDtypeStruct((run, kv_weight.shape[0], HD), kv_weight.dtype),
            (core,),
            (kv_weight,),
            "weight_copies",
        )
        run_weight = exchanged(copies, "dp", runs)
        run_weight, q_start, g_start, own_bits = lax.optimization_barrier(
            (run_weight, queries[0], out_grad[0], precision.reshape(2))
        )
        far_bits = swapped(own_bits)
        q_middle, g_middle = moved(q_start, run // 2), moved(g_start, -(run // 2))
        copies = jnp.broadcast_to(run_weight[None], (dp_count // run, *run_weight.shape))
        copies = lax.optimization_barrier(copies)
        near_weight = exchanged(copies, "dp", strides).reshape(width, HD)
        near_weight, plan, cosine, sine_part, far_bits, x_far = lax.optimization_barrier(
            (near_weight, plan, cosine, sine_part, far_bits, x_far)
        )
    with jax.named_scope("projection"):
        stacked = local_call(
            project_kernel,
            jax.ShapeDtypeStruct((columns, 2, tokens, HD), jnp.bfloat16),
            (core, own_bits, far_bits),
            (x_rows, x_far, near_weight, cosine, sine_part),
            "projection",
        )
    with jax.named_scope("kv_gather"):
        stacked, x_late, x_far_late, late_weight, q_middle, g_middle = lax.optimization_barrier(
            (stacked, x_rows, x_far, near_weight, q_middle, g_middle)
        )
        far_weight = swapped(late_weight)
        near = exchanged(stacked, "seq", column_groups).reshape(half_count, tokens, HD)
        own_half, given_half = turned_halves(parity, x_late, 2, "own_halves")
        (far_half,) = turned_halves(parity, x_far_late, 1, "far_half")
        q_cross, g_cross = moved(q_middle, run // 2), moved(g_middle, -(run // 2))
        columns_shape = jax.ShapeDtypeStruct((HD, QH * tokens), jnp.bfloat16)
        rows_shape = jax.ShapeDtypeStruct((QH * tokens, HD), jnp.bfloat16)
        query_shapes = (columns_shape, columns_shape, rows_shape, rows_shape)
        own_forms = local_call(
            query_kernel, query_shapes, (), (queries[0], out_grad[0]), "own_query_forms"
        )
        cross_forms = local_call(
            query_kernel, query_shapes, (), (q_cross, g_cross), "cross_query_forms"
        )
        near, own_forms, cross_forms, own_half, given_half, far_half = lax.optimization_barrier(
            (near, own_forms, cross_forms, own_half, given_half, far_half)
        )
        far = swapped(near)
    with jax.named_scope("attention"):
        totals = local_call(
            totals_kernel,
            jax.ShapeDtypeStruct((2, 3, QH * tokens), jnp.float32),
            (plan, core),
            (near, far, *own_forms[:2], *cross_forms[:2]),
            "attention_totals",
            (),
            48,
        )
        totals, given_half = lax.optimization_barrier((totals, given_half))
        other_totals = crossed(totals)
        next_half = passed(given_half)
        sum_tiles = (half_count // TILE_BLOCKS, TILE_BLOCKS * BLOCK, HD)
        dq_own, dq_sent, near_grad, far_grad = local_call(
            grads_kernel,
            (
                jax.ShapeDtypeStruct((tokens, QH * HD), jnp.float32),
                jax.ShapeDtypeStruct((tokens, QH * HD), jnp.bfloat16),
                jax.ShapeDtypeStruct(near.shape, jnp.bfloat16),
                jax.ShapeDtypeStruct(near.shape, jnp.bfloat16),
            ),
            (plan, core),
            (near, far, totals, other_totals, *own_forms, *cross_forms),
            "attention_grads",
            (
                pltpu.VMEM(sum_tiles, jnp.float32),
                pltpu.VMEM(sum_tiles, jnp.float32),
                pltpu.VMEM((HD, QH * tokens), jnp.float32),
            ),
            48,
        )
    with jax.named_scope("kv_reduce"):
        near_grad, far_grad, next_half = lax.optimization_barrier(
            (near_grad, far_grad, next_half)
        )
        pair = near_grad.astype(jnp.float32) + swapped(far_grad).astype(jnp.float32)
        pair = pair.astype(jnp.bfloat16).reshape(columns, 2, tokens, HD)
        pair, next_half, dq_sent = lax.optimization_barrier((pair, next_half, dq_sent))
        arrived = exchanged(pair, "seq", column_groups)
        next_far_half = swapped(next_half)
        dq_middle = moved(dq_sent, run // 2)
    with jax.named_scope("projection_grad"):
        settled = local_call(
            settle_kernel,
            jax.ShapeDtypeStruct((1, 2, tokens, HD), jnp.bfloat16),
            (core,),
            (arrived, cosine, sine_part),
            "projection_grad",
        )
    with jax.named_scope("weight_grad"):
        next_grads, next_far_half, dq_middle = lax.optimization_barrier(
            (passed(settled[0]), next_far_half, dq_middle)
        )
        piece = BLOCK // quads
        share = local_call(
            share_kernel,
            jax.ShapeDtypeStruct((quads, dp_count, piece, HD), jnp.bfloat16),
            (core,),
            (own_half, far_half, next_half, next_far_half, settled[0], next_grads),
            "weight_share",
        )
        quad_parts = exchanged(share, "seq", quad_groups)
        dq_back = moved(dq_middle, run // 2)
        quad_parts, dq_back = lax.optimization_barrier((quad_parts, dq_back))
        (quad_share,) = local_call(
            total_kernel,
            (jax.ShapeDtypeStruct((1, dp_count, piece, HD), jnp.bfloat16),),
            (),
            (quad_parts,),
            "quad_share",
        )
        share_parts = exchanged(quad_share[0], "dp")
        group_share = local_call(
            total_kernel,
            jax.ShapeDtypeStruct((seq_count, piece, HD), jnp.bfloat16),
            (),
            (share_parts,),
            "group_share",
        )
        gathered = exchanged(group_share, "seq")
        weight_grad = local_call(
            functools.partial(assemble_kernel, grad_scale),
            jax.ShapeDtypeStruct((width // dp_count, 2 * HD), jnp.float32),
            (),
            (gathered.reshape(2, quads, 2, 2, piece, HD),),
            "weight_grad",
        )
    with jax.named_scope("query_grad"):
        query_grad = (dq_own + dq_back.astype(jnp.float32)).astype(jnp.bfloat16)
    with jax.named_scope("input_grad"):
        both = settled[0]
        own = jnp.where(is_first, both[0], both[1])
        other = swapped(jnp.where(is_first, both[1], both[0]))
        proj_grad = jnp.concatenate(
            [jnp.where(is_first, own, other), jnp.where(is_first, other, own)], axis=1
        )
        input_grad = (dot_cols(own, near_weight) + dot_cols(other, far_weight)).astype(
            jnp.bfloat16
        )
    return (query_grad[None], proj_grad[None], input_grad[None], weight_grad)


def solution(mesh):
    in_specs = (
        P("dp", "seq", None),
        P("dp", "seq", None),
        P("dp", "seq", None),
        P("dp", None),
        P("dp", None),
        P("dp", "seq", None),
    )
    out_specs = (P("dp", "seq", None), P("dp", "seq", None), P("dp", "seq", None), P("dp", None))
    return jax.shard_map(body, mesh=mesh, in_specs=in_specs, out_specs=out_specs, check_vma=False)
```
